512 devices in a mesh: liq: 32 (over y, x, core), ill: 16 (over z).
Axes of the slice: x: 4, y: 4, z: 16, core: 2. Of those that a mesh axis runs over, the one named last changes fastest.
Arguments:
- right_side: float32 [256, 128, 512], P('liq', 'ill'), may hold values from -6 to 6
- value_guess: float32 [256, 128, 512], P('liq', 'ill'), may hold values from -6 to 6
- speed_liq: float32 [256, 128, 512], P('liq', 'ill'), may hold values from 200 to 2000
- speed_ill: float32 [256, 128, 512], P('liq', 'ill'), may hold values from 0.5 to 5
- flag_liq: int32 [256, 128, 512], P('liq', 'ill'), may hold values 0 or 1
- flag_ill: int32 [256, 128, 512], P('liq', 'ill'), may hold values 0 or 1
- jump_rates: float32 [512, 512], replicated, as said below
Outputs:
- policy_value: float32 [256, 128, 512], P('liq', 'ill')
The draws below stay inside these ranges and needn't reach their ends.
Inputs may be any that keep to these rules, and one draw needn't show every extreme that they name: `flag_liq`: one marks a drift toward higher liquid assets, zero toward lower. `flag_ill`: one marks a drift toward higher illiquid assets, zero toward lower. jump_rates[j, i] is the rate of a jump from income state i to state j; the diagonal is zero and no entry is negative.
All inputs are finite; a program needn't handle non-finite values. No bound on the sum of `flag_liq` or of `flag_ill` on one device may be relied on, other than what follows from the above.
Results may differ from the reference program's by a relative error of at most 0.00026.
Values sent between devices are 32-bit elements; how exact they have to be, the bound alone decides.
No kernel may reach another device: no remote copies, remote signals or barrier semaphores. Data moves between devices by JAX's collectives and lax.ppermute only.
A program may use at most 64 MiB of HBM per device.

```python
import math
import jax
import jax.numpy as jnp
from jax import lax

NZ = 512
SWEEPS = 4
NA = 256
NB = 128


def draw_jump_rates(key, part):
    key = jax.random.fold_in(key, 7)
    first = jax.random.fold_in(key, 0)
    values = jax.random.uniform(first, (NZ, NZ), jnp.float32) * (2.0 / NZ)
    rows = lax.broadcasted_iota(jnp.int32, (NZ, NZ), 0)
    cols = lax.broadcasted_iota(jnp.int32, (NZ, NZ), 1)
    return jnp.where(rows == cols, jnp.zeros_like(values), values).astype(jnp.float32)


def plant(array, own_key, smallest, high):
    longest = array.shape.index(max(array.shape))
    spots = []
    for shift in (0, 1):
        where = [jax.random.randint(jax.random.fold_in(own_key, axis), (), 0, length) for axis, length in enumerate(array.shape)]
        where[longest] = (where[longest] + shift) % array.shape[longest]
        spots.append(tuple(where))
    return array.at[spots[0]].set(smallest).at[spots[1]].set(high)


def block_scale(rng, extent, pieces, least, largest):
    loudness = 1.0
    for position, shards_of in pieces:
        draws = jax.random.uniform(jax.random.fold_in(jax.random.fold_in(rng, 6), position), (shards_of,), jnp.float32, least / len(pieces), largest / len(pieces))
        loudness = loudness * jnp.repeat(jnp.exp(draws), extent[position] // shards_of).reshape((-1,) + (1,) * (len(extent) - 1 - position))
    return loudness


def centred(stream_key, extent, spread, most, shards=(), kind=jnp.bfloat16):
    gain = block_scale(stream_key, extent, shards, -0.22, 0.18) if shards else 1.0
    drawn = jax.random.normal(stream_key, extent, jnp.float32) * spread * gain
    return jnp.minimum(jnp.maximum(drawn, -most), most).astype(kind)


def setup_inputs(seed: int = 0) -> dict:
    key_of = jax.random.split(jax.random.key(seed), 8)
    right_side = centred(key_of[0], (NA, NB, NZ), 1.0, 6.0, ((0, 32), (1, 16)), jnp.float32)
    value_guess = centred(key_of[1], (NA, NB, NZ), 1.0, 6.0, ((0, 32), (1, 16)), jnp.float32)
    speed_liq = jnp.clip(jnp.exp(math.log(2000.0) - 2.3025851 * jax.random.uniform(key_of[2], (NA, NB, NZ), jnp.float32) ** block_scale(key_of[2], (NA, NB, NZ), ((0, 32), (1, 16)), -0.2, 0.2)), 200.0, 2000.0)
    speed_ill = jnp.clip(jnp.exp(math.log(5.0) - 2.3025851 * jax.random.uniform(key_of[3], (NA, NB, NZ), jnp.float32) ** block_scale(key_of[3], (NA, NB, NZ), ((0, 32), (1, 16)), -0.2, 0.2)), 0.5, 5.0)
    flag_liq = plant((jax.random.randint(key_of[4], (NA, NB, NZ), 0, 2) < 1).astype(jnp.int32), jax.random.fold_in(key_of[4], 1), 0, 1)
    flag_ill = plant((jax.random.randint(key_of[5], (NA, NB, NZ), 0, 2) < 1).astype(jnp.int32), jax.random.fold_in(key_of[5], 1), 0, 1)
    jump_rates = draw_jump_rates(jax.random.fold_in(key_of[7], 71), 0)
    return dict(right_side=right_side, value_guess=value_guess, speed_liq=speed_liq, speed_ill=speed_ill, flag_liq=flag_liq, flag_ill=flag_ill, jump_rates=jump_rates)


OMEGA = 0.8
DISCOUNT = 0.05
HIGH = lax.Precision.HIGHEST

def income_part(field, jump_rates):
    rows = field.reshape(-1, field.shape[2])
    return jnp.dot(rows, jump_rates, precision=HIGH).reshape(field.shape)

def diagonal_of(fwd_a, bwd_a, fwd_b, bwd_b, outflow):
    return DISCOUNT + fwd_a + bwd_a + fwd_b + bwd_b + outflow[None, None, :]

def residual_of(padded, rhs, coefs, jump_rates):
    fwd_a, bwd_a, fwd_b, bwd_b, diag = coefs
    center = padded[1:-1, 1:-1]
    applied = diag * center - fwd_a * padded[2:, 1:-1] - bwd_a * padded[:-2, 1:-1]
    applied = applied - fwd_b * padded[1:-1, 2:] - bwd_b * padded[1:-1, :-2]
    applied = applied - income_part(center, jump_rates)
    return rhs - applied

def relax(padded, rhs, coefs, jump_rates):
    return padded[1:-1, 1:-1] + OMEGA * residual_of(padded, rhs, coefs, jump_rates) / coefs[4]

def restrict(field):
    size_a, size_b, size_z = field.shape
    return field.reshape(size_a // 2, 2, size_b // 2, 2, size_z).mean(axis=(1, 3))

def prolong(field):
    size_a, size_b, size_z = field.shape
    wide = jnp.broadcast_to(field[:, None, :, None, :], (size_a, 2, size_b, 2, size_z))
    return wide.reshape(2 * size_a, 2 * size_b, size_z)

def coarser(coefs):
    return tuple((0.5 * restrict(entry) for entry in coefs))

def line_solve(rhs, coefs):
    fwd_a, bwd_a, fwd_b, bwd_b, diag = coefs
    lower = jnp.transpose(-bwd_a, (1, 2, 0))
    upper = jnp.transpose(-fwd_a, (1, 2, 0))
    middle = jnp.transpose(diag, (1, 2, 0))
    length = lower.shape[2]
    place = lax.broadcasted_iota(jnp.int32, lower.shape, 2)
    lower = jnp.where(place == 0, jnp.zeros_like(lower), lower)
    upper = jnp.where(place == length - 1, jnp.zeros_like(upper), upper)
    target = jnp.transpose(rhs, (1, 2, 0))[..., None]
    solved = lax.linalg.tridiagonal_solve(lower, middle, upper, target)[..., 0]
    return jnp.transpose(solved, (2, 0, 1))

def pad_both(field):
    return jnp.pad(field, ((1, 1), (1, 1), (0, 0)))

def reference(right_side, value_guess, speed_liq, speed_ill, flag_liq, flag_ill, jump_rates):
    outflow = jnp.sum(jump_rates, axis=0)
    up_liq = flag_liq.astype(jnp.float32)
    up_ill = flag_ill.astype(jnp.float32)
    fine4 = (speed_liq * up_liq, speed_liq * (1.0 - up_liq), speed_ill * up_ill, speed_ill * (1.0 - up_ill))
    fine = fine4 + (diagonal_of(*fine4, outflow),)
    mid4 = coarser(fine4)
    mid = mid4 + (diagonal_of(*mid4, outflow),)
    low4 = coarser(mid4)
    low = low4 + (diagonal_of(*low4, outflow),)
    value = value_guess
    for step in range(2):
        value = relax(pad_both(value), right_side, fine, jump_rates)
    rhs_mid = restrict(residual_of(pad_both(value), right_side, fine, jump_rates))
    error_mid = OMEGA * rhs_mid / mid[4]
    error_mid = relax(pad_both(error_mid), rhs_mid, mid, jump_rates)
    rhs_low = restrict(residual_of(pad_both(error_mid), rhs_mid, mid, jump_rates))
    error_low = line_solve(rhs_low, low)
    for step in range(SWEEPS - 1):
        padded = jnp.pad(error_low, ((0, 0), (1, 1), (0, 0)))
        target = rhs_low + low[2] * padded[:, 2:] + low[3] * padded[:, :-2] + income_part(error_low, jump_rates)
        error_low = line_solve(target, low)
    error_mid = error_mid + prolong(error_low)
    for step in range(2):
        error_mid = relax(pad_both(error_mid), rhs_mid, mid, jump_rates)
    value = value + prolong(error_mid)
    for step in range(2):
        value = relax(pad_both(value), right_side, fine, jump_rates)
    return value
```

```python
import functools

import jax
import jax.numpy as jnp
from jax import lax
from jax.experimental import pallas as pl
from jax.experimental.pallas import tpu as pltpu
from jax.sharding import PartitionSpec as P

SWEEPS = 4
OMEGA = 0.8
DISCOUNT = 0.05
LANES = 128
F32 = jnp.float32
BF16 = jnp.bfloat16

Z = 4
TILE = 8


def first_half(shape):
    return lax.broadcasted_iota(jnp.int32, shape, len(shape) - 2) % TILE < Z


def swapped(x):
    return pltpu.roll(x.reshape(-1, TILE, LANES), Z, 1).reshape(x.shape)


def later(x):
    return pltpu.roll(x, x.shape[0] - Z, 0)


def earlier(x):
    return pltpu.roll(x, Z, 0)


def pair_sums(x):
    total = x + swapped(x)
    total = total.reshape(-1, 2, TILE, LANES)
    first, second = total[:, 0], total[:, 1]
    return jnp.where(first_half(first.shape), first, second).reshape(-1, LANES)


def doubled(x):
    other = swapped(x).reshape(-1, 1, TILE, LANES)
    x = x.reshape(-1, 1, TILE, LANES)
    mask = first_half(x.shape)
    pair = jnp.concatenate([jnp.where(mask, x, other), jnp.where(mask, other, x)], axis=1)
    return pair.reshape(-1, LANES)


def spread(outflow, rows):
    return jnp.concatenate([outflow] * (rows // TILE), axis=0)


def row(ref, a, width):
    return ref[pl.ds(a * width, width), :]


def product(wide, jhi_ref, jlo_ref):
    high = wide.astype(BF16)
    rest = (wide - high.astype(F32)).astype(BF16)
    dot = functools.partial(jnp.dot, preferred_element_type=F32)
    return dot(high, jhi_ref[...]) + (dot(high, jlo_ref[...]) + dot(rest, jhi_ref[...]))


def income(src, dst, pieces, jhi_ref, jlo_ref):
    wide = jnp.concatenate(
        [
            jnp.concatenate([src[pl.ds(s + c, n, stride=Z), :] for s, _, n in pieces], axis=0)
            for c in range(Z)
        ],
        axis=1,
    )
    result = product(wide, jhi_ref, jlo_ref)
    at = 0
    for _, d, n in pieces:
        for c in range(Z):
            dst[pl.ds(d + c, n, stride=Z), :] = result[at : at + n, c * LANES : (c + 1) * LANES]
        at += n


def rates_kernel(j_ref, jhi_ref, jlo_ref, out_ref):
    rates = j_ref[...]
    high = rates.astype(BF16)
    jhi_ref[...] = high
    jlo_ref[...] = (rates - high.astype(F32)).astype(BF16)
    total = jnp.sum(rates, axis=0, keepdims=True)
    for c in range(Z):
        piece = total[:, c * LANES : (c + 1) * LANES]
        out_ref[c : c + 1, :] = piece
        out_ref[c + Z : c + Z + 1, :] = piece


def pack_kernel(rhs, value, speed_a, speed_b, flag_a, flag_b, lo_ref, hi_ref):
    half = lo_ref.shape[2] // Z
    for a in range(rhs.shape[0]):
        up_a = flag_a[a].astype(F32)
        up_b = flag_b[a].astype(F32)
        fields = (
            value[a],
            rhs[a],
            speed_a[a] * up_a,
            speed_a[a] * (1.0 - up_a),
            speed_b[a] * up_b,
            speed_b[a] * (1.0 - up_b),
        )
        for k, x in enumerate(fields):
            for c in range(Z):
                piece = x[:, c * LANES : (c + 1) * LANES]
                lo_ref[k, a, pl.ds(c, half, stride=Z), :] = piece[:half]
                hi_ref[k, a, pl.ds(c, half, stride=Z), :] = piece[half:]


def widen_kernel(lo, hi, below, above, first_ref, second_ref):
    width = lo.shape[2]
    for out, start in ((first_ref, 0), (second_ref, 4)):
        for i, src in enumerate((below, lo, hi, above)):
            out[:, :, i * width : (i + 1) * width, :] = src[:, start : start + 4]


def fine_kernel(
    below, first, second, above, jhi, jlo, out,
    fine_ref, val_ref, rlo_ref, rhi_ref, mid_ref, low_ref, v0, v1, inc, res,
):
    outflow = spread(out[...], 64)
    for a in range(16):
        src = (below, first, second, above)[a // 4]
        here = pl.ds(64 * a, 64)
        v0[here, :] = src[0, a % 4]
        total = DISCOUNT + outflow
        for k in range(1, 6):
            x = src[k, a % 4]
            fine_ref[k - 1, here, :] = x
            if k > 1:
                total = total + x
        fine_ref[5, here, :] = OMEGA / total

    def applied(src, a):
        here = pl.ds(64 * a, 64)
        center = src[here, :]
        total = fine_ref[0, here, :] + inc[here, :]
        total = total + fine_ref[1, here, :] * row(src, a + 1, 64)
        total = total + fine_ref[2, here, :] * row(src, a - 1, 64)
        total = total + fine_ref[3, here, :] * later(center)
        total = total + fine_ref[4, here, :] * earlier(center)
        return center, total

    def sweep(src, dst, begin, end):
        income(src, inc, [(64 * begin, 64 * begin, 16 * (end - begin))], jhi, jlo)
        for a in range(begin, end):
            center, total = applied(src, a)
            here = pl.ds(64 * a, 64)
            dst[here, :] = (1.0 - OMEGA) * center + fine_ref[5, here, :] * total

    sweep(v0, v1, 1, 15)
    sweep(v1, val_ref, 2, 14)
    income(val_ref, inc, [(64 * 4, 64 * 4, 16 * 8)], jhi, jlo)

    def residual(a):
        center, total = applied(val_ref, a)
        here = pl.ds(64 * a, 64)
        diag = DISCOUNT + outflow
        for k in range(1, 5):
            diag = diag + fine_ref[k, here, :]
        return (total - diag * center)[16:48]

    for m in range(4):
        coarse = 0.25 * pair_sums(residual(4 + 2 * m) + residual(5 + 2 * m))
        rlo_ref[pl.ds(8 * m, 8), :] = coarse[:8]
        rhi_ref[pl.ds(8 * m, 8), :] = coarse[8:]

    outflow = spread(out[...], 32)
    for m in range(8):
        here = pl.ds(32 * m, 32)
        total = DISCOUNT + outflow
        for k in range(4):
            both = fine_ref[k + 1, pl.ds(128 * m, 64), :] + fine_ref[k + 1, pl.ds(128 * m + 64, 64), :]
            x = 0.125 * pair_sums(both)
            mid_ref[k, here, :] = x
            total = total + x
        mid_ref[4, here, :] = OMEGA / total
    for k in range(4):
        for m in range(2):
            at = 32 * (2 + 2 * m) + 8
            both = mid_ref[k, pl.ds(at, 16), :] + mid_ref[k, pl.ds(at + 32, 16), :]
            low_ref[k, pl.ds(8 * m, 8), :] = 0.125 * pair_sums(both)


def widen_mid_kernel(lo, hi, below, above, first_ref, second_ref):
    for m in range(4):
        out = (first_ref, second_ref)[m // 2]
        for i, src in enumerate((below, lo, hi, above)):
            out[pl.ds(32 * (m % 2) + 8 * i, 8), :] = src[pl.ds(8 * m, 8), :]


def mid_kernel(
    below, first, second, above, mid, low, jhi, jlo, out, pay_ref, err_ref, rhs_ref, e0, e1, inc
):
    for i, src in enumerate((below, first, second, above)):
        rhs_ref[pl.ds(64 * i, 64), :] = src[...]
    e0[...] = mid[4] * rhs_ref[...]

    def applied(src, a):
        here = pl.ds(32 * a, 32)
        center = src[here, :]
        total = rhs_ref[here, :] + inc[here, :]
        total = total + mid[0, here, :] * row(src, a + 1, 32)
        total = total + mid[1, here, :] * row(src, a - 1, 32)
        total = total + mid[2, here, :] * later(center)
        total = total + mid[3, here, :] * earlier(center)
        return center, total

    income(e0, inc, [(32, 32, 8 * 6)], jhi, jlo)
    for a in range(1, 7):
        center, total = applied(e0, a)
        here = pl.ds(32 * a, 32)
        e1[here, :] = (1.0 - OMEGA) * center + mid[4, here, :] * total
    income(e1, inc, [(64, 64, 8 * 4)], jhi, jlo)
    outflow = spread(out[...], 32)

    def residual(a):
        center, total = applied(e1, a)
        here = pl.ds(32 * a, 32)
        diag = DISCOUNT + outflow
        for k in range(4):
            diag = diag + mid[k, here, :]
        return (total - diag * center)[8:24]

    for m in range(2):
        pay_ref[pl.ds(8 * m, 8), :] = 0.25 * pair_sums(residual(2 + 2 * m) + residual(3 + 2 * m))
    for k in range(4):
        pay_ref[pl.ds(16 * (k + 1), 16), :] = low[k]
    for a in range(4):
        err_ref[pl.ds(16 * a, 16), :] = e1[pl.ds(32 * (a + 2) + 8, 16), :]


def solve_lines(target, weight, carry, link, middle, y, x_ref, offset):
    count = y.shape[0] // TILE
    half = count // 2
    top = bottom = None
    for i in range(half):
        j = count - 1 - i
        t = weight(i) * target(i)
        u = weight(j) * target(j)
        top = t if i == 0 else t + carry(i) * top
        bottom = u if i == 0 else u + carry(j) * bottom
        if i < half - 1:
            y[pl.ds(TILE * i, TILE), :] = top
            y[pl.ds(TILE * j, TILE), :] = bottom
    head = (top + link(half - 1) * bottom) * middle
    tail = bottom + link(half) * head
    for i in range(half - 1, -1, -1):
        j = count - 1 - i
        if i < half - 1:
            head = row(y, i, TILE) + link(i) * head
            tail = row(y, j, TILE) + link(j) * tail
        x_ref[pl.ds(offset + TILE * i, TILE), :] = head
        x_ref[pl.ds(offset + TILE * j, TILE), :] = tail


def send_lines(e, lo_ref, hi_ref):
    pairs = e[...].reshape(-1, 2, TILE, LANES)
    first, second = pairs[:, 0], pairs[:, 1]
    mask = first_half(first.shape)
    lo_ref[...] = jnp.where(mask, first, pltpu.roll(second, Z, 1)).reshape(-1, LANES)
    hi_ref[...] = jnp.where(mask, pltpu.roll(first, Z, 1), second).reshape(-1, LANES)


def first_solve_kernel(gathered, out, fac_ref, middle_ref, e_ref, lo_ref, hi_ref, y):
    count = e_ref.shape[0] // TILE
    half = count // 2

    def part(k, a):
        return gathered[pl.ds(80 * (a // 2) + 16 * k + 8 * (a % 2), TILE), :]

    outflow = DISCOUNT + out[...]
    gaps = [None, None]
    links = [None, None]
    for i in range(half):
        for side, a in ((0, i), (1, count - 1 - i)):
            here = pl.ds(TILE * a, TILE)
            inner, outer = (part(1, a), part(2, a)) if side == 0 else (part(2, a), part(1, a))
            fb, bb = part(3, a), part(4, a)
            slack = outflow + fb + bb
            slack = slack + (outer if i == 0 else outer * gaps[side])
            weight = 1.0 / (slack + inner)
            links[side] = inner * weight
            gaps[side] = slack * weight
            fac_ref[0, here, :] = part(0, a)
            fac_ref[1, here, :] = fb
            fac_ref[2, here, :] = bb
            fac_ref[3, here, :] = weight
            fac_ref[4, here, :] = outer * weight
            fac_ref[5, here, :] = links[side]
    middle_ref[...] = 1.0 / (gaps[0] + links[0] * gaps[1])
    solve_lines(
        lambda a: row(fac_ref.at[0], a, TILE),
        lambda a: row(fac_ref.at[3], a, TILE),
        lambda a: row(fac_ref.at[4], a, TILE),
        lambda a: row(fac_ref.at[5], a, TILE),
        middle_ref[...], y, e_ref, 0,
    )
    send_lines(e_ref, lo_ref, hi_ref)


def local_target_kernel(e, fac, jhi, jlo, t_ref):
    income(e, t_ref, [(0, 0, e.shape[0] // Z)], jhi, jlo)
    other = swapped(e[...])
    mask = first_half(other.shape)
    t_ref[...] = t_ref[...] + fac[0] + jnp.where(mask, fac[1], fac[2]) * other


def swept(t, fac, middle, below, above, y, x_ref, offset):
    mask = first_half((TILE, LANES))

    def target(a):
        low_side, high_side = row(below, a // 2, TILE), row(above, a // 2, TILE)
        if a % 2:
            low_side = pltpu.roll(low_side, Z, 0)
        else:
            high_side = pltpu.roll(high_side, Z, 0)
        near = jnp.where(mask, low_side, high_side)
        coupling = jnp.where(mask, row(fac.at[2], a, TILE), row(fac.at[1], a, TILE))
        return row(t, a, TILE) + coupling * near

    solve_lines(
        target,
        lambda a: row(fac.at[3], a, TILE),
        lambda a: row(fac.at[4], a, TILE),
        lambda a: row(fac.at[5], a, TILE),
        middle[...], y, x_ref, offset,
    )


def sweep_kernel(t, fac, middle, below, above, e_ref, lo_ref, hi_ref, y):
    swept(t, fac, middle, below, above, y, e_ref, 0)
    send_lines(e_ref, lo_ref, hi_ref)


def last_sweep_kernel(place, t, fac, middle, below, above, err, err_lo, err_hi, sum_ref, y, x):
    edge = 2 * TILE
    x[0:edge, :] = jnp.zeros((edge, LANES), F32)
    x[pl.ds(x.shape[0] - edge, edge), :] = jnp.zeros((edge, LANES), F32)
    swept(t, fac, middle, below, above, y, x, edge)
    start = place[0] * 2 * TILE
    for i in range(6):
        low = x[pl.ds(pl.multiple_of(start + i * TILE, TILE), TILE), :]
        fill = doubled(low)
        for m in (2 * i, 2 * i + 1):
            src = (err_lo, err, err_hi)[m // 4]
            sum_ref[pl.ds(16 * m, 16), :] = src[pl.ds(16 * (m % 4), 16), :] + fill


def last_kernel(
    own, below, above, mid, rhs_mid, fine, val, jhi, jlo, out_ref, ev, e1, e2, v0, v1, v2, inc
):
    for a in range(12):
        for i, src in enumerate((below, own, above)):
            ev[pl.ds(48 * a + 16 * i, 16), :] = src[pl.ds(16 * a, 16), :]

    income(ev, inc, [(48 * (a + 2) + 8, 32 * a, 8) for a in range(8)], jhi, jlo)
    for a in range(8):
        here = pl.ds(32 * a, 32)
        center = row(ev, a + 2, 48)
        total = rhs_mid[here, :] + inc[here, :]
        total = total + mid[0, here, :] * ev[pl.ds(48 * (a + 3) + 8, 32), :]
        total = total + mid[1, here, :] * ev[pl.ds(48 * (a + 1) + 8, 32), :]
        total = total + mid[2, here, :] * later(center)[8:40]
        total = total + mid[3, here, :] * earlier(center)[8:40]
        e1[here, :] = (1.0 - OMEGA) * center[8:40] + mid[4, here, :] * total

    income(e1, inc, [(32, 32, 8 * 6)], jhi, jlo)
    for a in range(1, 7):
        here = pl.ds(32 * a, 32)
        center = e1[here, :]
        total = rhs_mid[here, :] + inc[here, :]
        total = total + mid[0, here, :] * row(e1, a + 1, 32)
        total = total + mid[1, here, :] * row(e1, a - 1, 32)
        total = total + mid[2, here, :] * later(center)
        total = total + mid[3, here, :] * earlier(center)
        error = (1.0 - OMEGA) * center + mid[4, here, :] * total
        fill = doubled(error)
        for f in (2 * a, 2 * a + 1):
            v0[pl.ds(64 * f, 64), :] = val[pl.ds(64 * f, 64), :] + fill

    def sweep(src, dst, begin, end):
        income(src, inc, [(64 * begin, 64 * begin, 16 * (end - begin))], jhi, jlo)
        for a in range(begin, end):
            here = pl.ds(64 * a, 64)
            center = src[here, :]
            total = fine[0, here, :] + inc[here, :]
            total = total + fine[1, here, :] * row(src, a + 1, 64)
            total = total + fine[2, here, :] * row(src, a - 1, 64)
            total = total + fine[3, here, :] * later(center)
            total = total + fine[4, here, :] * earlier(center)
            dst[here, :] = (1.0 - OMEGA) * center + fine[5, here, :] * total

    sweep(v0, v1, 3, 13)
    sweep(v1, v2, 4, 12)
    for a in range(8):
        for c in range(Z):
            piece = v2[pl.ds(64 * (a + 4) + 16 + c, 8, stride=Z), :]
            out_ref[a, :, c * LANES : (c + 1) * LANES] = piece


def call(kernel, args, outs, scratch=(), flops=0, smem=0, limit=32):
    outs = [jax.ShapeDtypeStruct(*o) if isinstance(o, tuple) and isinstance(o[0], tuple) else jax.ShapeDtypeStruct(o, F32) for o in outs]
    spec = pl.BlockSpec(memory_space=pltpu.VMEM)
    moved = sum(x.size * x.dtype.itemsize for x in (*args, *outs))
    return pl.pallas_call(
        kernel,
        out_shape=outs,
        in_specs=[pl.BlockSpec(memory_space=pltpu.SMEM)] * smem + [spec] * (len(args) - smem),
        out_specs=[spec] * len(outs),
        scratch_shapes=[pltpu.VMEM(s, F32) for s in scratch],
        compiler_params=pltpu.CompilerParams(vmem_limit_bytes=limit * 2**20),
        cost_estimate=pl.CostEstimate(flops=flops, bytes_accessed=moved, transcendentals=0),
    )(*args)


def neighbours(lo, hi, axis):
    count = lax.axis_size(axis)
    below = lax.ppermute(hi, axis, [(i, i + 1) for i in range(count - 1)])
    above = lax.ppermute(lo, axis, [(i + 1, i) for i in range(count - 1)])
    return below, above


def body(right_side, value_guess, speed_liq, speed_ill, flag_liq, flag_ill, jump_rates):
    nz = jump_rates.shape[0]
    dot_flops = 2 * 3 * nz * nz
    half = (6, 8, 16, LANES)
    lo, hi = call(
        pack_kernel,
        (right_side, value_guess, speed_liq, speed_ill, flag_liq, flag_ill),
        [half, half],
    )
    jhi, jlo, out = call(
        rates_kernel, (jump_rates,), [((nz, nz), BF16), ((nz, nz), BF16), (TILE, LANES)]
    )
    below, above = neighbours(lo, hi, "ill")
    wide = (6, 4, 64, LANES)
    first, second = call(widen_kernel, (lo, hi, below, above), [wide, wide])
    below, above = neighbours(first, second, "liq")
    whole = (1024, LANES)
    fine, value, rlo, rhi, mid, low = call(
        fine_kernel,
        (below, first, second, above, jhi, jlo, out),
        [(6, 1024, LANES), whole, (32, LANES), (32, LANES), (5, 256, LANES), (4, 16, LANES)],
        [whole] * 4,
        flops=dot_flops * 550,
    )
    below, above = neighbours(rlo, rhi, "ill")
    first, second = call(widen_mid_kernel, (rlo, rhi, below, above), [(64, LANES)] * 2)
    below, above = neighbours(first, second, "liq")
    payload, error_mid, rhs_mid = call(
        mid_kernel,
        (below, first, second, above, mid, low, jhi, jlo, out),
        [(80, LANES), (64, LANES), (256, LANES)],
        [(256, LANES)] * 3,
        flops=dot_flops * 80,
    )
    err_lo, err_hi = neighbours(error_mid, error_mid, "liq")
    gathered = lax.all_gather(payload, "liq", axis=0, tiled=True)
    lines = gathered.shape[0] // 80 * 2 * TILE
    line, message = (lines, LANES), (lines // 2, LANES)
    fac, middle, e, lo, hi = call(
        first_solve_kernel, (gathered, out), [(6, *line), (TILE, LANES), line, message, message], [line]
    )
    for step in range(SWEEPS - 1):
        below, above = neighbours(lo, hi, "ill")
        (target,) = call(
            local_target_kernel, (e, fac, jhi, jlo), [line], flops=dot_flops * lines // Z
        )
        if step < SWEEPS - 2:
            e, lo, hi = call(
                sweep_kernel, (target, fac, middle, below, above), [line, message, message], [line]
            )
    place = lax.axis_index("liq").astype(jnp.int32).reshape(1)
    (total,) = call(
        last_sweep_kernel,
        (place, target, fac, middle, below, above, error_mid, err_lo, err_hi),
        [(192, LANES)],
        [line, (lines + 4 * TILE, LANES)],
        smem=1,
    )
    below, above = neighbours(total, total, "ill")
    (result,) = call(
        last_kernel,
        (total, below, above, mid, rhs_mid, fine, value, jhi, jlo),
        [right_side.shape],
        [(576, LANES), (256, LANES), (256, LANES), whole, whole, whole, whole],
        flops=dot_flops * 400,
    )
    return result


def solution(mesh):
    block = P("liq", "ill", None)
    return jax.shard_map(
        body, mesh=mesh, in_specs=(block,) * 6 + (P(),), out_specs=block, check_vma=False
    )
```

```python
import functools

import jax
import jax.numpy as jnp
from jax import lax
from jax.experimental import pallas as pl
from jax.experimental.pallas import tpu as pltpu
from jax.sharding import PartitionSpec as P

SWEEPS = 4
OMEGA = 0.8
DISCOUNT = 0.05
LANES = 128
F32 = jnp.float32
BF16 = jnp.bfloat16

Z = 4
TILE = 8


def first_half(shape):
    return lax.broadcasted_iota(jnp.int32, shape, len(shape) - 2) % TILE < Z


def swapped(x):
    return pltpu.roll(x.reshape(-1, TILE, LANES), Z, 1).reshape(x.shape)


def later(x):
    return pltpu.roll(x, x.shape[0] - Z, 0)


def earlier(x):
    return pltpu.roll(x, Z, 0)


def pair_sums(x):
    total = x + swapped(x)
    total = total.reshape(-1, 2, TILE, LANES)
    first, second = total[:, 0], total[:, 1]
    return jnp.where(first_half(first.shape), first, second).reshape(-1, LANES)


def doubled(x):
    other = swapped(x).reshape(-1, 1, TILE, LANES)
    x = x.reshape(-1, 1, TILE, LANES)
    mask = first_half(x.shape)
    pair = jnp.concatenate([jnp.where(mask, x, other), jnp.where(mask, other, x)], axis=1)
    return pair.reshape(-1, LANES)


def spread(outflow, rows):
    return jnp.concatenate([outflow] * (rows // TILE), axis=0)


def row(ref, a, width):
    return ref[pl.ds(a * width, width), :]


def product(wide, jhi_ref, jlo_ref):
    high = wide.astype(BF16)
    rest = (wide - high.astype(F32)).astype(BF16)
    dot = functools.partial(jnp.dot, preferred_element_type=F32)
    return dot(high, jhi_ref[...]) + (dot(high, jlo_ref[...]) + dot(rest, jhi_ref[...]))


def income(src, dst, pieces, jhi_ref, jlo_ref):
    wide = jnp.concatenate(
        [
            jnp.concatenate([src[pl.ds(s + c, n, stride=Z), :] for s, _, n in pieces], axis=0)
            for c in range(Z)
        ],
        axis=1,
    )
    result = product(wide, jhi_ref, jlo_ref)
    at = 0
    for _, d, n in pieces:
        for c in range(Z):
            dst[pl.ds(d + c, n, stride=Z), :] = result[at : at + n, c * LANES : (c + 1) * LANES]
        at += n


def rates_kernel(j_ref, jhi_ref, jlo_ref, out_ref):
    rates = j_ref[...]
    high = rates.astype(BF16)
    jhi_ref[...] = high
    jlo_ref[...] = (rates - high.astype(F32)).astype(BF16)
    total = jnp.sum(rates, axis=0, keepdims=True)
    for c in range(Z):
        piece = total[:, c * LANES : (c + 1) * LANES]
        out_ref[c : c + 1, :] = piece
        out_ref[c + Z : c + Z + 1, :] = piece


def pack_kernel(*refs):
    sources, (lo_ref, hi_ref, low_ref), buffers = refs[:6], refs[6:9], refs[9:15]
    mid, sems = refs[15:]
    copies = [
        pltpu.make_async_copy(src, dst, sems.at[i])
        for i, (src, dst) in enumerate(zip(sources, buffers))
    ]
    for copy in copies:
        copy.start()
    rhs, value, speed_a, speed_b, flag_a, flag_b = buffers
    half = lo_ref.shape[2] // Z

    def put(k, a, x):
        for c in range(Z):
            piece = x[:, c * LANES : (c + 1) * LANES]
            lo_ref[k, a, pl.ds(c, half, stride=Z), :] = piece[:half]
            hi_ref[k, a, pl.ds(c, half, stride=Z), :] = piece[half:]

    for copy in copies[2:]:
        copy.wait()
    points = rhs.shape[0]
    for a in range(points):
        for k, speed, flag in ((2, speed_a, flag_a), (4, speed_b, flag_b)):
            up = flag[a].astype(F32)
            put(k, a, speed[a] * up)
            put(k + 1, a, speed[a] * (1.0 - up))
    for k in range(2, 6):
        for m in range(points // 2):
            for i, src in enumerate((lo_ref, hi_ref)):
                both = src[k, 2 * m] + src[k, 2 * m + 1]
                mid[pl.ds(16 * m + 8 * i, 8), :] = 0.125 * pair_sums(both)
        for m in range(points // 4):
            both = mid[pl.ds(32 * m, 16), :] + mid[pl.ds(32 * m + 16, 16), :]
            low_ref[pl.ds(16 * (k - 2) + 8 * m, 8), :] = 0.125 * pair_sums(both)
    for copy in copies[:2]:
        copy.wait()
    for a in range(points):
        put(0, a, value[a])
        put(1, a, rhs[a])


def widen_kernel(lo, hi, below, above, first_ref, second_ref):
    width = lo.shape[2]
    for out, start in ((first_ref, 0), (second_ref, 4)):
        for i, src in enumerate((below, lo, hi, above)):
            out[:, :, i * width : (i + 1) * width, :] = src[:, start : start + 4]


def fine_kernel(
    below, first, second, above, jhi, jlo, out,
    fine_out, val_out, rlo_ref, rhi_ref, mid_ref, fine_ref, val_ref, v0, v1, inc, sems,
):
    outflow = spread(out[...], 64)
    for a in range(16):
        src = (below, first, second, above)[a // 4]
        here = pl.ds(64 * a, 64)
        v0[here, :] = src[0, a % 4]
        total = DISCOUNT + outflow
        for k in range(1, 6):
            x = src[k, a % 4]
            fine_ref[k - 1, here, :] = x
            if k > 1:
                total = total + x
        fine_ref[5, here, :] = OMEGA / total
    keep_fine = pltpu.make_async_copy(fine_ref, fine_out, sems.at[0])
    keep_fine.start()

    def applied(src, a):
        here = pl.ds(64 * a, 64)
        center = src[here, :]
        total = fine_ref[0, here, :] + inc[here, :]
        total = total + fine_ref[1, here, :] * row(src, a + 1, 64)
        total = total + fine_ref[2, here, :] * row(src, a - 1, 64)
        total = total + fine_ref[3, here, :] * later(center)
        total = total + fine_ref[4, here, :] * earlier(center)
        return center, total

    def sweep(src, dst, begin, end):
        income(src, inc, [(64 * begin, 64 * begin, 16 * (end - begin))], jhi, jlo)
        for a in range(begin, end):
            center, total = applied(src, a)
            here = pl.ds(64 * a, 64)
            dst[here, :] = (1.0 - OMEGA) * center + fine_ref[5, here, :] * total

    sweep(v0, v1, 1, 15)
    sweep(v1, val_ref, 2, 14)
    edge = jnp.zeros((128, LANES), F32)
    val_ref[0:128, :] = edge
    val_ref[896:1024, :] = edge
    keep_val = pltpu.make_async_copy(val_ref, val_out, sems.at[1])
    keep_val.start()
    income(val_ref, inc, [(64 * 4, 64 * 4, 16 * 8)], jhi, jlo)

    def residual(a):
        center, total = applied(val_ref, a)
        here = pl.ds(64 * a, 64)
        diag = DISCOUNT + outflow
        for k in range(1, 5):
            diag = diag + fine_ref[k, here, :]
        return (total - diag * center)[16:48]

    for m in range(4):
        coarse = 0.25 * pair_sums(residual(4 + 2 * m) + residual(5 + 2 * m))
        rlo_ref[pl.ds(8 * m, 8), :] = coarse[:8]
        rhi_ref[pl.ds(8 * m, 8), :] = coarse[8:]

    outflow = spread(out[...], 32)
    for m in range(8):
        here = pl.ds(32 * m, 32)
        total = DISCOUNT + outflow
        for k in range(4):
            both = fine_ref[k + 1, pl.ds(128 * m, 64), :] + fine_ref[k + 1, pl.ds(128 * m + 64, 64), :]
            x = 0.125 * pair_sums(both)
            mid_ref[k, here, :] = x
            total = total + x
        mid_ref[4, here, :] = OMEGA / total
    keep_fine.wait()
    keep_val.wait()


def widen_mid_kernel(lo, hi, below, above, first_ref, second_ref):
    for m in range(4):
        out = (first_ref, second_ref)[m // 2]
        for i, src in enumerate((below, lo, hi, above)):
            out[pl.ds(32 * (m % 2) + 8 * i, 8), :] = src[pl.ds(8 * m, 8), :]


def mid_kernel(
    below, first, second, above, mid, jhi, jlo, out, pay_ref, err_ref, rhs_ref, e0, e1, inc
):
    for i, src in enumerate((below, first, second, above)):
        rhs_ref[pl.ds(64 * i, 64), :] = src[...]
    e0[...] = mid[4] * rhs_ref[...]

    def applied(src, a):
        here = pl.ds(32 * a, 32)
        center = src[here, :]
        total = rhs_ref[here, :] + inc[here, :]
        total = total + mid[0, here, :] * row(src, a + 1, 32)
        total = total + mid[1, here, :] * row(src, a - 1, 32)
        total = total + mid[2, here, :] * later(center)
        total = total + mid[3, here, :] * earlier(center)
        return center, total

    income(e0, inc, [(32, 32, 8 * 6)], jhi, jlo)
    for a in range(1, 7):
        center, total = applied(e0, a)
        here = pl.ds(32 * a, 32)
        e1[here, :] = (1.0 - OMEGA) * center + mid[4, here, :] * total
    income(e1, inc, [(64, 64, 8 * 4)], jhi, jlo)
    outflow = spread(out[...], 32)

    def residual(a):
        center, total = applied(e1, a)
        here = pl.ds(32 * a, 32)
        diag = DISCOUNT + outflow
        for k in range(4):
            diag = diag + mid[k, here, :]
        return (total - diag * center)[8:24]

    for m in range(2):
        pay_ref[pl.ds(8 * m, 8), :] = 0.25 * pair_sums(residual(2 + 2 * m) + residual(3 + 2 * m))
    for a in range(4):
        err_ref[pl.ds(16 * a, 16), :] = e1[pl.ds(32 * (a + 2) + 8, 16), :]


def solve_lines(target, weight, carry, link, middle, y, x_ref, offset):
    count = y.shape[0] // TILE
    half = count // 2
    top = bottom = None
    for i in range(half):
        j = count - 1 - i
        t = weight(i) * target(i)
        u = weight(j) * target(j)
        top = t if i == 0 else t + carry(i) * top
        bottom = u if i == 0 else u + carry(j) * bottom
        if i < half - 1:
            y[pl.ds(TILE * i, TILE), :] = top
            y[pl.ds(TILE * j, TILE), :] = bottom
    head = (top + link(half - 1) * bottom) * middle
    tail = bottom + link(half) * head
    for i in range(half - 1, -1, -1):
        j = count - 1 - i
        if i < half - 1:
            head = row(y, i, TILE) + link(i) * head
            tail = row(y, j, TILE) + link(j) * tail
        x_ref[pl.ds(offset + TILE * i, TILE), :] = head
        x_ref[pl.ds(offset + TILE * j, TILE), :] = tail


def send_lines(e, lo_ref, hi_ref):
    pairs = e[...].reshape(-1, 2, TILE, LANES)
    first, second = pairs[:, 0], pairs[:, 1]
    mask = first_half(first.shape)
    lo_ref[...] = jnp.where(mask, first, pltpu.roll(second, Z, 1)).reshape(-1, LANES)
    hi_ref[...] = jnp.where(mask, pltpu.roll(first, Z, 1), second).reshape(-1, LANES)


def factor_kernel(gathered, out, fac_ref, middle_ref):
    count = fac_ref.shape[1] // TILE

    def part(k, a):
        return gathered[pl.ds(64 * (a // 2) + 16 * k + 8 * (a % 2), TILE), :]

    outflow = DISCOUNT + out[...]
    gaps = [None, None]
    links = [None, None]
    for i in range(count // 2):
        for side, a in ((0, i), (1, count - 1 - i)):
            here = pl.ds(TILE * a, TILE)
            inner, outer = (part(0, a), part(1, a)) if side == 0 else (part(1, a), part(0, a))
            fb, bb = part(2, a), part(3, a)
            slack = outflow + fb + bb
            slack = slack + (outer if i == 0 else outer * gaps[side])
            weight = 1.0 / (slack + inner)
            links[side] = inner * weight
            gaps[side] = slack * weight
            fac_ref[0, here, :] = fb
            fac_ref[1, here, :] = bb
            fac_ref[2, here, :] = weight
            fac_ref[3, here, :] = outer * weight
            fac_ref[4, here, :] = links[side]
    middle_ref[...] = 1.0 / (gaps[0] + links[0] * gaps[1])


def first_solve_kernel(
    rhs, fac, middle, err, err_lo, err_hi, e_ref, lo_ref, hi_ref, wide_ref, y
):
    for i, src in enumerate((err_lo, err, err_hi)):
        wide_ref[pl.ds(64 * i, 64), :] = src[...]
    solve_lines(
        lambda a: row(rhs, a, TILE),
        lambda a: row(fac.at[2], a, TILE),
        lambda a: row(fac.at[3], a, TILE),
        lambda a: row(fac.at[4], a, TILE),
        middle[...], y, e_ref, 0,
    )
    send_lines(e_ref, lo_ref, hi_ref)


def local_target_kernel(e, rhs, fac, jhi, jlo, t_ref):
    income(e, t_ref, [(0, 0, e.shape[0] // Z)], jhi, jlo)
    other = swapped(e[...])
    mask = first_half(other.shape)
    t_ref[...] = t_ref[...] + rhs[...] + jnp.where(mask, fac[0], fac[1]) * other


def swept(t, fac, middle, below, above, y, x_ref, offset):
    mask = first_half((TILE, LANES))

    def target(a):
        low_side, high_side = row(below, a // 2, TILE), row(above, a // 2, TILE)
        if a % 2:
            low_side = pltpu.roll(low_side, Z, 0)
        else:
            high_side = pltpu.roll(high_side, Z, 0)
        near = jnp.where(mask, low_side, high_side)
        coupling = jnp.where(mask, row(fac.at[1], a, TILE), row(fac.at[0], a, TILE))
        return row(t, a, TILE) + coupling * near

    solve_lines(
        target,
        lambda a: row(fac.at[2], a, TILE),
        lambda a: row(fac.at[3], a, TILE),
        lambda a: row(fac.at[4], a, TILE),
        middle[...], y, x_ref, offset,
    )


def sweep_kernel(t, fac, middle, below, above, e_ref, lo_ref, hi_ref, y):
    swept(t, fac, middle, below, above, y, e_ref, 0)
    send_lines(e_ref, lo_ref, hi_ref)


def last_sweep_kernel(place, t, fac, middle, below, above, err, sum_ref, y, x):
    edge = 2 * TILE
    x[0:edge, :] = jnp.zeros((edge, LANES), F32)
    x[pl.ds(x.shape[0] - edge, edge), :] = jnp.zeros((edge, LANES), F32)
    swept(t, fac, middle, below, above, y, x, edge)
    start = place[0] * 2 * TILE
    for i in range(6):
        low = x[pl.ds(pl.multiple_of(start + i * TILE, TILE), TILE), :]
        fill = doubled(low)
        for m in (2 * i, 2 * i + 1):
            sum_ref[pl.ds(16 * m, 16), :] = err[pl.ds(16 * m, 16), :] + fill


def last_kernel(
    own, below, above, mid, rhs_mid, fine, val, jhi, jlo, out_ref, ev, e1, e2, v0, v1, v2, inc
):
    for a in range(12):
        for i, src in enumerate((below, own, above)):
            ev[pl.ds(48 * a + 16 * i, 16), :] = src[pl.ds(16 * a, 16), :]

    income(ev, inc, [(48 * (a + 2) + 8, 32 * a, 8) for a in range(8)], jhi, jlo)
    for a in range(8):
        here = pl.ds(32 * a, 32)
        center = row(ev, a + 2, 48)
        total = rhs_mid[here, :] + inc[here, :]
        total = total + mid[0, here, :] * ev[pl.ds(48 * (a + 3) + 8, 32), :]
        total = total + mid[1, here, :] * ev[pl.ds(48 * (a + 1) + 8, 32), :]
        total = total + mid[2, here, :] * later(center)[8:40]
        total = total + mid[3, here, :] * earlier(center)[8:40]
        e1[here, :] = (1.0 - OMEGA) * center[8:40] + mid[4, here, :] * total

    income(e1, inc, [(32, 32, 8 * 6)], jhi, jlo)
    for a in range(1, 7):
        here = pl.ds(32 * a, 32)
        center = e1[here, :]
        total = rhs_mid[here, :] + inc[here, :]
        total = total + mid[0, here, :] * row(e1, a + 1, 32)
        total = total + mid[1, here, :] * row(e1, a - 1, 32)
        total = total + mid[2, here, :] * later(center)
        total = total + mid[3, here, :] * earlier(center)
        error = (1.0 - OMEGA) * center + mid[4, here, :] * total
        fill = doubled(error)
        for f in (2 * a, 2 * a + 1):
            v0[pl.ds(64 * f, 64), :] = val[pl.ds(64 * f, 64), :] + fill

    def sweep(src, dst, begin, end):
        income(src, inc, [(64 * begin, 64 * begin, 16 * (end - begin))], jhi, jlo)
        for a in range(begin, end):
            here = pl.ds(64 * a, 64)
            center = src[here, :]
            total = fine[0, here, :] + inc[here, :]
            total = total + fine[1, here, :] * row(src, a + 1, 64)
            total = total + fine[2, here, :] * row(src, a - 1, 64)
            total = total + fine[3, here, :] * later(center)
            total = total + fine[4, here, :] * earlier(center)
            dst[here, :] = (1.0 - OMEGA) * center + fine[5, here, :] * total

    sweep(v0, v1, 3, 13)
    sweep(v1, v2, 4, 12)
    for a in range(8):
        for c in range(Z):
            piece = v2[pl.ds(64 * (a + 4) + 16 + c, 8, stride=Z), :]
            out_ref[a, :, c * LANES : (c + 1) * LANES] = piece


def call(kernel, args, outs, scratch=(), flops=0, places=(), out_places=(), limit=24):
    outs = [x if isinstance(x, jax.ShapeDtypeStruct) else jax.ShapeDtypeStruct(x, F32) for x in outs]
    moved = sum(x.size * x.dtype.itemsize for x in (*args, *outs))

    def specs(kinds, count):
        kinds = list(kinds) + [pltpu.VMEM] * (count - len(kinds))
        return [pl.BlockSpec(memory_space=kind) for kind in kinds]

    return pl.pallas_call(
        kernel,
        out_shape=outs,
        in_specs=specs(places, len(args)),
        out_specs=specs(out_places, len(outs)),
        scratch_shapes=[pltpu.VMEM(s, F32) if isinstance(s, tuple) else s for s in scratch],
        compiler_params=pltpu.CompilerParams(vmem_limit_bytes=limit * 2**20),
        cost_estimate=pl.CostEstimate(flops=flops, bytes_accessed=moved, transcendentals=0),
    )(*args)


def neighbours(lo, hi, axis):
    count = lax.axis_size(axis)
    below = lax.ppermute(hi, axis, [(i, i + 1) for i in range(count - 1)])
    above = lax.ppermute(lo, axis, [(i + 1, i) for i in range(count - 1)])
    return below, above


def body(right_side, value_guess, speed_liq, speed_ill, flag_liq, flag_ill, jump_rates):
    nz = jump_rates.shape[0]
    dot_flops = 2 * 3 * nz * nz
    inputs = (right_side, value_guess, speed_liq, speed_ill, flag_liq, flag_ill)
    half = (6, 8, 16, LANES)
    lo, hi, low = call(
        pack_kernel,
        inputs,
        [half, half, (64, LANES)],
        [pltpu.VMEM(x.shape, x.dtype) for x in inputs]
        + [(64, LANES), pltpu.SemaphoreType.DMA((6,))],
        places=[pltpu.HBM] * 6,
    )
    coefs = lax.all_gather(low, "liq", axis=0, tiled=True)
    rates = jax.ShapeDtypeStruct((nz, nz), BF16)
    jhi, jlo, out = call(rates_kernel, (jump_rates,), [rates, rates, (TILE, LANES)])
    below, above = neighbours(lo, hi, "ill")
    wide = (6, 4, 64, LANES)
    first, second = call(widen_kernel, (lo, hi, below, above), [wide, wide])
    below, above = neighbours(first, second, "liq")
    whole, six = (1024, LANES), (6, 1024, LANES)
    fine, value, rlo, rhi, mid = call(
        fine_kernel,
        (below, first, second, above, jhi, jlo, out),
        [six, whole, (32, LANES), (32, LANES), (5, 256, LANES)],
        [six, whole, whole, whole, whole, pltpu.SemaphoreType.DMA((2,))],
        flops=dot_flops * 550,
        out_places=[pltpu.HBM] * 2,
    )
    below, above = neighbours(rlo, rhi, "ill")
    first, second = call(widen_mid_kernel, (rlo, rhi, below, above), [(64, LANES)] * 2)
    below, above = neighbours(first, second, "liq")
    rhs_low, error_mid, rhs_mid = call(
        mid_kernel,
        (below, first, second, above, mid, jhi, jlo, out),
        [(16, LANES), (64, LANES), (256, LANES)],
        [(256, LANES)] * 3,
        flops=dot_flops * 80,
    )
    err_lo, err_hi = neighbours(error_mid, error_mid, "liq")
    rhs = lax.all_gather(rhs_low, "liq", axis=0, tiled=True)
    lines = rhs.shape[0]
    line, message = (lines, LANES), (lines // 2, LANES)
    fac, middle = call(factor_kernel, (coefs, out), [(5, *line), (TILE, LANES)])
    e, lo, hi, err = call(
        first_solve_kernel,
        (rhs, fac, middle, error_mid, err_lo, err_hi),
        [line, message, message, (192, LANES)],
        [line],
    )
    for step in range(SWEEPS - 1):
        below, above = neighbours(lo, hi, "ill")
        (target,) = call(
            local_target_kernel, (e, rhs, fac, jhi, jlo), [line], flops=dot_flops * lines // Z
        )
        if step < SWEEPS - 2:
            e, lo, hi = call(
                sweep_kernel, (target, fac, middle, below, above), [line, message, message], [line]
            )
    place = lax.axis_index("liq").astype(jnp.int32).reshape(1)
    (total,) = call(
        last_sweep_kernel,
        (place, target, fac, middle, below, above, err),
        [(192, LANES)],
        [line, (lines + 4 * TILE, LANES)],
        places=[pltpu.SMEM],
    )
    below, above = neighbours(total, total, "ill")
    (result,) = call(
        last_kernel,
        (total, below, above, mid, rhs_mid, fine, value, jhi, jlo),
        [right_side.shape],
        [(576, LANES), (256, LANES), (256, LANES), whole, whole, whole, whole],
        flops=dot_flops * 400,
    )
    return result


def solution(mesh):
    block = P("liq", "ill", None)
    return jax.shard_map(
        body, mesh=mesh, in_specs=(block,) * 6 + (P(),), out_specs=block, check_vma=False
    )
```

```python
import functools

import jax
import jax.numpy as jnp
from jax import lax
from jax.experimental import pallas as pl
from jax.experimental.pallas import tpu as pltpu
from jax.sharding import PartitionSpec as P

SWEEPS = 4
OMEGA = 0.8
DISCOUNT = 0.05
LANES = 128
F32 = jnp.float32
BF16 = jnp.bfloat16

Z = 4
TILE = 8


def first_half(shape):
    return lax.broadcasted_iota(jnp.int32, shape, len(shape) - 2) % TILE < Z


def swapped(x):
    return pltpu.roll(x.reshape(-1, TILE, LANES), Z, 1).reshape(x.shape)


def later(x):
    return pltpu.roll(x, x.shape[0] - Z, 0)


def earlier(x):
    return pltpu.roll(x, Z, 0)


def pair_sums(x):
    total = x + swapped(x)
    total = total.reshape(-1, 2, TILE, LANES)
    first, second = total[:, 0], total[:, 1]
    return jnp.where(first_half(first.shape), first, second).reshape(-1, LANES)


def doubled(x):
    other = swapped(x).reshape(-1, 1, TILE, LANES)
    x = x.reshape(-1, 1, TILE, LANES)
    mask = first_half(x.shape)
    pair = jnp.concatenate([jnp.where(mask, x, other), jnp.where(mask, other, x)], axis=1)
    return pair.reshape(-1, LANES)


def spread(outflow, rows):
    return jnp.concatenate([outflow] * (rows // TILE), axis=0)


def row(ref, a, width):
    return ref[pl.ds(a * width, width), :]


def product(wide, jhi_ref, jlo_ref):
    high = wide.astype(BF16)
    rest = (wide - high.astype(F32)).astype(BF16)
    dot = functools.partial(jnp.dot, preferred_element_type=F32)
    return dot(high, jhi_ref[...]) + (dot(high, jlo_ref[...]) + dot(rest, jhi_ref[...]))


def income(src, dst, pieces, jhi_ref, jlo_ref):
    wide = jnp.concatenate(
        [
            jnp.concatenate([src[pl.ds(s + c, n, stride=Z), :] for s, _, n in pieces], axis=0)
            for c in range(Z)
        ],
        axis=1,
    )
    result = product(wide, jhi_ref, jlo_ref)
    at = 0
    for _, d, n in pieces:
        for c in range(Z):
            dst[pl.ds(d + c, n, stride=Z), :] = result[at : at + n, c * LANES : (c + 1) * LANES]
        at += n


def rates_kernel(j_ref, own, jhi_ref, jlo_ref, out_ref, own_ref):
    own_ref[...] = own[...]
    rates = j_ref[...]
    high = rates.astype(BF16)
    jhi_ref[...] = high
    jlo_ref[...] = (rates - high.astype(F32)).astype(BF16)
    total = jnp.sum(rates, axis=0, keepdims=True)
    for c in range(Z):
        piece = total[:, c * LANES : (c + 1) * LANES]
        out_ref[c : c + 1, :] = piece
        out_ref[c + Z : c + Z + 1, :] = piece


def pack_kernel(*refs):
    sources, (own_ref, lo_ref, hi_ref, low_ref), buffers = refs[:6], refs[6:10], refs[10:16]
    sems = refs[16]
    copies = [
        pltpu.make_async_copy(src, dst, sems.at[i])
        for i, (src, dst) in enumerate(zip(sources, buffers))
    ]
    for copy in copies:
        copy.start()
    rhs, value, speed_a, speed_b, flag_a, flag_b = buffers

    def put(start, x):
        for c in range(Z):
            own_ref[pl.ds(start + c, 8, stride=Z), :] = x[:, c * LANES : (c + 1) * LANES]

    for copy in copies:
        copy.wait()
    for a in range(8):
        put(32 * a, value[a])
        put(256 + 32 * a, rhs[a])
        for k, speed, flag in ((2, speed_a, flag_a), (4, speed_b, flag_b)):
            up = flag[a].astype(F32)
            put(256 * k + 32 * a, speed[a] * up)
            put(256 * (k + 1) + 32 * a, speed[a] * (1.0 - up))
    for k in range(4):
        for m in range(4):
            at = 256 * (k + 2) + 64 * m
            mid = 0.125 * pair_sums(own_ref[pl.ds(at, 32), :] + own_ref[pl.ds(at + 32, 32), :])
            own_ref[pl.ds(1536 + 64 * k + 16 * m, 16), :] = mid
            lo_ref[pl.ds(448 + 32 * k + 8 * m, 8), :] = mid[:8]
            hi_ref[pl.ds(448 + 32 * k + 8 * m, 8), :] = mid[8:]
    for a in range(8):
        lo_ref[pl.ds(16 * a, 16), :] = own_ref[pl.ds(32 * a, 16), :]
        hi_ref[pl.ds(16 * a, 16), :] = own_ref[pl.ds(32 * a + 16, 16), :]
        for k in range(5):
            at = 256 * (k + 1) + 32 * a
            lo_ref[pl.ds(128 + 64 * k + 8 * a, 8), :] = own_ref[pl.ds(at, 8), :]
            hi_ref[pl.ds(128 + 64 * k + 8 * a, 8), :] = own_ref[pl.ds(at + 24, 8), :]
    for k in range(4):
        for m in range(2):
            at = 1536 + 64 * k + 32 * m
            both = own_ref[pl.ds(at, 16), :] + own_ref[pl.ds(at + 16, 16), :]
            low_ref[pl.ds(16 * k + 8 * m, 8), :] = 0.125 * pair_sums(both)


def widen_kernel(own, below, above, wide_ref, up_ref, down_ref):
    def put(begin, piece, up, down):
        wide_ref[pl.ds(begin, piece.shape[0]), :] = piece
        if up is not None:
            up_ref[pl.ds(up, piece.shape[0]), :] = piece
        if down is not None:
            down_ref[pl.ds(down, piece.shape[0]), :] = piece

    def joined(at, width, other, part):
        ends = [src[pl.ds(other, part), :] for src in (below, above)]
        return jnp.concatenate([ends[0], own[pl.ds(at, width), :], ends[1]], axis=0)

    for a in range(8):
        piece = joined(32 * a, 32, 16 * a, 16)
        put(64 * a, piece, 64 * (a - 1) if a > 0 else None, 64 * a if a < 7 else None)
        for k in range(5):
            piece = joined(256 * (k + 1) + 32 * a, 32, 128 + 64 * k + 8 * a, 8)
            at = 448 + 288 * k
            up = at + 48 * (a - 2) if a > 1 else None
            put(512 + 384 * k + 48 * a, piece, up, at + 48 * a if a < 6 else None)
    for m in range(4):
        for k in range(4):
            piece = joined(1536 + 64 * k + 16 * m, 16, 448 + 32 * k + 8 * m, 8)
            at = 1888 + 64 * k
            up = at + 32 * (m - 2) if m > 1 else None
            put(2432 + 128 * k + 32 * m, piece, up, at + 32 * m if m < 2 else None)


def fine_kernel(
    below, own, above, jhi, jlo, out,
    keep_ref, val_ref, rhs_ref, lo_ref, hi_ref, mid_ref, v0, v1, v2, inc, f,
):
    v0[0:448, :] = below[0:448, :]
    v0[448:960, :] = own[0:512, :]
    v0[960:1408, :] = above[0:448, :]
    outflow = spread(out[...], 48)
    for a in range(20):
        here = pl.ds(48 * a, 48)
        total = DISCOUNT + outflow
        for k in range(5):
            if a < 6:
                x = below[pl.ds(448 + 288 * k + 48 * a, 48), :]
            elif a < 14:
                x = own[pl.ds(512 + 384 * k + 48 * (a - 6), 48), :]
            else:
                x = above[pl.ds(448 + 288 * k + 48 * (a - 14), 48), :]
            f[k, here, :] = x
            if k:
                total = total + x
        f[5, here, :] = OMEGA / total

    def rest(a):
        here = pl.ds(48 * a, 48)
        return f[0, here, :], f[1, here, :], f[2, here, :], f[3, here, :], f[4, here, :]

    income(v0, inc, [(64, 64, 16 * 20)], jhi, jlo)
    for a in range(20):
        rhs, fa, ba, fb, bb = rest(a)
        center = row(v0, a + 1, 64)
        total = rhs + inc[pl.ds(64 * (a + 1) + 8, 48), :]
        total = total + fa * v0[pl.ds(64 * (a + 2) + 8, 48), :]
        total = total + ba * v0[pl.ds(64 * a + 8, 48), :]
        total = total + fb * later(center)[8:56] + bb * earlier(center)[8:56]
        here = pl.ds(48 * a, 48)
        v1[here, :] = (1.0 - OMEGA) * center[8:56] + f[5, here, :] * total

    def applied(src, a):
        rhs, fa, ba, fb, bb = rest(a)
        center = row(src, a, 48)
        total = rhs + row(inc, a, 48) + fa * row(src, a + 1, 48) + ba * row(src, a - 1, 48)
        return center, total + fb * later(center) + bb * earlier(center)

    income(v1, inc, [(48, 48, 12 * 18)], jhi, jlo)
    for a in range(1, 19):
        center, total = applied(v1, a)
        here = pl.ds(48 * a, 48)
        v2[here, :] = (1.0 - OMEGA) * center + f[5, here, :] * total
    income(v2, inc, [(96, 96, 12 * 16)], jhi, jlo)

    def residual(a):
        center, total = applied(v2, a)
        diag = DISCOUNT + outflow
        for x in rest(a)[1:]:
            diag = diag + x
        return (total - diag * center)[8:40]

    for m in range(8):
        coarse = 0.25 * pair_sums(residual(2 + 2 * m) + residual(3 + 2 * m))
        rhs_ref[pl.ds(16 * m, 16), :] = coarse
        lo_ref[pl.ds(8 * m, 8), :] = coarse[:8]
        hi_ref[pl.ds(8 * m, 8), :] = coarse[8:]
    for a in range(12):
        value = row(v2, a + 4, 48)[8:40]
        val_ref[pl.ds(32 * a, 32), :] = value
        lo_ref[pl.ds(64 + 8 * a, 8), :] = value[:8]
        hi_ref[pl.ds(64 + 8 * a, 8), :] = value[24:]
    for k in range(6):
        keep_ref[k] = f[k, pl.ds(48 * 4, 48 * 12), :]

    outflow = spread(out[...], 32)
    for m in range(8):
        here = pl.ds(32 * m, 32)
        total = DISCOUNT + outflow
        for k in range(4):
            if m < 2:
                x = below[pl.ds(1888 + 64 * k + 32 * m, 32), :]
            elif m < 6:
                x = own[pl.ds(2432 + 128 * k + 32 * (m - 2), 32), :]
            else:
                x = above[pl.ds(1888 + 64 * k + 32 * (m - 6), 32), :]
            mid_ref[k, here, :] = x
            total = total + x
        mid_ref[4, here, :] = OMEGA / total


def mid_kernel(
    own, val, below, above, mid, jhi, jlo, out, pay_ref, err_ref, rhs_ref, wide_ref, e0, e1, inc
):
    for a in range(8):
        for i, piece in enumerate((below[pl.ds(8 * a, 8), :], row(own, a, 16), above[pl.ds(8 * a, 8), :])):
            rhs_ref[pl.ds(32 * a + (0, 8, 24)[i], piece.shape[0]), :] = piece
    for a in range(12):
        ends = [src[pl.ds(64 + 8 * a, 8), :] for src in (below, above)]
        wide_ref[pl.ds(48 * a, 8), :] = ends[0]
        wide_ref[pl.ds(48 * a + 8, 32), :] = row(val, a, 32)
        wide_ref[pl.ds(48 * a + 40, 8), :] = ends[1]
    e0[...] = mid[4] * rhs_ref[...]

    def applied(src, a):
        here = pl.ds(32 * a, 32)
        center = src[here, :]
        total = rhs_ref[here, :] + inc[here, :]
        total = total + mid[0, here, :] * row(src, a + 1, 32)
        total = total + mid[1, here, :] * row(src, a - 1, 32)
        total = total + mid[2, here, :] * later(center)
        total = total + mid[3, here, :] * earlier(center)
        return center, total

    income(e0, inc, [(32, 32, 8 * 6)], jhi, jlo)
    for a in range(1, 7):
        center, total = applied(e0, a)
        here = pl.ds(32 * a, 32)
        e1[here, :] = (1.0 - OMEGA) * center + mid[4, here, :] * total
    income(e1, inc, [(64, 64, 8 * 4)], jhi, jlo)
    outflow = spread(out[...], 32)

    def residual(a):
        center, total = applied(e1, a)
        here = pl.ds(32 * a, 32)
        diag = DISCOUNT + outflow
        for k in range(4):
            diag = diag + mid[k, here, :]
        return (total - diag * center)[8:24]

    for m in range(2):
        pay_ref[pl.ds(8 * m, 8), :] = 0.25 * pair_sums(residual(2 + 2 * m) + residual(3 + 2 * m))
    for a in range(4):
        err_ref[pl.ds(16 * a, 16), :] = e1[pl.ds(32 * (a + 2) + 8, 16), :]


def solve_lines(target, weight, carry, link, middle, y, x_ref, offset):
    count = y.shape[0] // TILE
    half = count // 2
    top = bottom = None
    for i in range(half):
        j = count - 1 - i
        t = weight(i) * target(i)
        u = weight(j) * target(j)
        top = t if i == 0 else t + carry(i) * top
        bottom = u if i == 0 else u + carry(j) * bottom
        if i < half - 1:
            y[pl.ds(TILE * i, TILE), :] = top
            y[pl.ds(TILE * j, TILE), :] = bottom
    head = (top + link(half - 1) * bottom) * middle
    tail = bottom + link(half) * head
    for i in range(half - 1, -1, -1):
        j = count - 1 - i
        if i < half - 1:
            head = row(y, i, TILE) + link(i) * head
            tail = row(y, j, TILE) + link(j) * tail
        x_ref[pl.ds(offset + TILE * i, TILE), :] = head
        x_ref[pl.ds(offset + TILE * j, TILE), :] = tail


def send_lines(e, lo_ref, hi_ref):
    pairs = e[...].reshape(-1, 2, TILE, LANES)
    first, second = pairs[:, 0], pairs[:, 1]
    mask = first_half(first.shape)
    lo_ref[...] = jnp.where(mask, first, pltpu.roll(second, Z, 1)).reshape(-1, LANES)
    hi_ref[...] = jnp.where(mask, pltpu.roll(first, Z, 1), second).reshape(-1, LANES)


def factor_kernel(gathered, out, fac_ref, middle_ref):
    count = fac_ref.shape[1] // TILE

    def part(k, a):
        return gathered[pl.ds(64 * (a // 2) + 16 * k + 8 * (a % 2), TILE), :]

    outflow = DISCOUNT + out[...]
    gaps = [None, None]
    links = [None, None]
    for i in range(count // 2):
        for side, a in ((0, i), (1, count - 1 - i)):
            here = pl.ds(TILE * a, TILE)
            inner, outer = (part(0, a), part(1, a)) if side == 0 else (part(1, a), part(0, a))
            fb, bb = part(2, a), part(3, a)
            slack = outflow + fb + bb
            slack = slack + (outer if i == 0 else outer * gaps[side])
            weight = 1.0 / (slack + inner)
            links[side] = inner * weight
            gaps[side] = slack * weight
            fac_ref[0, here, :] = fb
            fac_ref[1, here, :] = bb
            fac_ref[2, here, :] = weight
            fac_ref[3, here, :] = outer * weight
            fac_ref[4, here, :] = links[side]
    middle_ref[...] = 1.0 / (gaps[0] + links[0] * gaps[1])


def first_solve_kernel(
    rhs, fac, middle, err, err_lo, err_hi, e_ref, lo_ref, hi_ref, wide_ref, y
):
    for i, src in enumerate((err_lo, err, err_hi)):
        wide_ref[pl.ds(64 * i, 64), :] = src[...]
    solve_lines(
        lambda a: row(rhs, a, TILE),
        lambda a: row(fac.at[2], a, TILE),
        lambda a: row(fac.at[3], a, TILE),
        lambda a: row(fac.at[4], a, TILE),
        middle[...], y, e_ref, 0,
    )
    send_lines(e_ref, lo_ref, hi_ref)


def local_target_kernel(e, rhs, fac, jhi, jlo, t_ref):
    income(e, t_ref, [(0, 0, e.shape[0] // Z)], jhi, jlo)
    other = swapped(e[...])
    mask = first_half(other.shape)
    t_ref[...] = t_ref[...] + rhs[...] + jnp.where(mask, fac[0], fac[1]) * other


def swept(t, fac, middle, below, above, y, x_ref, offset):
    mask = first_half((TILE, LANES))

    def target(a):
        low_side, high_side = row(below, a // 2, TILE), row(above, a // 2, TILE)
        if a % 2:
            low_side = pltpu.roll(low_side, Z, 0)
        else:
            high_side = pltpu.roll(high_side, Z, 0)
        near = jnp.where(mask, low_side, high_side)
        coupling = jnp.where(mask, row(fac.at[1], a, TILE), row(fac.at[0], a, TILE))
        return row(t, a, TILE) + coupling * near

    solve_lines(
        target,
        lambda a: row(fac.at[2], a, TILE),
        lambda a: row(fac.at[3], a, TILE),
        lambda a: row(fac.at[4], a, TILE),
        middle[...], y, x_ref, offset,
    )


def sweep_kernel(t, fac, middle, below, above, e_ref, lo_ref, hi_ref, y):
    swept(t, fac, middle, below, above, y, e_ref, 0)
    send_lines(e_ref, lo_ref, hi_ref)


def last_sweep_kernel(place, t, fac, middle, below, above, err, sum_ref, y, x):
    edge = 2 * TILE
    x[0:edge, :] = jnp.zeros((edge, LANES), F32)
    x[pl.ds(x.shape[0] - edge, edge), :] = jnp.zeros((edge, LANES), F32)
    swept(t, fac, middle, below, above, y, x, edge)
    start = place[0] * 2 * TILE
    for i in range(6):
        low = x[pl.ds(pl.multiple_of(start + i * TILE, TILE), TILE), :]
        fill = doubled(low)
        for m in (2 * i, 2 * i + 1):
            sum_ref[pl.ds(16 * m, 16), :] = err[pl.ds(16 * m, 16), :] + fill


def last_kernel(
    own, below, above, mid, rhs_mid, fine, val, jhi, jlo, out_ref, ev, e1, e2, v0, v1, v2, inc
):
    for a in range(12):
        for i, src in enumerate((below, own, above)):
            ev[pl.ds(48 * a + 16 * i, 16), :] = src[pl.ds(16 * a, 16), :]

    income(ev, inc, [(48 * (a + 2) + 8, 32 * a, 8) for a in range(8)], jhi, jlo)
    for a in range(8):
        here = pl.ds(32 * a, 32)
        center = row(ev, a + 2, 48)
        total = rhs_mid[here, :] + inc[here, :]
        total = total + mid[0, here, :] * ev[pl.ds(48 * (a + 3) + 8, 32), :]
        total = total + mid[1, here, :] * ev[pl.ds(48 * (a + 1) + 8, 32), :]
        total = total + mid[2, here, :] * later(center)[8:40]
        total = total + mid[3, here, :] * earlier(center)[8:40]
        e1[here, :] = (1.0 - OMEGA) * center[8:40] + mid[4, here, :] * total

    income(e1, inc, [(32, 32, 8 * 6)], jhi, jlo)
    for a in range(1, 7):
        here = pl.ds(32 * a, 32)
        center = e1[here, :]
        total = rhs_mid[here, :] + inc[here, :]
        total = total + mid[0, here, :] * row(e1, a + 1, 32)
        total = total + mid[1, here, :] * row(e1, a - 1, 32)
        total = total + mid[2, here, :] * later(center)
        total = total + mid[3, here, :] * earlier(center)
        error = (1.0 - OMEGA) * center + mid[4, here, :] * total
        fill = doubled(error)[8:56]
        for f in (2 * a - 2, 2 * a - 1):
            v0[pl.ds(48 * f, 48), :] = row(val, f, 48) + fill

    def sweep(src, dst, begin, end):
        income(src, inc, [(48 * begin, 48 * begin, 12 * (end - begin))], jhi, jlo)
        for a in range(begin, end):
            here = pl.ds(48 * a, 48)
            center = src[here, :]
            total = fine[0, here, :] + inc[here, :]
            total = total + fine[1, here, :] * row(src, a + 1, 48)
            total = total + fine[2, here, :] * row(src, a - 1, 48)
            total = total + fine[3, here, :] * later(center)
            total = total + fine[4, here, :] * earlier(center)
            dst[here, :] = (1.0 - OMEGA) * center + fine[5, here, :] * total

    sweep(v0, v1, 1, 11)
    sweep(v1, v2, 2, 10)
    for a in range(8):
        for c in range(Z):
            piece = v2[pl.ds(48 * (a + 2) + 8 + c, 8, stride=Z), :]
            out_ref[a, :, c * LANES : (c + 1) * LANES] = piece


def call(kernel, args, outs, scratch=(), flops=0, places=(), limit=24):
    outs = [x if isinstance(x, jax.ShapeDtypeStruct) else jax.ShapeDtypeStruct(x, F32) for x in outs]
    moved = sum(x.size * x.dtype.itemsize for x in (*args, *outs))
    kinds = list(places) + [pltpu.VMEM] * (len(args) - len(places))
    return pl.pallas_call(
        kernel,
        out_shape=outs,
        in_specs=[pl.BlockSpec(memory_space=kind) for kind in kinds],
        out_specs=[pl.BlockSpec(memory_space=pltpu.VMEM)] * len(outs),
        scratch_shapes=[pltpu.VMEM(s, F32) if isinstance(s, tuple) else s for s in scratch],
        compiler_params=pltpu.CompilerParams(vmem_limit_bytes=limit * 2**20),
        cost_estimate=pl.CostEstimate(flops=flops, bytes_accessed=moved, transcendentals=0),
    )(*args)


def neighbours(lo, hi, axis):
    count = lax.axis_size(axis)
    below = lax.ppermute(hi, axis, [(i, i + 1) for i in range(count - 1)])
    above = lax.ppermute(lo, axis, [(i + 1, i) for i in range(count - 1)])
    return below, above


def body(right_side, value_guess, speed_liq, speed_ill, flag_liq, flag_ill, jump_rates):
    nz = jump_rates.shape[0]
    dot_flops = 2 * 3 * nz * nz
    inputs = (right_side, value_guess, speed_liq, speed_ill, flag_liq, flag_ill)
    own, lo, hi, low = call(
        pack_kernel,
        inputs,
        [(1792, LANES), (576, LANES), (576, LANES), (64, LANES)],
        [pltpu.VMEM(x.shape, x.dtype) for x in inputs] + [pltpu.SemaphoreType.DMA((6,))],
        places=[pltpu.HBM] * 6,
        limit=57,
    )
    below, above = neighbours(lo, hi, "ill")
    coefs = lax.all_gather(low, "liq", axis=0, tiled=True)
    rates = jax.ShapeDtypeStruct((nz, nz), BF16)
    jhi, jlo, out, own = call(
        rates_kernel, (jump_rates, own), [rates, rates, (TILE, LANES), own.shape]
    )
    wide, up, down = call(
        widen_kernel, (own, below, above), [(2944, LANES), (2144, LANES), (2144, LANES)]
    )
    below, above = neighbours(down, up, "liq")
    fine, value, rhs_mid, lo, hi, mid = call(
        fine_kernel,
        (below, wide, above, jhi, jlo, out),
        [(6, 576, LANES), (384, LANES), (128, LANES), (160, LANES), (160, LANES), (5, 256, LANES)],
        [(1408, LANES), (960, LANES), (960, LANES), (1408, LANES), (6, 960, LANES)],
        flops=dot_flops * 730,
    )
    below, above = neighbours(lo, hi, "ill")
    rhs_low, error_mid, rhs_mid, value = call(
        mid_kernel,
        (rhs_mid, value, below, above, mid, jhi, jlo, out),
        [(16, LANES), (64, LANES), (256, LANES), (576, LANES)],
        [(256, LANES)] * 3,
        flops=dot_flops * 80,
    )
    err_lo, err_hi = neighbours(error_mid, error_mid, "liq")
    rhs = lax.all_gather(rhs_low, "liq", axis=0, tiled=True)
    lines = rhs.shape[0]
    line, message = (lines, LANES), (lines // 2, LANES)
    fac, middle = call(factor_kernel, (coefs, out), [(5, *line), (TILE, LANES)])
    e, lo, hi, err = call(
        first_solve_kernel,
        (rhs, fac, middle, error_mid, err_lo, err_hi),
        [line, message, message, (192, LANES)],
        [line],
    )
    for step in range(SWEEPS - 1):
        below, above = neighbours(lo, hi, "ill")
        (target,) = call(
            local_target_kernel,
            (e, rhs, fac, jhi, jlo),
            [line],
            flops=dot_flops * lines // Z,
        )
        if step < SWEEPS - 2:
            e, lo, hi = call(
                sweep_kernel, (target, fac, middle, below, above), [line, message, message], [line]
            )
    place = lax.axis_index("liq").astype(jnp.int32).reshape(1)
    (total,) = call(
        last_sweep_kernel,
        (place, target, fac, middle, below, above, err),
        [(192, LANES)],
        [line, (lines + 4 * TILE, LANES)],
        places=[pltpu.SMEM],
    )
    below, above = neighbours(total, total, "ill")
    (result,) = call(
        last_kernel,
        (total, below, above, mid, rhs_mid, fine, value, jhi, jlo),
        [right_side.shape],
        [(576, LANES), (256, LANES), (256, LANES)] + [(576, LANES)] * 4,
        flops=dot_flops * 330,
    )
    return result


def solution(mesh):
    block = P("liq", "ill", None)
    return jax.shard_map(
        body, mesh=mesh, in_specs=(block,) * 6 + (P(),), out_specs=block, check_vma=False
    )
```

```python
import functools

import jax
import jax.numpy as jnp
from jax import lax
from jax.experimental import pallas as pl
from jax.experimental.pallas import tpu as pltpu
from jax.sharding import PartitionSpec as P

SWEEPS = 4
OMEGA = 0.8
DISCOUNT = 0.05
LANES = 128
F32 = jnp.float32
BF16 = jnp.bfloat16

Z = 4
TILE = 8


def first_half(shape):
    return lax.broadcasted_iota(jnp.int32, shape, len(shape) - 2) % TILE < Z


def swapped(x):
    return pltpu.roll(x.reshape(-1, TILE, LANES), Z, 1).reshape(x.shape)


def later(x):
    return pltpu.roll(x, x.shape[0] - Z, 0)


def earlier(x):
    return pltpu.roll(x, Z, 0)


def pair_sums(x):
    total = x + swapped(x)
    total = total.reshape(-1, 2, TILE, LANES)
    first, second = total[:, 0], total[:, 1]
    return jnp.where(first_half(first.shape), first, second).reshape(-1, LANES)


def doubled(x):
    other = swapped(x).reshape(-1, 1, TILE, LANES)
    x = x.reshape(-1, 1, TILE, LANES)
    mask = first_half(x.shape)
    pair = jnp.concatenate([jnp.where(mask, x, other), jnp.where(mask, other, x)], axis=1)
    return pair.reshape(-1, LANES)


def spread(outflow, rows):
    return jnp.concatenate([outflow] * (rows // TILE), axis=0)


def row(ref, a, width):
    return ref[pl.ds(a * width, width), :]


def product(wide, jhi_ref, jlo_ref):
    high = wide.astype(BF16)
    rest = (wide - high.astype(F32)).astype(BF16)
    dot = functools.partial(jnp.dot, preferred_element_type=F32)
    return dot(high, jhi_ref[...]) + (dot(high, jlo_ref[...]) + dot(rest, jhi_ref[...]))


def income(src, dst, pieces, jhi_ref, jlo_ref):
    wide = jnp.concatenate(
        [
            jnp.concatenate([src[pl.ds(s + c, n, stride=Z), :] for s, _, n in pieces], axis=0)
            for c in range(Z)
        ],
        axis=1,
    )
    result = product(wide, jhi_ref, jlo_ref)
    at = 0
    for _, d, n in pieces:
        for c in range(Z):
            dst[pl.ds(d + c, n, stride=Z), :] = result[at : at + n, c * LANES : (c + 1) * LANES]
        at += n


def rates_kernel(j_ref, own, jhi_ref, jlo_ref, out_ref, own_ref):
    own_ref[...] = own[...]
    rates = j_ref[...]
    high = rates.astype(BF16)
    jhi_ref[...] = high
    jlo_ref[...] = (rates - high.astype(F32)).astype(BF16)
    total = jnp.sum(rates, axis=0, keepdims=True)
    for c in range(Z):
        piece = total[:, c * LANES : (c + 1) * LANES]
        out_ref[c : c + 1, :] = piece
        out_ref[c + Z : c + Z + 1, :] = piece


def pack_kernel(*refs):
    sources, outs, buffers, sems = refs[:6], refs[6:12], refs[12:18], refs[18]
    own_ref, lo_ref, hi_ref, up_ref, down_ref, low_ref = outs
    copies = [
        pltpu.make_async_copy(src, dst, sems.at[i])
        for i, (src, dst) in enumerate(zip(sources, buffers))
    ]
    for copy in copies:
        copy.start()
    rhs, value, speed_a, speed_b, flag_a, flag_b = buffers

    def put(start, x):
        for c in range(Z):
            own_ref[pl.ds(start + c, 8, stride=Z), :] = x[:, c * LANES : (c + 1) * LANES]

    for copy in copies:
        copy.wait()
    for a in range(8):
        put(32 * a, value[a])
        put(256 + 32 * a, rhs[a])
        for k, speed, flag in ((2, speed_a, flag_a), (4, speed_b, flag_b)):
            up = flag[a].astype(F32)
            put(256 * k + 32 * a, speed[a] * up)
            put(256 * (k + 1) + 32 * a, speed[a] * (1.0 - up))
    for k in range(4):
        for m in range(4):
            at = 256 * (k + 2) + 64 * m
            mid = 0.125 * pair_sums(own_ref[pl.ds(at, 32), :] + own_ref[pl.ds(at + 32, 32), :])
            own_ref[pl.ds(1536 + 64 * k + 16 * m, 16), :] = mid
            lo_ref[pl.ds(448 + 32 * k + 8 * m, 8), :] = mid[:8]
            hi_ref[pl.ds(448 + 32 * k + 8 * m, 8), :] = mid[8:]
    for a in range(8):
        lo_ref[pl.ds(16 * a, 16), :] = own_ref[pl.ds(32 * a, 16), :]
        hi_ref[pl.ds(16 * a, 16), :] = own_ref[pl.ds(32 * a + 16, 16), :]
        for k in range(5):
            at = 256 * (k + 1) + 32 * a
            lo_ref[pl.ds(128 + 64 * k + 8 * a, 8), :] = own_ref[pl.ds(at, 8), :]
            hi_ref[pl.ds(128 + 64 * k + 8 * a, 8), :] = own_ref[pl.ds(at + 24, 8), :]
    up_ref[0:224, :] = own_ref[32:256, :]
    down_ref[0:224, :] = own_ref[0:224, :]
    for k in range(5):
        here = pl.ds(224 + 192 * k, 192)
        up_ref[here, :] = own_ref[pl.ds(256 * (k + 1) + 64, 192), :]
        down_ref[here, :] = own_ref[pl.ds(256 * (k + 1), 192), :]
    for k in range(4):
        for m in range(2):
            at = 1536 + 64 * k + 32 * m
            both = own_ref[pl.ds(at, 16), :] + own_ref[pl.ds(at + 16, 16), :]
            low_ref[pl.ds(16 * k + 8 * m, 8), :] = 0.125 * pair_sums(both)


def corner_kernel(below, above, up_ref, down_ref):
    def put(out, at, src, width):
        out[pl.ds(at, width), :] = below[pl.ds(src, width), :]
        out[pl.ds(at + width, width), :] = above[pl.ds(src, width), :]

    for out, shift in ((up_ref, 1), (down_ref, 0)):
        for i in range(6):
            put(out, 32 * i, 16 * (i + 2 * shift), 16)
        for k in range(5):
            for i in range(5):
                put(out, 192 + 80 * k + 16 * i, 128 + 64 * k + 8 * (i + 3 * shift), 8)
        for k in range(4):
            for i in range(2):
                put(out, 592 + 32 * k + 16 * i, 448 + 32 * k + 8 * (i + 2 * shift), 8)


def fine_kernel(
    own, ill_below, ill_above, below, above, far_below, far_above, jhi, jlo, out,
    keep_ref, val_ref, rhs_ref, lo_ref, hi_ref, mid_ref, v0, v1, v2, inc, f,
):
    def joined(first, middle, last):
        parts = [ref[pl.ds(at, width), :] for ref, at, width in (first, middle, last)]
        return jnp.concatenate(parts, axis=0)

    def padded(middle, width):
        edge = jnp.zeros((width, LANES), F32)
        ref, at, count = middle
        return jnp.concatenate([edge, ref[pl.ds(at, count), :], edge], axis=0)

    for a in range(22):
        if a < 7:
            i, far, middle = a - 1, far_below, (below, 32 * a, 32)
        elif a < 15:
            i, far, middle = a - 7, None, (own, 32 * (a - 7), 32)
        else:
            i, far, middle = a - 15, far_above, (above, 32 * (a - 15), 32)
        if far is None:
            x = joined((ill_below, 16 * i, 16), middle, (ill_above, 16 * i, 16))
        elif 0 <= i < 6:
            x = joined((far, 32 * i, 16), middle, (far, 32 * i + 16, 16))
        else:
            x = padded(middle, 16)
        v0[pl.ds(64 * a, 64), :] = x
    outflow = spread(out[...], 48)
    for a in range(20):
        here = pl.ds(48 * a, 48)
        total = DISCOUNT + outflow
        for k in range(5):
            if a < 6:
                i, far, middle = a - 1, far_below, (below, 224 + 192 * k + 32 * a, 32)
            elif a < 14:
                i, far, middle = a - 6, None, (own, 256 * (k + 1) + 32 * (a - 6), 32)
            else:
                i, far, middle = a - 14, far_above, (above, 224 + 192 * k + 32 * (a - 14), 32)
            if far is None:
                at = 128 + 64 * k + 8 * i
                x = joined((ill_below, at, 8), middle, (ill_above, at, 8))
            elif 0 <= i < 5:
                at = 192 + 80 * k + 16 * i
                x = joined((far, at, 8), middle, (far, at + 8, 8))
            else:
                x = padded(middle, 8)
            f[k, here, :] = x
            if k:
                total = total + x
        f[5, here, :] = OMEGA / total

    def rest(a):
        here = pl.ds(48 * a, 48)
        return f[0, here, :], f[1, here, :], f[2, here, :], f[3, here, :], f[4, here, :]

    income(v0, inc, [(64, 64, 16 * 20)], jhi, jlo)
    for a in range(20):
        rhs, fa, ba, fb, bb = rest(a)
        center = row(v0, a + 1, 64)
        total = rhs + inc[pl.ds(64 * (a + 1) + 8, 48), :]
        total = total + fa * v0[pl.ds(64 * (a + 2) + 8, 48), :]
        total = total + ba * v0[pl.ds(64 * a + 8, 48), :]
        total = total + fb * later(center)[8:56] + bb * earlier(center)[8:56]
        here = pl.ds(48 * a, 48)
        v1[here, :] = (1.0 - OMEGA) * center[8:56] + f[5, here, :] * total

    def applied(src, a):
        rhs, fa, ba, fb, bb = rest(a)
        center = row(src, a, 48)
        total = rhs + row(inc, a, 48) + fa * row(src, a + 1, 48) + ba * row(src, a - 1, 48)
        return center, total + fb * later(center) + bb * earlier(center)

    income(v1, inc, [(48, 48, 12 * 18)], jhi, jlo)
    for a in range(1, 19):
        center, total = applied(v1, a)
        here = pl.ds(48 * a, 48)
        v2[here, :] = (1.0 - OMEGA) * center + f[5, here, :] * total
    income(v2, inc, [(96, 96, 12 * 16)], jhi, jlo)

    def residual(a):
        center, total = applied(v2, a)
        diag = DISCOUNT + outflow
        for x in rest(a)[1:]:
            diag = diag + x
        return (total - diag * center)[8:40]

    for m in range(8):
        coarse = 0.25 * pair_sums(residual(2 + 2 * m) + residual(3 + 2 * m))
        rhs_ref[pl.ds(16 * m, 16), :] = coarse
        lo_ref[pl.ds(8 * m, 8), :] = coarse[:8]
        hi_ref[pl.ds(8 * m, 8), :] = coarse[8:]
    for a in range(12):
        value = row(v2, a + 4, 48)[8:40]
        val_ref[pl.ds(32 * a, 32), :] = value
        lo_ref[pl.ds(64 + 8 * a, 8), :] = value[:8]
        hi_ref[pl.ds(64 + 8 * a, 8), :] = value[24:]
    for k in range(6):
        keep_ref[k] = f[k, pl.ds(48 * 4, 48 * 12), :]

    outflow = spread(out[...], 32)
    for m in range(8):
        here = pl.ds(32 * m, 32)
        total = DISCOUNT + outflow
        for k in range(4):
            if m < 2 or m > 5:
                far, at = (far_below, 592 + 32 * k + 16 * m) if m < 2 else (far_above, 592 + 32 * k + 16 * (m - 6))
                both = f[k + 1, pl.ds(48 * (2 + 2 * m) + 8, 32), :] + f[k + 1, pl.ds(48 * (3 + 2 * m) + 8, 32), :]
                middle = 0.125 * pair_sums(both)
                x = jnp.concatenate([far[pl.ds(at, 8), :], middle, far[pl.ds(at + 8, 8), :]], axis=0)
            else:
                at = 448 + 32 * k + 8 * (m - 2)
                x = joined((ill_below, at, 8), (own, 1536 + 64 * k + 16 * (m - 2), 16), (ill_above, at, 8))
            mid_ref[k, here, :] = x
            total = total + x
        mid_ref[4, here, :] = OMEGA / total


def mid_kernel(
    own, val, below, above, mid, jhi, jlo, out, pay_ref, err_ref, rhs_ref, wide_ref, e0, e1, inc
):
    for a in range(8):
        for i, piece in enumerate((below[pl.ds(8 * a, 8), :], row(own, a, 16), above[pl.ds(8 * a, 8), :])):
            rhs_ref[pl.ds(32 * a + (0, 8, 24)[i], piece.shape[0]), :] = piece
    for a in range(12):
        ends = [src[pl.ds(64 + 8 * a, 8), :] for src in (below, above)]
        wide_ref[pl.ds(48 * a, 8), :] = ends[0]
        wide_ref[pl.ds(48 * a + 8, 32), :] = row(val, a, 32)
        wide_ref[pl.ds(48 * a + 40, 8), :] = ends[1]
    e0[...] = mid[4] * rhs_ref[...]

    def applied(src, a):
        here = pl.ds(32 * a, 32)
        center = src[here, :]
        total = rhs_ref[here, :] + inc[here, :]
        total = total + mid[0, here, :] * row(src, a + 1, 32)
        total = total + mid[1, here, :] * row(src, a - 1, 32)
        total = total + mid[2, here, :] * later(center)
        total = total + mid[3, here, :] * earlier(center)
        return center, total

    income(e0, inc, [(32, 32, 8 * 6)], jhi, jlo)
    for a in range(1, 7):
        center, total = applied(e0, a)
        here = pl.ds(32 * a, 32)
        e1[here, :] = (1.0 - OMEGA) * center + mid[4, here, :] * total
    income(e1, inc, [(64, 64, 8 * 4)], jhi, jlo)
    outflow = spread(out[...], 32)

    def residual(a):
        center, total = applied(e1, a)
        here = pl.ds(32 * a, 32)
        diag = DISCOUNT + outflow
        for k in range(4):
            diag = diag + mid[k, here, :]
        return (total - diag * center)[8:24]

    for m in range(2):
        pay_ref[pl.ds(8 * m, 8), :] = 0.25 * pair_sums(residual(2 + 2 * m) + residual(3 + 2 * m))
    for a in range(6):
        err_ref[pl.ds(16 * a, 16), :] = e1[pl.ds(32 * (a + 1) + 8, 16), :]
    pay_ref[16:48, :] = err_ref[32:64, :]


def solve_lines(target, weight, carry, link, middle, y, x_ref, offset):
    count = y.shape[0] // TILE
    half = count // 2
    top = bottom = None
    for i in range(half):
        j = count - 1 - i
        t = weight(i) * target(i)
        u = weight(j) * target(j)
        top = t if i == 0 else t + carry(i) * top
        bottom = u if i == 0 else u + carry(j) * bottom
        if i < half - 1:
            y[pl.ds(TILE * i, TILE), :] = top
            y[pl.ds(TILE * j, TILE), :] = bottom
    head = (top + link(half - 1) * bottom) * middle
    tail = bottom + link(half) * head
    for i in range(half - 1, -1, -1):
        j = count - 1 - i
        if i < half - 1:
            head = row(y, i, TILE) + link(i) * head
            tail = row(y, j, TILE) + link(j) * tail
        x_ref[pl.ds(offset + TILE * i, TILE), :] = head
        x_ref[pl.ds(offset + TILE * j, TILE), :] = tail


def send_lines(e, lo_ref, hi_ref):
    pairs = e[...].reshape(-1, 2, TILE, LANES)
    first, second = pairs[:, 0], pairs[:, 1]
    mask = first_half(first.shape)
    lo_ref[...] = jnp.where(mask, first, pltpu.roll(second, Z, 1)).reshape(-1, LANES)
    hi_ref[...] = jnp.where(mask, pltpu.roll(first, Z, 1), second).reshape(-1, LANES)


def factor_kernel(gathered, out, fac_ref, middle_ref):
    count = fac_ref.shape[1] // TILE

    def part(k, a):
        return gathered[pl.ds(64 * (a // 2) + 16 * k + 8 * (a % 2), TILE), :]

    outflow = DISCOUNT + out[...]
    gaps = [None, None]
    links = [None, None]
    for i in range(count // 2):
        for side, a in ((0, i), (1, count - 1 - i)):
            here = pl.ds(TILE * a, TILE)
            inner, outer = (part(0, a), part(1, a)) if side == 0 else (part(1, a), part(0, a))
            fb, bb = part(2, a), part(3, a)
            slack = outflow + fb + bb
            slack = slack + (outer if i == 0 else outer * gaps[side])
            weight = 1.0 / (slack + inner)
            links[side] = inner * weight
            gaps[side] = slack * weight
            fac_ref[0, here, :] = fb
            fac_ref[1, here, :] = bb
            fac_ref[2, here, :] = weight
            fac_ref[3, here, :] = outer * weight
            fac_ref[4, here, :] = links[side]
    middle_ref[...] = 1.0 / (gaps[0] + links[0] * gaps[1])


def first_solve_kernel(gathered, fac, middle, e_ref, lo_ref, hi_ref, y):
    solve_lines(
        lambda a: gathered[pl.ds(48 * (a // 2) + 8 * (a % 2), TILE), :],
        lambda a: row(fac.at[2], a, TILE),
        lambda a: row(fac.at[3], a, TILE),
        lambda a: row(fac.at[4], a, TILE),
        middle[...], y, e_ref, 0,
    )
    send_lines(e_ref, lo_ref, hi_ref)


def local_target(e, rhs, fac, jhi, jlo, t_ref):
    income(e, t_ref, [(0, 0, e.shape[0] // Z)], jhi, jlo)
    other = swapped(e[...])
    mask = first_half(other.shape)
    t_ref[...] = t_ref[...] + rhs[...] + jnp.where(mask, fac[0], fac[1]) * other


def first_target_kernel(place, gathered, err, e, fac, jhi, jlo, t_ref, rhs_ref, wide_ref):
    blocks = e.shape[0] // (2 * TILE)
    for i in range(blocks):
        rhs_ref[pl.ds(16 * i, 16), :] = gathered[pl.ds(48 * i, 16), :]
    local_target(e, rhs_ref, fac, jhi, jlo, t_ref)
    here = place[0]
    wide_ref[32:128, :] = err[...]
    for at, block, inside in ((0, here - 1, here > 0), (128, here + 1, here < blocks - 1)):
        block = jnp.minimum(jnp.maximum(block, 0), blocks - 1)
        start = pl.multiple_of(block * 48 + 16, 16)
        piece = gathered[pl.ds(start, 32), :]
        wide_ref[pl.ds(at, 32), :] = jnp.where(inside, piece, jnp.zeros_like(piece))


def swept(t, fac, middle, below, above, y, x_ref, offset):
    mask = first_half((TILE, LANES))

    def target(a):
        low_side, high_side = row(below, a // 2, TILE), row(above, a // 2, TILE)
        if a % 2:
            low_side = pltpu.roll(low_side, Z, 0)
        else:
            high_side = pltpu.roll(high_side, Z, 0)
        near = jnp.where(mask, low_side, high_side)
        coupling = jnp.where(mask, row(fac.at[1], a, TILE), row(fac.at[0], a, TILE))
        return row(t, a, TILE) + coupling * near

    solve_lines(
        target,
        lambda a: row(fac.at[2], a, TILE),
        lambda a: row(fac.at[3], a, TILE),
        lambda a: row(fac.at[4], a, TILE),
        middle[...], y, x_ref, offset,
    )


def sweep_kernel(t, fac, middle, below, above, e_ref, lo_ref, hi_ref, y):
    swept(t, fac, middle, below, above, y, e_ref, 0)
    send_lines(e_ref, lo_ref, hi_ref)


def last_sweep_kernel(place, t, fac, middle, below, above, err, sum_ref, y, x):
    edge = 2 * TILE
    x[0:edge, :] = jnp.zeros((edge, LANES), F32)
    x[pl.ds(x.shape[0] - edge, edge), :] = jnp.zeros((edge, LANES), F32)
    swept(t, fac, middle, below, above, y, x, edge)
    start = place[0] * 2 * TILE
    for i in range(6):
        low = x[pl.ds(pl.multiple_of(start + i * TILE, TILE), TILE), :]
        fill = doubled(low)
        for m in (2 * i - 1, 2 * i):
            if 0 <= m < 10:
                sum_ref[pl.ds(16 * m, 16), :] = err[pl.ds(16 * m, 16), :] + fill


def last_kernel(
    own, below, above, mid, rhs_mid, fine, val, jhi, jlo, out_ref, ev, e1, e2, v0, v1, v2, inc
):
    for a in range(10):
        for i, src in enumerate((below, own, above)):
            ev[pl.ds(48 * a + 16 * i, 16), :] = src[pl.ds(16 * a, 16), :]

    income(ev, inc, [(48 * (a + 1) + 8, 32 * a, 8) for a in range(8)], jhi, jlo)
    for a in range(8):
        here = pl.ds(32 * a, 32)
        center = row(ev, a + 1, 48)
        total = rhs_mid[here, :] + inc[here, :]
        total = total + mid[0, here, :] * ev[pl.ds(48 * (a + 2) + 8, 32), :]
        total = total + mid[1, here, :] * ev[pl.ds(48 * a + 8, 32), :]
        total = total + mid[2, here, :] * later(center)[8:40]
        total = total + mid[3, here, :] * earlier(center)[8:40]
        e1[here, :] = (1.0 - OMEGA) * center[8:40] + mid[4, here, :] * total

    income(e1, inc, [(32, 32, 8 * 6)], jhi, jlo)
    for a in range(1, 7):
        here = pl.ds(32 * a, 32)
        center = e1[here, :]
        total = rhs_mid[here, :] + inc[here, :]
        total = total + mid[0, here, :] * row(e1, a + 1, 32)
        total = total + mid[1, here, :] * row(e1, a - 1, 32)
        total = total + mid[2, here, :] * later(center)
        total = total + mid[3, here, :] * earlier(center)
        error = (1.0 - OMEGA) * center + mid[4, here, :] * total
        fill = doubled(error)[8:56]
        for f in (2 * a - 2, 2 * a - 1):
            v0[pl.ds(48 * f, 48), :] = row(val, f, 48) + fill

    def sweep(src, dst, begin, end):
        income(src, inc, [(48 * begin, 48 * begin, 12 * (end - begin))], jhi, jlo)
        for a in range(begin, end):
            here = pl.ds(48 * a, 48)
            center = src[here, :]
            total = fine[0, here, :] + inc[here, :]
            total = total + fine[1, here, :] * row(src, a + 1, 48)
            total = total + fine[2, here, :] * row(src, a - 1, 48)
            total = total + fine[3, here, :] * later(center)
            total = total + fine[4, here, :] * earlier(center)
            dst[here, :] = (1.0 - OMEGA) * center + fine[5, here, :] * total

    sweep(v0, v1, 1, 11)
    sweep(v1, v2, 2, 10)
    for a in range(8):
        for c in range(Z):
            piece = v2[pl.ds(48 * (a + 2) + 8 + c, 8, stride=Z), :]
            out_ref[a, :, c * LANES : (c + 1) * LANES] = piece


def call(kernel, args, outs, scratch=(), flops=0, places=(), limit=24):
    outs = [x if isinstance(x, jax.ShapeDtypeStruct) else jax.ShapeDtypeStruct(x, F32) for x in outs]
    moved = sum(x.size * x.dtype.itemsize for x in (*args, *outs))
    kinds = list(places) + [pltpu.VMEM] * (len(args) - len(places))
    return pl.pallas_call(
        kernel,
        out_shape=outs,
        in_specs=[pl.BlockSpec(memory_space=kind) for kind in kinds],
        out_specs=[pl.BlockSpec(memory_space=pltpu.VMEM)] * len(outs),
        scratch_shapes=[pltpu.VMEM(s, F32) if isinstance(s, tuple) else s for s in scratch],
        compiler_params=pltpu.CompilerParams(vmem_limit_bytes=limit * 2**20),
        cost_estimate=pl.CostEstimate(flops=flops, bytes_accessed=moved, transcendentals=0),
    )(*args)


def neighbours(lo, hi, axis):
    count = lax.axis_size(axis)
    below = lax.ppermute(hi, axis, [(i, i + 1) for i in range(count - 1)])
    above = lax.ppermute(lo, axis, [(i + 1, i) for i in range(count - 1)])
    return below, above


def body(right_side, value_guess, speed_liq, speed_ill, flag_liq, flag_ill, jump_rates):
    nz = jump_rates.shape[0]
    dot_flops = 2 * 3 * nz * nz
    inputs = (right_side, value_guess, speed_liq, speed_ill, flag_liq, flag_ill)
    own, lo, hi, up, down, low = call(
        pack_kernel,
        inputs,
        [(1792, LANES)] + [(576, LANES)] * 2 + [(1184, LANES)] * 2 + [(64, LANES)],
        [pltpu.VMEM(x.shape, x.dtype) for x in inputs] + [pltpu.SemaphoreType.DMA((6,))],
        places=[pltpu.HBM] * 6,
        limit=57,
    )
    ill_below, ill_above = neighbours(lo, hi, "ill")
    below, above = neighbours(down, up, "liq")
    coefs = lax.all_gather(low, "liq", axis=0, tiled=True)
    rates = jax.ShapeDtypeStruct((nz, nz), BF16)
    jhi, jlo, out, own = call(
        rates_kernel, (jump_rates, own), [rates, rates, (TILE, LANES), own.shape]
    )
    up, down = call(corner_kernel, (ill_below, ill_above), [(720, LANES)] * 2)
    far_below, far_above = neighbours(down, up, "liq")
    fine, value, rhs_mid, lo, hi, mid = call(
        fine_kernel,
        (own, ill_below, ill_above, below, above, far_below, far_above, jhi, jlo, out),
        [(6, 576, LANES), (384, LANES), (128, LANES), (160, LANES), (160, LANES), (5, 256, LANES)],
        [(1408, LANES), (960, LANES), (960, LANES), (1408, LANES), (6, 960, LANES)],
        flops=dot_flops * 730,
    )
    below, above = neighbours(lo, hi, "ill")
    payload, err, rhs_mid, value = call(
        mid_kernel,
        (rhs_mid, value, below, above, mid, jhi, jlo, out),
        [(48, LANES), (96, LANES), (256, LANES), (576, LANES)],
        [(256, LANES)] * 3,
        flops=dot_flops * 80,
    )
    gathered = lax.all_gather(payload, "liq", axis=0, tiled=True)
    lines = gathered.shape[0] // 48 * 2 * TILE
    line, message = (lines, LANES), (lines // 2, LANES)
    fac, middle = call(factor_kernel, (coefs, out), [(5, *line), (TILE, LANES)])
    e, lo, hi = call(
        first_solve_kernel, (gathered, fac, middle), [line, message, message], [line]
    )
    place = lax.axis_index("liq").astype(jnp.int32).reshape(1)
    for step in range(SWEEPS - 1):
        below, above = neighbours(lo, hi, "ill")
        flops = dot_flops * lines // Z
        if step == 0:
            target, rhs, err = call(
                first_target_kernel,
                (place, gathered, err, e, fac, jhi, jlo),
                [line, line, (160, LANES)],
                flops=flops,
                places=[pltpu.SMEM],
            )
        else:
            (target,) = call(local_target, (e, rhs, fac, jhi, jlo), [line], flops=flops)
        if step < SWEEPS - 2:
            e, lo, hi = call(
                sweep_kernel, (target, fac, middle, below, above), [line, message, message], [line]
            )
    (total,) = call(
        last_sweep_kernel,
        (place, target, fac, middle, below, above, err),
        [(160, LANES)],
        [line, (lines + 4 * TILE, LANES)],
        places=[pltpu.SMEM],
    )
    below, above = neighbours(total, total, "ill")
    (result,) = call(
        last_kernel,
        (total, below, above, mid, rhs_mid, fine, value, jhi, jlo),
        [right_side.shape],
        [(480, LANES), (256, LANES), (256, LANES)] + [(576, LANES)] * 4,
        flops=dot_flops * 330,
    )
    return result


def solution(mesh):
    block = P("liq", "ill", None)
    return jax.shard_map(
        body, mesh=mesh, in_specs=(block,) * 6 + (P(),), out_specs=block, check_vma=False
    )
```

```python
import functools

import jax
import jax.numpy as jnp
from jax import lax
from jax.experimental import pallas as pl
from jax.experimental.pallas import tpu as pltpu
from jax.sharding import PartitionSpec as P

SWEEPS = 4
OMEGA = 0.8
DISCOUNT = 0.05
LANES = 128
F32 = jnp.float32
BF16 = jnp.bfloat16

Z = 4
TILE = 8


def first_half(shape):
    return lax.broadcasted_iota(jnp.int32, shape, len(shape) - 2) % TILE < Z


def swapped(x):
    return pltpu.roll(x.reshape(-1, TILE, LANES), Z, 1).reshape(x.shape)


def later(x):
    return pltpu.roll(x, x.shape[0] - Z, 0)


def earlier(x):
    return pltpu.roll(x, Z, 0)


def pair_sums(x):
    total = x + swapped(x)
    total = total.reshape(-1, 2, TILE, LANES)
    first, second = total[:, 0], total[:, 1]
    return jnp.where(first_half(first.shape), first, second).reshape(-1, LANES)


def doubled(x):
    other = swapped(x).reshape(-1, 1, TILE, LANES)
    x = x.reshape(-1, 1, TILE, LANES)
    mask = first_half(x.shape)
    pair = jnp.concatenate([jnp.where(mask, x, other), jnp.where(mask, other, x)], axis=1)
    return pair.reshape(-1, LANES)


def spread(outflow, rows):
    return jnp.concatenate([outflow] * (rows // TILE), axis=0)


def row(ref, a, width):
    return ref[pl.ds(a * width, width), :]


def product(wide, jhi_ref, jlo_ref):
    high = wide.astype(BF16)
    rest = (wide - high.astype(F32)).astype(BF16)
    dot = functools.partial(jnp.dot, preferred_element_type=F32)
    count = wide.shape[0]
    both = dot(jnp.concatenate([high, rest], axis=0), jhi_ref[...])
    return both[:count] + (both[count:] + dot(high, jlo_ref[...]))


def income(src, dst, pieces, jhi_ref, jlo_ref):
    wide = jnp.concatenate(
        [
            jnp.concatenate([src[pl.ds(s + c, n, stride=Z), :] for s, _, n in pieces], axis=0)
            for c in range(Z)
        ],
        axis=1,
    )
    result = product(wide, jhi_ref, jlo_ref)
    at = 0
    for _, d, n in pieces:
        for c in range(Z):
            dst[pl.ds(d + c, n, stride=Z), :] = result[at : at + n, c * LANES : (c + 1) * LANES]
        at += n


def rates_kernel(j_ref, own, jhi_ref, jlo_ref, out_ref, own_ref):
    own_ref[...] = own[...]
    rates = j_ref[...]
    high = rates.astype(BF16)
    jhi_ref[...] = high
    jlo_ref[...] = (rates - high.astype(F32)).astype(BF16)
    total = jnp.sum(rates, axis=0, keepdims=True)
    for c in range(Z):
        piece = total[:, c * LANES : (c + 1) * LANES]
        out_ref[c : c + 1, :] = piece
        out_ref[c + Z : c + Z + 1, :] = piece


def unpack(sources, buffers, own_ref, sems):
    copies = [
        pltpu.make_async_copy(src, dst, sems.at[i])
        for i, (src, dst) in enumerate(zip(sources, buffers))
    ]
    for copy in copies:
        copy.start()
    rhs, value, speed_a, speed_b, flag_a, flag_b = buffers

    def put(start, x):
        for c in range(Z):
            own_ref[pl.ds(start + c, 8, stride=Z), :] = x[:, c * LANES : (c + 1) * LANES]

    for copy in copies:
        copy.wait()
    for a in range(8):
        put(32 * a, value[a])
        put(256 + 32 * a, rhs[a])
        for k, speed, flag in ((2, speed_a, flag_a), (4, speed_b, flag_b)):
            up = flag[a].astype(F32)
            put(256 * k + 32 * a, speed[a] * up)
            put(256 * (k + 1) + 32 * a, speed[a] * (1.0 - up))
    for k in range(4):
        for m in range(4):
            at = 256 * (k + 2) + 64 * m
            mid = 0.125 * pair_sums(own_ref[pl.ds(at, 32), :] + own_ref[pl.ds(at + 32, 32), :])
            own_ref[pl.ds(1536 + 64 * k + 16 * m, 16), :] = mid


def pack_kernel(*refs):
    sources, outs, buffers = refs[:6], refs[6:11], refs[11:17]
    lo_ref, hi_ref, up_ref, down_ref, low_ref = outs
    own_ref, sems = refs[17:]
    unpack(sources, buffers, own_ref, sems)
    for k in range(4):
        for m in range(4):
            mid = own_ref[pl.ds(1536 + 64 * k + 16 * m, 16), :]
            lo_ref[pl.ds(448 + 32 * k + 8 * m, 8), :] = mid[:8]
            hi_ref[pl.ds(448 + 32 * k + 8 * m, 8), :] = mid[8:]
    for a in range(8):
        lo_ref[pl.ds(16 * a, 16), :] = own_ref[pl.ds(32 * a, 16), :]
        hi_ref[pl.ds(16 * a, 16), :] = own_ref[pl.ds(32 * a + 16, 16), :]
        for k in range(5):
            at = 256 * (k + 1) + 32 * a
            lo_ref[pl.ds(128 + 64 * k + 8 * a, 8), :] = own_ref[pl.ds(at, 8), :]
            hi_ref[pl.ds(128 + 64 * k + 8 * a, 8), :] = own_ref[pl.ds(at + 24, 8), :]
    up_ref[0:224, :] = own_ref[32:256, :]
    down_ref[0:224, :] = own_ref[0:224, :]
    for k in range(5):
        here = pl.ds(224 + 192 * k, 192)
        up_ref[here, :] = own_ref[pl.ds(256 * (k + 1) + 64, 192), :]
        down_ref[here, :] = own_ref[pl.ds(256 * (k + 1), 192), :]
    for k in range(4):
        for m in range(2):
            at = 1536 + 64 * k + 32 * m
            both = own_ref[pl.ds(at, 16), :] + own_ref[pl.ds(at + 16, 16), :]
            low_ref[pl.ds(16 * k + 8 * m, 8), :] = 0.125 * pair_sums(both)


def own_kernel(*refs):
    unpack(refs[:6], refs[7:13], refs[6], refs[13])


def corner_kernel(below, above, up_ref, down_ref):
    def put(out, at, src, width):
        out[pl.ds(at, width), :] = below[pl.ds(src, width), :]
        out[pl.ds(at + width, width), :] = above[pl.ds(src, width), :]

    for out, shift in ((up_ref, 1), (down_ref, 0)):
        for i in range(6):
            put(out, 32 * i, 16 * (i + 2 * shift), 16)
        for k in range(5):
            for i in range(5):
                put(out, 192 + 80 * k + 16 * i, 128 + 64 * k + 8 * (i + 3 * shift), 8)
        for k in range(4):
            for i in range(2):
                put(out, 592 + 32 * k + 16 * i, 448 + 32 * k + 8 * (i + 2 * shift), 8)


def assemblers(own, ill_below, ill_above, below, above, far_below, far_above):
    def joined(first, middle, last):
        parts = [ref[pl.ds(at, width), :] for ref, at, width in (first, middle, last)]
        return jnp.concatenate(parts, axis=0)

    def padded(middle, width):
        edge = jnp.zeros((width, LANES), F32)
        ref, at, count = middle
        return jnp.concatenate([edge, ref[pl.ds(at, count), :], edge], axis=0)

    def value(a):
        if a < 7:
            i, far, middle = a - 1, far_below, (below, 32 * a, 32)
        elif a < 15:
            i, far, middle = a - 7, None, (own, 32 * (a - 7), 32)
        else:
            i, far, middle = a - 15, far_above, (above, 32 * (a - 15), 32)
        if far is None:
            return joined((ill_below, 16 * i, 16), middle, (ill_above, 16 * i, 16))
        if 0 <= i < 6:
            return joined((far, 32 * i, 16), middle, (far, 32 * i + 16, 16))
        return padded(middle, 16)

    def field(k, a):
        if a < 6:
            i, far, middle = a - 1, far_below, (below, 224 + 192 * k + 32 * a, 32)
        elif a < 14:
            i, far, middle = a - 6, None, (own, 256 * (k + 1) + 32 * (a - 6), 32)
        else:
            i, far, middle = a - 14, far_above, (above, 224 + 192 * k + 32 * (a - 14), 32)
        if far is None:
            at = 128 + 64 * k + 8 * i
            return joined((ill_below, at, 8), middle, (ill_above, at, 8))
        if 0 <= i < 5:
            at = 192 + 80 * k + 16 * i
            return joined((far, at, 8), middle, (far, at + 8, 8))
        return padded(middle, 8)

    def mid(k, m):
        if 1 < m < 6:
            at = 448 + 32 * k + 8 * (m - 2)
            middle = (own, 1536 + 64 * k + 16 * (m - 2), 16)
            return joined((ill_below, at, 8), middle, (ill_above, at, 8))
        near, i = (below, 2 * m + 2) if m < 2 else (above, 2 * m - 12)
        at = 224 + 192 * (k + 1) + 32 * i
        far, corner = (far_below, 16 * m) if m < 2 else (far_above, 16 * (m - 6))
        corner += 592 + 32 * k
        middle = 0.125 * pair_sums(near[pl.ds(at, 32), :] + near[pl.ds(at + 32, 32), :])
        return jnp.concatenate([far[pl.ds(corner, 8), :], middle, far[pl.ds(corner + 8, 8), :]], axis=0)

    return value, field, mid


def keep_kernel(own, ill_below, ill_above, below, above, far_below, far_above, out, keep_ref, mid_ref):
    _, field, mid = assemblers(own, ill_below, ill_above, below, above, far_below, far_above)
    outflow = spread(out[...], 48)
    for a in range(12):
        here = pl.ds(48 * a, 48)
        total = DISCOUNT + outflow
        for k in range(5):
            x = field(k, a + 4)
            keep_ref[k, here, :] = x
            if k:
                total = total + x
        keep_ref[5, here, :] = OMEGA / total
    outflow = spread(out[...], 32)
    for m in range(8):
        here = pl.ds(32 * m, 32)
        total = DISCOUNT + outflow
        for k in range(4):
            x = mid(k, m)
            mid_ref[k, here, :] = x
            total = total + x
        mid_ref[4, here, :] = OMEGA / total


def fine_kernel(
    own, ill_below, ill_above, below, above, far_below, far_above, jhi, jlo, out,
    val_ref, rhs_ref, lo_ref, hi_ref, v0, v1, v2, inc, f,
):
    value, field, _ = assemblers(own, ill_below, ill_above, below, above, far_below, far_above)
    for a in range(22):
        v0[pl.ds(64 * a, 64), :] = value(a)
    outflow = spread(out[...], 48)
    for a in range(20):
        here = pl.ds(48 * a, 48)
        total = DISCOUNT + outflow
        for k in range(5):
            x = field(k, a)
            f[k, here, :] = x
            if k:
                total = total + x
        f[5, here, :] = OMEGA / total

    def rest(a):
        here = pl.ds(48 * a, 48)
        return f[0, here, :], f[1, here, :], f[2, here, :], f[3, here, :], f[4, here, :]

    income(v0, inc, [(64, 64, 16 * 20)], jhi, jlo)
    for a in range(20):
        rhs, fa, ba, fb, bb = rest(a)
        center = row(v0, a + 1, 64)
        total = rhs + inc[pl.ds(64 * (a + 1) + 8, 48), :]
        total = total + fa * v0[pl.ds(64 * (a + 2) + 8, 48), :]
        total = total + ba * v0[pl.ds(64 * a + 8, 48), :]
        total = total + fb * later(center)[8:56] + bb * earlier(center)[8:56]
        here = pl.ds(48 * a, 48)
        v1[here, :] = (1.0 - OMEGA) * center[8:56] + f[5, here, :] * total

    def applied(src, a):
        rhs, fa, ba, fb, bb = rest(a)
        center = row(src, a, 48)
        total = rhs + row(inc, a, 48) + fa * row(src, a + 1, 48) + ba * row(src, a - 1, 48)
        return center, total + fb * later(center) + bb * earlier(center)

    income(v1, inc, [(48, 48, 12 * 18)], jhi, jlo)
    for a in range(1, 19):
        center, total = applied(v1, a)
        here = pl.ds(48 * a, 48)
        v2[here, :] = (1.0 - OMEGA) * center + f[5, here, :] * total
    income(v2, inc, [(96, 96, 12 * 16)], jhi, jlo)

    def residual(a):
        center, total = applied(v2, a)
        diag = DISCOUNT + outflow
        for x in rest(a)[1:]:
            diag = diag + x
        return (total - diag * center)[8:40]

    for m in range(8):
        coarse = 0.25 * pair_sums(residual(2 + 2 * m) + residual(3 + 2 * m))
        rhs_ref[pl.ds(16 * m, 16), :] = coarse
        lo_ref[pl.ds(8 * m, 8), :] = coarse[:8]
        hi_ref[pl.ds(8 * m, 8), :] = coarse[8:]
    for a in range(12):
        value = row(v2, a + 4, 48)[8:40]
        val_ref[pl.ds(32 * a, 32), :] = value
        lo_ref[pl.ds(64 + 8 * a, 8), :] = value[:8]
        hi_ref[pl.ds(64 + 8 * a, 8), :] = value[24:]


def widen_rhs(own, below, above, rhs_ref):
    for a in range(8):
        for i, piece in enumerate((below[pl.ds(8 * a, 8), :], row(own, a, 16), above[pl.ds(8 * a, 8), :])):
            rhs_ref[pl.ds(32 * a + (0, 8, 24)[i], piece.shape[0]), :] = piece


def widen_value(val, below, above, wide_ref):
    for a in range(12):
        ends = [src[pl.ds(64 + 8 * a, 8), :] for src in (below, above)]
        wide_ref[pl.ds(48 * a, 8), :] = ends[0]
        wide_ref[pl.ds(48 * a + 8, 32), :] = row(val, a, 32)
        wide_ref[pl.ds(48 * a + 40, 8), :] = ends[1]


def mid_kernel(own, below, above, mid, jhi, jlo, out, pay_ref, err_ref, rhs_ref, e0, e1, inc):
    widen_rhs(own, below, above, rhs_ref)
    e0[...] = mid[4] * rhs_ref[...]

    def applied(src, a):
        here = pl.ds(32 * a, 32)
        center = src[here, :]
        total = rhs_ref[here, :] + inc[here, :]
        total = total + mid[0, here, :] * row(src, a + 1, 32)
        total = total + mid[1, here, :] * row(src, a - 1, 32)
        total = total + mid[2, here, :] * later(center)
        total = total + mid[3, here, :] * earlier(center)
        return center, total

    income(e0, inc, [(32, 32, 8 * 6)], jhi, jlo)
    for a in range(1, 7):
        center, total = applied(e0, a)
        here = pl.ds(32 * a, 32)
        e1[here, :] = (1.0 - OMEGA) * center + mid[4, here, :] * total
    income(e1, inc, [(64, 64, 8 * 4)], jhi, jlo)
    outflow = spread(out[...], 32)

    def residual(a):
        center, total = applied(e1, a)
        here = pl.ds(32 * a, 32)
        diag = DISCOUNT + outflow
        for k in range(4):
            diag = diag + mid[k, here, :]
        return (total - diag * center)[8:24]

    for m in range(2):
        pay_ref[pl.ds(8 * m, 8), :] = 0.25 * pair_sums(residual(2 + 2 * m) + residual(3 + 2 * m))
    for a in range(6):
        err_ref[pl.ds(16 * a, 16), :] = e1[pl.ds(32 * (a + 1) + 8, 16), :]
    pay_ref[16:48, :] = err_ref[32:64, :]


def solve_lines(target, weight, carry, link, middle, y, x_ref, offset):
    count = y.shape[0] // TILE
    half = count // 2
    top = bottom = None
    for i in range(half):
        j = count - 1 - i
        t = weight(i) * target(i)
        u = weight(j) * target(j)
        top = t if i == 0 else t + carry(i) * top
        bottom = u if i == 0 else u + carry(j) * bottom
        if i < half - 1:
            y[pl.ds(TILE * i, TILE), :] = top
            y[pl.ds(TILE * j, TILE), :] = bottom
    head = (top + link(half - 1) * bottom) * middle
    tail = bottom + link(half) * head
    for i in range(half - 1, -1, -1):
        j = count - 1 - i
        if i < half - 1:
            head = row(y, i, TILE) + link(i) * head
            tail = row(y, j, TILE) + link(j) * tail
        x_ref[pl.ds(offset + TILE * i, TILE), :] = head
        x_ref[pl.ds(offset + TILE * j, TILE), :] = tail


def send_lines(e, lo_ref, hi_ref):
    pairs = e[...].reshape(-1, 2, TILE, LANES)
    first, second = pairs[:, 0], pairs[:, 1]
    mask = first_half(first.shape)
    lo_ref[...] = jnp.where(mask, first, pltpu.roll(second, Z, 1)).reshape(-1, LANES)
    hi_ref[...] = jnp.where(mask, pltpu.roll(first, Z, 1), second).reshape(-1, LANES)


def factor_kernel(gathered, out, fac_ref, middle_ref):
    count = fac_ref.shape[1] // TILE

    def part(k, a):
        return gathered[pl.ds(64 * (a // 2) + 16 * k + 8 * (a % 2), TILE), :]

    outflow = DISCOUNT + out[...]
    gaps = [None, None]
    links = [None, None]
    for i in range(count // 2):
        for side, a in ((0, i), (1, count - 1 - i)):
            here = pl.ds(TILE * a, TILE)
            inner, outer = (part(0, a), part(1, a)) if side == 0 else (part(1, a), part(0, a))
            fb, bb = part(2, a), part(3, a)
            slack = outflow + fb + bb
            slack = slack + (outer if i == 0 else outer * gaps[side])
            weight = 1.0 / (slack + inner)
            links[side] = inner * weight
            gaps[side] = slack * weight
            fac_ref[0, here, :] = fb
            fac_ref[1, here, :] = bb
            fac_ref[2, here, :] = weight
            fac_ref[3, here, :] = outer * weight
            fac_ref[4, here, :] = links[side]
    middle_ref[...] = 1.0 / (gaps[0] + links[0] * gaps[1])


def first_solve_kernel(gathered, fac, middle, e_ref, lo_ref, hi_ref, y):
    solve_lines(
        lambda a: gathered[pl.ds(48 * (a // 2) + 8 * (a % 2), TILE), :],
        lambda a: row(fac.at[2], a, TILE),
        lambda a: row(fac.at[3], a, TILE),
        lambda a: row(fac.at[4], a, TILE),
        middle[...], y, e_ref, 0,
    )
    send_lines(e_ref, lo_ref, hi_ref)


def local_target(e, rhs, fac, jhi, jlo, t_ref):
    income(e, t_ref, [(0, 0, e.shape[0] // Z)], jhi, jlo)
    other = swapped(e[...])
    mask = first_half(other.shape)
    t_ref[...] = t_ref[...] + rhs[...] + jnp.where(mask, fac[0], fac[1]) * other


def first_target_kernel(
    gathered, err, e, fac, jhi, jlo, rhs_mid, val, below, above,
    t_ref, rhs_ref, wide_ref, rhs_wide_ref, val_wide_ref,
):
    blocks = e.shape[0] // (2 * TILE)
    for i in range(blocks):
        rhs_ref[pl.ds(16 * i, 16), :] = gathered[pl.ds(48 * i, 16), :]
    local_target(e, rhs_ref, fac, jhi, jlo, t_ref)
    widen_rhs(rhs_mid, below, above, rhs_wide_ref)
    widen_value(val, below, above, val_wide_ref)
    here = lax.axis_index("liq")
    wide_ref[32:128, :] = err[...]
    for at, block, inside in ((0, here - 1, here > 0), (128, here + 1, here < blocks - 1)):
        block = jnp.minimum(jnp.maximum(block, 0), blocks - 1)
        start = pl.multiple_of(block * 48 + 16, 16)
        piece = gathered[pl.ds(start, 32), :]
        wide_ref[pl.ds(at, 32), :] = jnp.where(inside, piece, jnp.zeros_like(piece))


def swept(t, fac, middle, below, above, y, x_ref, offset):
    mask = first_half((TILE, LANES))

    def target(a):
        low_side, high_side = row(below, a // 2, TILE), row(above, a // 2, TILE)
        if a % 2:
            low_side = pltpu.roll(low_side, Z, 0)
        else:
            high_side = pltpu.roll(high_side, Z, 0)
        near = jnp.where(mask, low_side, high_side)
        coupling = jnp.where(mask, row(fac.at[1], a, TILE), row(fac.at[0], a, TILE))
        return row(t, a, TILE) + coupling * near

    solve_lines(
        target,
        lambda a: row(fac.at[2], a, TILE),
        lambda a: row(fac.at[3], a, TILE),
        lambda a: row(fac.at[4], a, TILE),
        middle[...], y, x_ref, offset,
    )


def sweep_kernel(t, fac, middle, below, above, e_ref, lo_ref, hi_ref, y):
    swept(t, fac, middle, below, above, y, e_ref, 0)
    send_lines(e_ref, lo_ref, hi_ref)


def last_sweep_kernel(t, fac, middle, below, above, err, sum_ref, y, x):
    edge = 2 * TILE
    x[0:edge, :] = jnp.zeros((edge, LANES), F32)
    x[pl.ds(x.shape[0] - edge, edge), :] = jnp.zeros((edge, LANES), F32)
    swept(t, fac, middle, below, above, y, x, edge)
    start = lax.axis_index("liq") * 2 * TILE
    for i in range(6):
        low = x[pl.ds(pl.multiple_of(start + i * TILE, TILE), TILE), :]
        fill = doubled(low)
        for m in (2 * i - 1, 2 * i):
            if 0 <= m < 10:
                sum_ref[pl.ds(16 * m, 16), :] = err[pl.ds(16 * m, 16), :] + fill


def last_kernel(
    own, below, above, mid, rhs_mid, fine, val, jhi, jlo, out_ref, ev, e1, e2, v0, v1, v2, inc
):
    for a in range(10):
        for i, src in enumerate((below, own, above)):
            ev[pl.ds(48 * a + 16 * i, 16), :] = src[pl.ds(16 * a, 16), :]

    income(ev, inc, [(48 * (a + 1) + 8, 32 * a, 8) for a in range(8)], jhi, jlo)
    for a in range(8):
        here = pl.ds(32 * a, 32)
        center = row(ev, a + 1, 48)
        total = rhs_mid[here, :] + inc[here, :]
        total = total + mid[0, here, :] * ev[pl.ds(48 * (a + 2) + 8, 32), :]
        total = total + mid[1, here, :] * ev[pl.ds(48 * a + 8, 32), :]
        total = total + mid[2, here, :] * later(center)[8:40]
        total = total + mid[3, here, :] * earlier(center)[8:40]
        e1[here, :] = (1.0 - OMEGA) * center[8:40] + mid[4, here, :] * total

    income(e1, inc, [(32, 32, 8 * 6)], jhi, jlo)
    for a in range(1, 7):
        here = pl.ds(32 * a, 32)
        center = e1[here, :]
        total = rhs_mid[here, :] + inc[here, :]
        total = total + mid[0, here, :] * row(e1, a + 1, 32)
        total = total + mid[1, here, :] * row(e1, a - 1, 32)
        total = total + mid[2, here, :] * later(center)
        total = total + mid[3, here, :] * earlier(center)
        error = (1.0 - OMEGA) * center + mid[4, here, :] * total
        fill = doubled(error)[8:56]
        for f in (2 * a - 2, 2 * a - 1):
            v0[pl.ds(48 * f, 48), :] = row(val, f, 48) + fill

    def sweep(src, dst, begin, end):
        income(src, inc, [(48 * begin, 48 * begin, 12 * (end - begin))], jhi, jlo)
        for a in range(begin, end):
            here = pl.ds(48 * a, 48)
            center = src[here, :]
            total = fine[0, here, :] + inc[here, :]
            total = total + fine[1, here, :] * row(src, a + 1, 48)
            total = total + fine[2, here, :] * row(src, a - 1, 48)
            total = total + fine[3, here, :] * later(center)
            total = total + fine[4, here, :] * earlier(center)
            dst[here, :] = (1.0 - OMEGA) * center + fine[5, here, :] * total

    sweep(v0, v1, 1, 11)
    sweep(v1, v2, 2, 10)
    for a in range(8):
        for c in range(Z):
            piece = v2[pl.ds(48 * (a + 2) + 8 + c, 8, stride=Z), :]
            out_ref[a, :, c * LANES : (c + 1) * LANES] = piece


def call(kernel, args, outs, scratch=(), flops=0, places=(), limit=24):
    outs = [x if isinstance(x, jax.ShapeDtypeStruct) else jax.ShapeDtypeStruct(x, F32) for x in outs]
    moved = sum(x.size * x.dtype.itemsize for x in (*args, *outs))
    kinds = list(places) + [pltpu.VMEM] * (len(args) - len(places))
    return pl.pallas_call(
        kernel,
        out_shape=outs,
        in_specs=[pl.BlockSpec(memory_space=kind) for kind in kinds],
        out_specs=[pl.BlockSpec(memory_space=pltpu.VMEM)] * len(outs),
        scratch_shapes=[pltpu.VMEM(s, F32) if isinstance(s, tuple) else s for s in scratch],
        compiler_params=pltpu.CompilerParams(vmem_limit_bytes=limit * 2**20),
        cost_estimate=pl.CostEstimate(flops=flops, bytes_accessed=moved, transcendentals=0),
    )(*args)


def neighbours(lo, hi, axis):
    count = lax.axis_size(axis)
    below = lax.ppermute(hi, axis, [(i, i + 1) for i in range(count - 1)])
    above = lax.ppermute(lo, axis, [(i + 1, i) for i in range(count - 1)])
    return below, above


def body(right_side, value_guess, speed_liq, speed_ill, flag_liq, flag_ill, jump_rates):
    nz = jump_rates.shape[0]
    dot_flops = 2 * 3 * nz * nz
    inputs = (right_side, value_guess, speed_liq, speed_ill, flag_liq, flag_ill)
    buffers = [pltpu.VMEM(x.shape, x.dtype) for x in inputs]
    sems = pltpu.SemaphoreType.DMA((6,))
    lo, hi, up, down, low = call(
        pack_kernel,
        inputs,
        [(576, LANES)] * 2 + [(1184, LANES)] * 2 + [(64, LANES)],
        buffers + [(1792, LANES), sems],
        places=[pltpu.HBM] * 6,
        limit=57,
    )
    ill_below, ill_above = neighbours(lo, hi, "ill")
    below, above = neighbours(down, up, "liq")
    coefs = lax.all_gather(low, "liq", axis=0, tiled=True)
    rates = jax.ShapeDtypeStruct((nz, nz), BF16)
    (own,) = call(
        own_kernel, inputs, [(1792, LANES)], buffers + [sems], places=[pltpu.HBM] * 6, limit=57
    )
    jhi, jlo, out, own = call(
        rates_kernel, (jump_rates, own), [rates, rates, (TILE, LANES), own.shape]
    )
    up, down = call(corner_kernel, (ill_below, ill_above), [(720, LANES)] * 2)
    far_below, far_above = neighbours(down, up, "liq")
    pieces = (own, ill_below, ill_above, below, above, far_below, far_above)
    value, rhs_mid, lo, hi = call(
        fine_kernel,
        (*pieces, jhi, jlo, out),
        [(384, LANES), (128, LANES), (160, LANES), (160, LANES)],
        [(1408, LANES), (960, LANES), (960, LANES), (1408, LANES), (6, 960, LANES)],
        flops=dot_flops * 730,
    )
    mid_below, mid_above = neighbours(lo, hi, "ill")
    fine, mid = call(keep_kernel, (*pieces, out), [(6, 576, LANES), (5, 256, LANES)])
    payload, err = call(
        mid_kernel,
        (rhs_mid, mid_below, mid_above, mid, jhi, jlo, out),
        [(48, LANES), (96, LANES)],
        [(256, LANES)] * 4,
        flops=dot_flops * 80,
    )
    gathered = lax.all_gather(payload, "liq", axis=0, tiled=True)
    lines = gathered.shape[0] // 48 * 2 * TILE
    line, message = (lines, LANES), (lines // 2, LANES)
    fac, middle = call(factor_kernel, (coefs, out), [(5, *line), (TILE, LANES)])
    e, lo, hi = call(
        first_solve_kernel, (gathered, fac, middle), [line, message, message], [line]
    )
    for step in range(SWEEPS - 1):
        below, above = neighbours(lo, hi, "ill")
        flops = dot_flops * lines // Z
        if step == 0:
            target, rhs, err, rhs_mid, value = call(
                first_target_kernel,
                (gathered, err, e, fac, jhi, jlo, rhs_mid, value, mid_below, mid_above),
                [line, line, (160, LANES), (256, LANES), (576, LANES)],
                flops=flops,
            )
        else:
            (target,) = call(local_target, (e, rhs, fac, jhi, jlo), [line], flops=flops)
        if step < SWEEPS - 2:
            e, lo, hi = call(
                sweep_kernel, (target, fac, middle, below, above), [line, message, message], [line]
            )
    (total,) = call(
        last_sweep_kernel,
        (target, fac, middle, below, above, err),
        [(160, LANES)],
        [line, (lines + 4 * TILE, LANES)],
    )
    below, above = neighbours(total, total, "ill")
    (result,) = call(
        last_kernel,
        (total, below, above, mid, rhs_mid, fine, value, jhi, jlo),
        [right_side.shape],
        [(480, LANES), (256, LANES), (256, LANES)] + [(576, LANES)] * 4,
        flops=dot_flops * 330,
    )
    return result


def solution(mesh):
    block = P("liq", "ill", None)
    return jax.shard_map(
        body, mesh=mesh, in_specs=(block,) * 6 + (P(),), out_specs=block, check_vma=False
    )
```

```python
import functools

import jax
import jax.numpy as jnp
from jax import lax
from jax.experimental import pallas as pl
from jax.experimental.pallas import tpu as pltpu
from jax.sharding import PartitionSpec as P

SWEEPS = 4
OMEGA = 0.8
DISCOUNT = 0.05
LANES = 128
F32 = jnp.float32
BF16 = jnp.bfloat16

Z = 4
TILE = 8


def first_half(shape):
    return lax.broadcasted_iota(jnp.int32, shape, len(shape) - 2) % TILE < Z


def swapped(x):
    return pltpu.roll(x.reshape(-1, TILE, LANES), Z, 1).reshape(x.shape)


def later(x):
    return pltpu.roll(x, x.shape[0] - Z, 0)


def earlier(x):
    return pltpu.roll(x, Z, 0)


def pair_sums(x):
    total = x + swapped(x)
    total = total.reshape(-1, 2, TILE, LANES)
    first, second = total[:, 0], total[:, 1]
    return jnp.where(first_half(first.shape), first, second).reshape(-1, LANES)


def doubled(x):
    other = swapped(x).reshape(-1, 1, TILE, LANES)
    x = x.reshape(-1, 1, TILE, LANES)
    mask = first_half(x.shape)
    pair = jnp.concatenate([jnp.where(mask, x, other), jnp.where(mask, other, x)], axis=1)
    return pair.reshape(-1, LANES)


def spread(outflow, rows):
    return jnp.concatenate([outflow] * (rows // TILE), axis=0)


def row(ref, a, width):
    return ref[pl.ds(a * width, width), :]


def product(wide, jhi_ref, jlo_ref):
    high = wide.astype(BF16)
    rest = (wide - high.astype(F32)).astype(BF16)
    dot = functools.partial(jnp.dot, preferred_element_type=F32)
    count = wide.shape[0]
    both = dot(jnp.concatenate([high, rest], axis=0), jhi_ref[...])
    return both[:count] + (both[count:] + dot(high, jlo_ref[...]))


def income(src, dst, pieces, jhi_ref, jlo_ref):
    wide = jnp.concatenate(
        [
            jnp.concatenate([src[pl.ds(s + c, n, stride=Z), :] for s, _, n in pieces], axis=0)
            for c in range(Z)
        ],
        axis=1,
    )
    result = product(wide, jhi_ref, jlo_ref)
    at = 0
    for _, d, n in pieces:
        for c in range(Z):
            dst[pl.ds(d + c, n, stride=Z), :] = result[at : at + n, c * LANES : (c + 1) * LANES]
        at += n


def rates_kernel(j_ref, own, jhi_ref, jlo_ref, out_ref, own_ref):
    own_ref[...] = own[...]
    rates = j_ref[...]
    high = rates.astype(BF16)
    jhi_ref[...] = high
    jlo_ref[...] = (rates - high.astype(F32)).astype(BF16)
    total = jnp.sum(rates, axis=0, keepdims=True)
    for c in range(Z):
        piece = total[:, c * LANES : (c + 1) * LANES]
        out_ref[c : c + 1, :] = piece
        out_ref[c + Z : c + Z + 1, :] = piece


def unpack(sources, buffers, own_ref, sems):
    copies = [
        pltpu.make_async_copy(src, dst, sems.at[i])
        for i, (src, dst) in enumerate(zip(sources, buffers))
    ]
    for copy in copies:
        copy.start()
    rhs, value, speed_a, speed_b, flag_a, flag_b = buffers

    def put(start, x):
        for c in range(Z):
            own_ref[pl.ds(start + c, 8, stride=Z), :] = x[:, c * LANES : (c + 1) * LANES]

    for copy in copies:
        copy.wait()
    for a in range(8):
        put(32 * a, value[a])
        put(256 + 32 * a, rhs[a])
        for k, speed, flag in ((2, speed_a, flag_a), (4, speed_b, flag_b)):
            up = flag[a].astype(F32)
            put(256 * k + 32 * a, speed[a] * up)
            put(256 * (k + 1) + 32 * a, speed[a] * (1.0 - up))
    for k in range(4):
        for m in range(4):
            at = 256 * (k + 2) + 64 * m
            mid = 0.125 * pair_sums(own_ref[pl.ds(at, 32), :] + own_ref[pl.ds(at + 32, 32), :])
            own_ref[pl.ds(1536 + 64 * k + 16 * m, 16), :] = mid


def pack_kernel(*refs):
    sources, outs, buffers = refs[:6], refs[6:11], refs[11:17]
    lo_ref, hi_ref, up_ref, down_ref, copies_ref = outs
    own_ref, sems = refs[17:]
    unpack(sources, buffers, own_ref, sems)
    for k in range(4):
        for m in range(4):
            mid = own_ref[pl.ds(1536 + 64 * k + 16 * m, 16), :]
            lo_ref[pl.ds(448 + 32 * k + 8 * m, 8), :] = mid[:8]
            hi_ref[pl.ds(448 + 32 * k + 8 * m, 8), :] = mid[8:]
    for a in range(8):
        lo_ref[pl.ds(16 * a, 16), :] = own_ref[pl.ds(32 * a, 16), :]
        hi_ref[pl.ds(16 * a, 16), :] = own_ref[pl.ds(32 * a + 16, 16), :]
        for k in range(5):
            at = 256 * (k + 1) + 32 * a
            lo_ref[pl.ds(128 + 64 * k + 8 * a, 8), :] = own_ref[pl.ds(at, 8), :]
            hi_ref[pl.ds(128 + 64 * k + 8 * a, 8), :] = own_ref[pl.ds(at + 24, 8), :]
    up_ref[0:224, :] = own_ref[32:256, :]
    down_ref[0:224, :] = own_ref[0:224, :]
    for k in range(5):
        here = pl.ds(224 + 192 * k, 192)
        up_ref[here, :] = own_ref[pl.ds(256 * (k + 1) + 64, 192), :]
        down_ref[here, :] = own_ref[pl.ds(256 * (k + 1), 192), :]
    for k in range(4):
        for m in range(2):
            at = 1536 + 64 * k + 32 * m
            both = own_ref[pl.ds(at, 16), :] + own_ref[pl.ds(at + 16, 16), :]
            low = 0.125 * pair_sums(both)
            for i in range(copies_ref.shape[0] // 64):
                copies_ref[pl.ds(64 * i + 16 * k + 8 * m, 8), :] = low


def own_kernel(*refs):
    unpack(refs[:6], refs[7:13], refs[6], refs[13])


def corner_kernel(below, above, up_ref, down_ref):
    def put(out, at, src, width):
        out[pl.ds(at, width), :] = below[pl.ds(src, width), :]
        out[pl.ds(at + width, width), :] = above[pl.ds(src, width), :]

    for out, shift in ((up_ref, 1), (down_ref, 0)):
        for i in range(6):
            put(out, 32 * i, 16 * (i + 2 * shift), 16)
        for k in range(5):
            for i in range(5):
                put(out, 192 + 80 * k + 16 * i, 128 + 64 * k + 8 * (i + 3 * shift), 8)
        for k in range(4):
            for i in range(2):
                put(out, 592 + 32 * k + 16 * i, 448 + 32 * k + 8 * (i + 2 * shift), 8)


def assemblers(own, ill_below, ill_above, below, above, far_below, far_above):
    def joined(first, middle, last):
        parts = [ref[pl.ds(at, width), :] for ref, at, width in (first, middle, last)]
        return jnp.concatenate(parts, axis=0)

    def padded(middle, width):
        edge = jnp.zeros((width, LANES), F32)
        ref, at, count = middle
        return jnp.concatenate([edge, ref[pl.ds(at, count), :], edge], axis=0)

    def value(a):
        if a < 7:
            i, far, middle = a - 1, far_below, (below, 32 * a, 32)
        elif a < 15:
            i, far, middle = a - 7, None, (own, 32 * (a - 7), 32)
        else:
            i, far, middle = a - 15, far_above, (above, 32 * (a - 15), 32)
        if far is None:
            return joined((ill_below, 16 * i, 16), middle, (ill_above, 16 * i, 16))
        if 0 <= i < 6:
            return joined((far, 32 * i, 16), middle, (far, 32 * i + 16, 16))
        return padded(middle, 16)

    def field(k, a):
        if a < 6:
            i, far, middle = a - 1, far_below, (below, 224 + 192 * k + 32 * a, 32)
        elif a < 14:
            i, far, middle = a - 6, None, (own, 256 * (k + 1) + 32 * (a - 6), 32)
        else:
            i, far, middle = a - 14, far_above, (above, 224 + 192 * k + 32 * (a - 14), 32)
        if far is None:
            at = 128 + 64 * k + 8 * i
            return joined((ill_below, at, 8), middle, (ill_above, at, 8))
        if 0 <= i < 5:
            at = 192 + 80 * k + 16 * i
            return joined((far, at, 8), middle, (far, at + 8, 8))
        return padded(middle, 8)

    def mid(k, m):
        if 1 < m < 6:
            at = 448 + 32 * k + 8 * (m - 2)
            middle = (own, 1536 + 64 * k + 16 * (m - 2), 16)
            return joined((ill_below, at, 8), middle, (ill_above, at, 8))
        near, i = (below, 2 * m + 2) if m < 2 else (above, 2 * m - 12)
        at = 224 + 192 * (k + 1) + 32 * i
        far, corner = (far_below, 16 * m) if m < 2 else (far_above, 16 * (m - 6))
        corner += 592 + 32 * k
        middle = 0.125 * pair_sums(near[pl.ds(at, 32), :] + near[pl.ds(at + 32, 32), :])
        return jnp.concatenate([far[pl.ds(corner, 8), :], middle, far[pl.ds(corner + 8, 8), :]], axis=0)

    return value, field, mid


def keep_kernel(own, ill_below, ill_above, below, above, far_below, far_above, out, keep_ref, mid_ref):
    _, field, mid = assemblers(own, ill_below, ill_above, below, above, far_below, far_above)
    outflow = spread(out[...], 48)
    for a in range(12):
        here = pl.ds(48 * a, 48)
        total = DISCOUNT + outflow
        for k in range(5):
            x = field(k, a + 4)
            keep_ref[k, here, :] = x
            if k:
                total = total + x
        keep_ref[5, here, :] = OMEGA / total
    outflow = spread(out[...], 32)
    for m in range(8):
        here = pl.ds(32 * m, 32)
        total = DISCOUNT + outflow
        for k in range(4):
            x = mid(k, m)
            mid_ref[k, here, :] = x
            total = total + x
        mid_ref[4, here, :] = OMEGA / total


def fine_kernel(
    own, ill_below, ill_above, below, above, far_below, far_above, jhi, jlo, out,
    val_ref, rhs_ref, lo_ref, hi_ref, v0, v1, v2, inc, f,
):
    value, field, _ = assemblers(own, ill_below, ill_above, below, above, far_below, far_above)
    for a in range(22):
        v0[pl.ds(64 * a, 64), :] = value(a)
    outflow = spread(out[...], 48)
    for a in range(20):
        here = pl.ds(48 * a, 48)
        total = DISCOUNT + outflow
        for k in range(5):
            x = field(k, a)
            f[k, here, :] = x
            if k:
                total = total + x
        f[5, here, :] = OMEGA / total

    def rest(a):
        here = pl.ds(48 * a, 48)
        return f[0, here, :], f[1, here, :], f[2, here, :], f[3, here, :], f[4, here, :]

    income(v0, inc, [(64, 64, 16 * 20)], jhi, jlo)
    for a in range(20):
        rhs, fa, ba, fb, bb = rest(a)
        center = row(v0, a + 1, 64)
        total = rhs + inc[pl.ds(64 * (a + 1) + 8, 48), :]
        total = total + fa * v0[pl.ds(64 * (a + 2) + 8, 48), :]
        total = total + ba * v0[pl.ds(64 * a + 8, 48), :]
        total = total + fb * later(center)[8:56] + bb * earlier(center)[8:56]
        here = pl.ds(48 * a, 48)
        v1[here, :] = (1.0 - OMEGA) * center[8:56] + f[5, here, :] * total

    def applied(src, a):
        rhs, fa, ba, fb, bb = rest(a)
        center = row(src, a, 48)
        total = rhs + row(inc, a, 48) + fa * row(src, a + 1, 48) + ba * row(src, a - 1, 48)
        return center, total + fb * later(center) + bb * earlier(center)

    income(v1, inc, [(48, 48, 12 * 18)], jhi, jlo)
    for a in range(1, 19):
        center, total = applied(v1, a)
        here = pl.ds(48 * a, 48)
        v2[here, :] = (1.0 - OMEGA) * center + f[5, here, :] * total
    income(v2, inc, [(96, 96, 12 * 16)], jhi, jlo)

    def residual(a):
        center, total = applied(v2, a)
        diag = DISCOUNT + outflow
        for x in rest(a)[1:]:
            diag = diag + x
        return (total - diag * center)[8:40]

    for m in range(8):
        coarse = 0.25 * pair_sums(residual(2 + 2 * m) + residual(3 + 2 * m))
        rhs_ref[pl.ds(16 * m, 16), :] = coarse
        lo_ref[pl.ds(8 * m, 8), :] = coarse[:8]
        hi_ref[pl.ds(8 * m, 8), :] = coarse[8:]
    for a in range(12):
        value = row(v2, a + 4, 48)[8:40]
        val_ref[pl.ds(32 * a, 32), :] = value
        lo_ref[pl.ds(64 + 8 * a, 8), :] = value[:8]
        hi_ref[pl.ds(64 + 8 * a, 8), :] = value[24:]


def widen_rhs(own, below, above, rhs_ref):
    for a in range(8):
        for i, piece in enumerate((below[pl.ds(8 * a, 8), :], row(own, a, 16), above[pl.ds(8 * a, 8), :])):
            rhs_ref[pl.ds(32 * a + (0, 8, 24)[i], piece.shape[0]), :] = piece


def widen_value(val, below, above, wide_ref):
    for a in range(12):
        ends = [src[pl.ds(64 + 8 * a, 8), :] for src in (below, above)]
        wide_ref[pl.ds(48 * a, 8), :] = ends[0]
        wide_ref[pl.ds(48 * a + 8, 32), :] = row(val, a, 32)
        wide_ref[pl.ds(48 * a + 40, 8), :] = ends[1]


def mid_kernel(own, below, above, mid, jhi, jlo, out, _, pay_ref, err_ref, rhs_ref, e0, e1, inc):
    widen_rhs(own, below, above, rhs_ref)
    e0[...] = mid[4] * rhs_ref[...]

    def applied(src, a):
        here = pl.ds(32 * a, 32)
        center = src[here, :]
        total = rhs_ref[here, :] + inc[here, :]
        total = total + mid[0, here, :] * row(src, a + 1, 32)
        total = total + mid[1, here, :] * row(src, a - 1, 32)
        total = total + mid[2, here, :] * later(center)
        total = total + mid[3, here, :] * earlier(center)
        return center, total

    income(e0, inc, [(32, 32, 8 * 6)], jhi, jlo)
    for a in range(1, 7):
        center, total = applied(e0, a)
        here = pl.ds(32 * a, 32)
        e1[here, :] = (1.0 - OMEGA) * center + mid[4, here, :] * total
    income(e1, inc, [(64, 64, 8 * 4)], jhi, jlo)
    outflow = spread(out[...], 32)

    def residual(a):
        center, total = applied(e1, a)
        here = pl.ds(32 * a, 32)
        diag = DISCOUNT + outflow
        for k in range(4):
            diag = diag + mid[k, here, :]
        return (total - diag * center)[8:24]

    for m in range(2):
        pay_ref[pl.ds(8 * m, 8), :] = 0.25 * pair_sums(residual(2 + 2 * m) + residual(3 + 2 * m))
    for a in range(6):
        err_ref[pl.ds(16 * a, 16), :] = e1[pl.ds(32 * (a + 1) + 8, 16), :]
    pay_ref[16:48, :] = err_ref[32:64, :]


def solve_lines(target, weight, carry, link, middle, y, x_ref, offset):
    count = y.shape[0] // TILE
    half = count // 2
    top = bottom = None
    for i in range(half):
        j = count - 1 - i
        t = weight(i) * target(i)
        u = weight(j) * target(j)
        top = t if i == 0 else t + carry(i) * top
        bottom = u if i == 0 else u + carry(j) * bottom
        if i < half - 1:
            y[pl.ds(TILE * i, TILE), :] = top
            y[pl.ds(TILE * j, TILE), :] = bottom
    head = (top + link(half - 1) * bottom) * middle
    tail = bottom + link(half) * head
    for i in range(half - 1, -1, -1):
        j = count - 1 - i
        if i < half - 1:
            head = row(y, i, TILE) + link(i) * head
            tail = row(y, j, TILE) + link(j) * tail
        x_ref[pl.ds(offset + TILE * i, TILE), :] = head
        x_ref[pl.ds(offset + TILE * j, TILE), :] = tail


def send_lines(e, lo_ref, hi_ref):
    pairs = e[...].reshape(-1, 2, TILE, LANES)
    first, second = pairs[:, 0], pairs[:, 1]
    mask = first_half(first.shape)
    lo_ref[...] = jnp.where(mask, first, pltpu.roll(second, Z, 1)).reshape(-1, LANES)
    hi_ref[...] = jnp.where(mask, pltpu.roll(first, Z, 1), second).reshape(-1, LANES)


def factor_kernel(gathered, out, fac_ref, middle_ref):
    count = fac_ref.shape[1] // TILE

    def part(k, a):
        return gathered[pl.ds(64 * (a // 2) + 16 * k + 8 * (a % 2), TILE), :]

    outflow = DISCOUNT + out[...]
    gaps = [None, None]
    links = [None, None]
    for i in range(count // 2):
        for side, a in ((0, i), (1, count - 1 - i)):
            here = pl.ds(TILE * a, TILE)
            inner, outer = (part(0, a), part(1, a)) if side == 0 else (part(1, a), part(0, a))
            fb, bb = part(2, a), part(3, a)
            slack = outflow + fb + bb
            slack = slack + (outer if i == 0 else outer * gaps[side])
            weight = 1.0 / (slack + inner)
            links[side] = inner * weight
            gaps[side] = slack * weight
            fac_ref[0, here, :] = fb
            fac_ref[1, here, :] = bb
            fac_ref[2, here, :] = weight
            fac_ref[3, here, :] = outer * weight
            fac_ref[4, here, :] = links[side]
    middle_ref[...] = 1.0 / (gaps[0] + links[0] * gaps[1])


def first_solve_kernel(gathered, fac, middle, e_ref, lo_ref, hi_ref, y):
    solve_lines(
        lambda a: gathered[pl.ds(48 * (a // 2) + 8 * (a % 2), TILE), :],
        lambda a: row(fac.at[2], a, TILE),
        lambda a: row(fac.at[3], a, TILE),
        lambda a: row(fac.at[4], a, TILE),
        middle[...], y, e_ref, 0,
    )
    send_lines(e_ref, lo_ref, hi_ref)


def local_target(e, rhs, fac, jhi, jlo, t_ref):
    income(e, t_ref, [(0, 0, e.shape[0] // Z)], jhi, jlo)
    other = swapped(e[...])
    mask = first_half(other.shape)
    t_ref[...] = t_ref[...] + rhs[...] + jnp.where(mask, fac[0], fac[1]) * other


def first_target_kernel(
    gathered, err, e, fac, jhi, jlo, rhs_mid, val, below, above,
    t_ref, rhs_ref, wide_ref, rhs_wide_ref, val_wide_ref,
):
    blocks = e.shape[0] // (2 * TILE)
    for i in range(blocks):
        rhs_ref[pl.ds(16 * i, 16), :] = gathered[pl.ds(48 * i, 16), :]
    local_target(e, rhs_ref, fac, jhi, jlo, t_ref)
    widen_rhs(rhs_mid, below, above, rhs_wide_ref)
    widen_value(val, below, above, val_wide_ref)
    here = lax.axis_index("liq")
    wide_ref[32:128, :] = err[...]
    for at, block, inside in ((0, here - 1, here > 0), (128, here + 1, here < blocks - 1)):
        block = jnp.minimum(jnp.maximum(block, 0), blocks - 1)
        start = pl.multiple_of(block * 48 + 16, 16)
        piece = gathered[pl.ds(start, 32), :]
        wide_ref[pl.ds(at, 32), :] = jnp.where(inside, piece, jnp.zeros_like(piece))


def swept(t, fac, middle, below, above, y, x_ref, offset):
    mask = first_half((TILE, LANES))

    def target(a):
        low_side, high_side = row(below, a // 2, TILE), row(above, a // 2, TILE)
        if a % 2:
            low_side = pltpu.roll(low_side, Z, 0)
        else:
            high_side = pltpu.roll(high_side, Z, 0)
        near = jnp.where(mask, low_side, high_side)
        coupling = jnp.where(mask, row(fac.at[1], a, TILE), row(fac.at[0], a, TILE))
        return row(t, a, TILE) + coupling * near

    solve_lines(
        target,
        lambda a: row(fac.at[2], a, TILE),
        lambda a: row(fac.at[3], a, TILE),
        lambda a: row(fac.at[4], a, TILE),
        middle[...], y, x_ref, offset,
    )


def sweep_kernel(t, fac, middle, below, above, e_ref, lo_ref, hi_ref, y):
    swept(t, fac, middle, below, above, y, e_ref, 0)
    send_lines(e_ref, lo_ref, hi_ref)


def last_sweep_kernel(t, fac, middle, below, above, err, sum_ref, y, x):
    edge = 2 * TILE
    x[0:edge, :] = jnp.zeros((edge, LANES), F32)
    x[pl.ds(x.shape[0] - edge, edge), :] = jnp.zeros((edge, LANES), F32)
    swept(t, fac, middle, below, above, y, x, edge)
    start = lax.axis_index("liq") * 2 * TILE
    for i in range(6):
        low = x[pl.ds(pl.multiple_of(start + i * TILE, TILE), TILE), :]
        fill = doubled(low)
        for m in (2 * i - 1, 2 * i):
            if 0 <= m < 10:
                sum_ref[pl.ds(16 * m, 16), :] = err[pl.ds(16 * m, 16), :] + fill


def last_kernel(
    own, below, above, mid, rhs_mid, fine, val, jhi, jlo, out_ref, ev, e1, e2, v0, v1, v2, inc
):
    for a in range(10):
        for i, src in enumerate((below, own, above)):
            ev[pl.ds(48 * a + 16 * i, 16), :] = src[pl.ds(16 * a, 16), :]

    income(ev, inc, [(48 * (a + 1) + 8, 32 * a, 8) for a in range(8)], jhi, jlo)
    for a in range(8):
        here = pl.ds(32 * a, 32)
        center = row(ev, a + 1, 48)
        total = rhs_mid[here, :] + inc[here, :]
        total = total + mid[0, here, :] * ev[pl.ds(48 * (a + 2) + 8, 32), :]
        total = total + mid[1, here, :] * ev[pl.ds(48 * a + 8, 32), :]
        total = total + mid[2, here, :] * later(center)[8:40]
        total = total + mid[3, here, :] * earlier(center)[8:40]
        e1[here, :] = (1.0 - OMEGA) * center[8:40] + mid[4, here, :] * total

    income(e1, inc, [(32, 32, 8 * 6)], jhi, jlo)
    for a in range(1, 7):
        here = pl.ds(32 * a, 32)
        center = e1[here, :]
        total = rhs_mid[here, :] + inc[here, :]
        total = total + mid[0, here, :] * row(e1, a + 1, 32)
        total = total + mid[1, here, :] * row(e1, a - 1, 32)
        total = total + mid[2, here, :] * later(center)
        total = total + mid[3, here, :] * earlier(center)
        error = (1.0 - OMEGA) * center + mid[4, here, :] * total
        fill = doubled(error)[8:56]
        for f in (2 * a - 2, 2 * a - 1):
            v0[pl.ds(48 * f, 48), :] = row(val, f, 48) + fill

    def sweep(src, dst, begin, end):
        income(src, inc, [(48 * begin, 48 * begin, 12 * (end - begin))], jhi, jlo)
        for a in range(begin, end):
            here = pl.ds(48 * a, 48)
            center = src[here, :]
            total = fine[0, here, :] + inc[here, :]
            total = total + fine[1, here, :] * row(src, a + 1, 48)
            total = total + fine[2, here, :] * row(src, a - 1, 48)
            total = total + fine[3, here, :] * later(center)
            total = total + fine[4, here, :] * earlier(center)
            dst[here, :] = (1.0 - OMEGA) * center + fine[5, here, :] * total

    sweep(v0, v1, 1, 11)
    sweep(v1, v2, 2, 10)
    for a in range(8):
        for c in range(Z):
            piece = v2[pl.ds(48 * (a + 2) + 8 + c, 8, stride=Z), :]
            out_ref[a, :, c * LANES : (c + 1) * LANES] = piece


def call(kernel, args, outs, scratch=(), flops=0, places=(), limit=24):
    outs = [x if isinstance(x, jax.ShapeDtypeStruct) else jax.ShapeDtypeStruct(x, F32) for x in outs]
    moved = sum(x.size * x.dtype.itemsize for x in (*args, *outs))
    kinds = list(places) + [pltpu.VMEM] * (len(args) - len(places))
    return pl.pallas_call(
        kernel,
        out_shape=outs,
        in_specs=[pl.BlockSpec(memory_space=kind) for kind in kinds],
        out_specs=[pl.BlockSpec(memory_space=pltpu.VMEM)] * len(outs),
        scratch_shapes=[pltpu.VMEM(s, F32) if isinstance(s, tuple) else s for s in scratch],
        compiler_params=pltpu.CompilerParams(vmem_limit_bytes=limit * 2**20),
        cost_estimate=pl.CostEstimate(flops=flops, bytes_accessed=moved, transcendentals=0),
    )(*args)


def neighbours(lo, hi, axis):
    count = lax.axis_size(axis)
    below = lax.ppermute(hi, axis, [(i, i + 1) for i in range(count - 1)])
    above = lax.ppermute(lo, axis, [(i + 1, i) for i in range(count - 1)])
    return below, above


def body(right_side, value_guess, speed_liq, speed_ill, flag_liq, flag_ill, jump_rates):
    nz = jump_rates.shape[0]
    dot_flops = 2 * 3 * nz * nz
    inputs = (right_side, value_guess, speed_liq, speed_ill, flag_liq, flag_ill)
    buffers = [pltpu.VMEM(x.shape, x.dtype) for x in inputs]
    sems = pltpu.SemaphoreType.DMA((6,))
    lo, hi, up, down, copies = call(
        pack_kernel,
        inputs,
        [(576, LANES)] * 2 + [(1184, LANES)] * 2 + [(64 * lax.axis_size("liq"), LANES)],
        buffers + [(1792, LANES), sems],
        places=[pltpu.HBM] * 6,
        limit=57,
    )
    ill_below, ill_above = neighbours(lo, hi, "ill")
    below, above = neighbours(down, up, "liq")
    coefs = lax.all_to_all(copies, "liq", 0, 0, tiled=True)
    rates = jax.ShapeDtypeStruct((nz, nz), BF16)
    (own,) = call(
        own_kernel, inputs, [(1792, LANES)], buffers + [sems], places=[pltpu.HBM] * 6, limit=57
    )
    jhi, jlo, out, own = call(
        rates_kernel, (jump_rates, own), [rates, rates, (TILE, LANES), own.shape]
    )
    up, down = call(corner_kernel, (ill_below, ill_above), [(720, LANES)] * 2)
    far_below, far_above = neighbours(down, up, "liq")
    pieces = (own, ill_below, ill_above, below, above, far_below, far_above)
    value, rhs_mid, lo, hi = call(
        fine_kernel,
        (*pieces, jhi, jlo, out),
        [(384, LANES), (128, LANES), (160, LANES), (160, LANES)],
        [(1408, LANES), (960, LANES), (960, LANES), (1408, LANES), (6, 960, LANES)],
        flops=dot_flops * 730,
    )
    mid_below, mid_above = neighbours(lo, hi, "ill")
    fine, mid = call(keep_kernel, (*pieces, out), [(6, 576, LANES), (5, 256, LANES)])
    lines = coefs.shape[0] // 4
    line, message = (lines, LANES), (lines // 2, LANES)
    fac, middle = call(factor_kernel, (coefs, out), [(5, *line), (TILE, LANES)])
    payload, err = call(
        mid_kernel,
        (rhs_mid, mid_below, mid_above, mid, jhi, jlo, out, middle),
        [(48, LANES), (96, LANES)],
        [(256, LANES)] * 4,
        flops=dot_flops * 80,
    )
    gathered = lax.all_gather(payload, "liq", axis=0, tiled=True)
    e, lo, hi = call(
        first_solve_kernel, (gathered, fac, middle), [line, message, message], [line]
    )
    for step in range(SWEEPS - 1):
        below, above = neighbours(lo, hi, "ill")
        flops = dot_flops * lines // Z
        if step == 0:
            target, rhs, err, rhs_mid, value = call(
                first_target_kernel,
                (gathered, err, e, fac, jhi, jlo, rhs_mid, value, mid_below, mid_above),
                [line, line, (160, LANES), (256, LANES), (576, LANES)],
                flops=flops,
            )
        else:
            (target,) = call(local_target, (e, rhs, fac, jhi, jlo), [line], flops=flops)
        if step < SWEEPS - 2:
            e, lo, hi = call(
                sweep_kernel, (target, fac, middle, below, above), [line, message, message], [line]
            )
    (total,) = call(
        last_sweep_kernel,
        (target, fac, middle, below, above, err),
        [(160, LANES)],
        [line, (lines + 4 * TILE, LANES)],
    )
    below, above = neighbours(total, total, "ill")
    (result,) = call(
        last_kernel,
        (total, below, above, mid, rhs_mid, fine, value, jhi, jlo),
        [right_side.shape],
        [(480, LANES), (256, LANES), (256, LANES)] + [(576, LANES)] * 4,
        flops=dot_flops * 330,
    )
    return result


def solution(mesh):
    block = P("liq", "ill", None)
    return jax.shard_map(
        body, mesh=mesh, in_specs=(block,) * 6 + (P(),), out_specs=block, check_vma=False
    )
```

```python
import functools

import jax
import jax.numpy as jnp
from jax import lax
from jax.experimental import pallas as pl
from jax.experimental.pallas import tpu as pltpu
from jax.sharding import PartitionSpec as P

SWEEPS = 4
OMEGA = 0.8
DISCOUNT = 0.05
LANES = 128
F32 = jnp.float32
BF16 = jnp.bfloat16

Z = 4
TILE = 8


def first_half(shape):
    return lax.broadcasted_iota(jnp.int32, shape, len(shape) - 2) % TILE < Z


def swapped(x):
    return pltpu.roll(x.reshape(-1, TILE, LANES), Z, 1).reshape(x.shape)


def later(x):
    return pltpu.roll(x, x.shape[0] - Z, 0)


def earlier(x):
    return pltpu.roll(x, Z, 0)


def pair_sums(x):
    total = x + swapped(x)
    total = total.reshape(-1, 2, TILE, LANES)
    first, second = total[:, 0], total[:, 1]
    return jnp.where(first_half(first.shape), first, second).reshape(-1, LANES)


def doubled(x):
    other = swapped(x).reshape(-1, 1, TILE, LANES)
    x = x.reshape(-1, 1, TILE, LANES)
    mask = first_half(x.shape)
    pair = jnp.concatenate([jnp.where(mask, x, other), jnp.where(mask, other, x)], axis=1)
    return pair.reshape(-1, LANES)


def spread(outflow, rows):
    return jnp.concatenate([outflow] * (rows // TILE), axis=0)


def row(ref, a, width):
    return ref[pl.ds(a * width, width), :]


def product(wide, jhi_ref, jlo_ref):
    high = wide.astype(BF16)
    rest = (wide - high.astype(F32)).astype(BF16)
    dot = functools.partial(jnp.dot, preferred_element_type=F32)
    count = wide.shape[0]
    both = dot(jnp.concatenate([high, rest], axis=0), jhi_ref[...])
    return both[:count] + (both[count:] + dot(high, jlo_ref[...]))


def income(src, dst, pieces, jhi_ref, jlo_ref):
    wide = jnp.concatenate(
        [
            jnp.concatenate([src[pl.ds(s + c, n, stride=Z), :] for s, _, n in pieces], axis=0)
            for c in range(Z)
        ],
        axis=1,
    )
    result = product(wide, jhi_ref, jlo_ref)
    at = 0
    for _, d, n in pieces:
        for c in range(Z):
            dst[pl.ds(d + c, n, stride=Z), :] = result[at : at + n, c * LANES : (c + 1) * LANES]
        at += n


def rates_kernel(j_ref, own, jhi_ref, jlo_ref, out_ref, own_ref):
    own_ref[...] = own[...]
    rates = j_ref[...]
    high = rates.astype(BF16)
    jhi_ref[...] = high
    jlo_ref[...] = (rates - high.astype(F32)).astype(BF16)
    total = jnp.sum(rates, axis=0, keepdims=True)
    for c in range(Z):
        piece = total[:, c * LANES : (c + 1) * LANES]
        out_ref[c : c + 1, :] = piece
        out_ref[c + Z : c + Z + 1, :] = piece


def unpack(sources, buffers, own_ref, sems):
    copies = [
        pltpu.make_async_copy(src, dst, sems.at[i])
        for i, (src, dst) in enumerate(zip(sources, buffers))
    ]
    for copy in copies:
        copy.start()
    rhs, value, speed_a, speed_b, flag_a, flag_b = buffers

    def put(start, x):
        for c in range(Z):
            own_ref[pl.ds(start + c, 8, stride=Z), :] = x[:, c * LANES : (c + 1) * LANES]

    for copy in copies:
        copy.wait()
    for a in range(8):
        put(32 * a, value[a])
        put(256 + 32 * a, rhs[a])
        for k, speed, flag in ((2, speed_a, flag_a), (4, speed_b, flag_b)):
            up = flag[a].astype(F32)
            put(256 * k + 32 * a, speed[a] * up)
            put(256 * (k + 1) + 32 * a, speed[a] * (1.0 - up))
    for k in range(4):
        for m in range(4):
            at = 256 * (k + 2) + 64 * m
            mid = 0.125 * pair_sums(own_ref[pl.ds(at, 32), :] + own_ref[pl.ds(at + 32, 32), :])
            own_ref[pl.ds(1536 + 64 * k + 16 * m, 16), :] = mid


def pack_kernel(*refs):
    sources, outs, buffers = refs[:6], refs[6:11], refs[11:17]
    lo_ref, hi_ref, up_ref, down_ref, low_ref = outs
    own_ref, sems = refs[17:]
    unpack(sources, buffers, own_ref, sems)
    for k in range(4):
        for m in range(4):
            mid = own_ref[pl.ds(1536 + 64 * k + 16 * m, 16), :]
            lo_ref[pl.ds(448 + 32 * k + 8 * m, 8), :] = mid[:8]
            hi_ref[pl.ds(448 + 32 * k + 8 * m, 8), :] = mid[8:]
    for a in range(8):
        lo_ref[pl.ds(16 * a, 16), :] = own_ref[pl.ds(32 * a, 16), :]
        hi_ref[pl.ds(16 * a, 16), :] = own_ref[pl.ds(32 * a + 16, 16), :]
        for k in range(5):
            at = 256 * (k + 1) + 32 * a
            lo_ref[pl.ds(128 + 64 * k + 8 * a, 8), :] = own_ref[pl.ds(at, 8), :]
            hi_ref[pl.ds(128 + 64 * k + 8 * a, 8), :] = own_ref[pl.ds(at + 24, 8), :]
    up_ref[0:224, :] = own_ref[32:256, :]
    down_ref[0:224, :] = own_ref[0:224, :]
    for k in range(5):
        here = pl.ds(224 + 192 * k, 192)
        up_ref[here, :] = own_ref[pl.ds(256 * (k + 1) + 64, 192), :]
        down_ref[here, :] = own_ref[pl.ds(256 * (k + 1), 192), :]
    for k in range(4):
        for m in range(2):
            at = 1536 + 64 * k + 32 * m
            both = own_ref[pl.ds(at, 16), :] + own_ref[pl.ds(at + 16, 16), :]
            low_ref[pl.ds(16 * k + 8 * m, 8), :] = 0.125 * pair_sums(both)


def copies_kernel(low, _, all_ref):
    piece = low[...]
    for i in range(all_ref.shape[0] // 64):
        all_ref[pl.ds(64 * i, 64), :] = piece


def own_kernel(*refs):
    unpack(refs[:6], refs[7:13], refs[6], refs[13])


def corner_kernel(below, above, up_ref, down_ref):
    def put(out, at, src, width):
        out[pl.ds(at, width), :] = below[pl.ds(src, width), :]
        out[pl.ds(at + width, width), :] = above[pl.ds(src, width), :]

    for out, shift in ((up_ref, 1), (down_ref, 0)):
        for i in range(6):
            put(out, 32 * i, 16 * (i + 2 * shift), 16)
        for k in range(5):
            for i in range(5):
                put(out, 192 + 80 * k + 16 * i, 128 + 64 * k + 8 * (i + 3 * shift), 8)
        for k in range(4):
            for i in range(2):
                put(out, 592 + 32 * k + 16 * i, 448 + 32 * k + 8 * (i + 2 * shift), 8)


def assemblers(own, ill_below, ill_above, below, above, far_below, far_above):
    def joined(first, middle, last):
        parts = [ref[pl.ds(at, width), :] for ref, at, width in (first, middle, last)]
        return jnp.concatenate(parts, axis=0)

    def padded(middle, width):
        edge = jnp.zeros((width, LANES), F32)
        ref, at, count = middle
        return jnp.concatenate([edge, ref[pl.ds(at, count), :], edge], axis=0)

    def value(a):
        if a < 7:
            i, far, middle = a - 1, far_below, (below, 32 * a, 32)
        elif a < 15:
            i, far, middle = a - 7, None, (own, 32 * (a - 7), 32)
        else:
            i, far, middle = a - 15, far_above, (above, 32 * (a - 15), 32)
        if far is None:
            return joined((ill_below, 16 * i, 16), middle, (ill_above, 16 * i, 16))
        if 0 <= i < 6:
            return joined((far, 32 * i, 16), middle, (far, 32 * i + 16, 16))
        return padded(middle, 16)

    def field(k, a):
        if a < 6:
            i, far, middle = a - 1, far_below, (below, 224 + 192 * k + 32 * a, 32)
        elif a < 14:
            i, far, middle = a - 6, None, (own, 256 * (k + 1) + 32 * (a - 6), 32)
        else:
            i, far, middle = a - 14, far_above, (above, 224 + 192 * k + 32 * (a - 14), 32)
        if far is None:
            at = 128 + 64 * k + 8 * i
            return joined((ill_below, at, 8), middle, (ill_above, at, 8))
        if 0 <= i < 5:
            at = 192 + 80 * k + 16 * i
            return joined((far, at, 8), middle, (far, at + 8, 8))
        return padded(middle, 8)

    def mid(k, m):
        if 1 < m < 6:
            at = 448 + 32 * k + 8 * (m - 2)
            middle = (own, 1536 + 64 * k + 16 * (m - 2), 16)
            return joined((ill_below, at, 8), middle, (ill_above, at, 8))
        near, i = (below, 2 * m + 2) if m < 2 else (above, 2 * m - 12)
        at = 224 + 192 * (k + 1) + 32 * i
        far, corner = (far_below, 16 * m) if m < 2 else (far_above, 16 * (m - 6))
        corner += 592 + 32 * k
        middle = 0.125 * pair_sums(near[pl.ds(at, 32), :] + near[pl.ds(at + 32, 32), :])
        return jnp.concatenate([far[pl.ds(corner, 8), :], middle, far[pl.ds(corner + 8, 8), :]], axis=0)

    return value, field, mid


def keep_kernel(own, ill_below, ill_above, below, above, far_below, far_above, out, keep_ref, mid_ref):
    _, field, mid = assemblers(own, ill_below, ill_above, below, above, far_below, far_above)
    outflow = spread(out[...], 48)
    for a in range(12):
        here = pl.ds(48 * a, 48)
        total = DISCOUNT + outflow
        for k in range(5):
            x = field(k, a + 4)
            keep_ref[k, here, :] = x
            if k:
                total = total + x
        keep_ref[5, here, :] = OMEGA / total
    outflow = spread(out[...], 32)
    for m in range(8):
        here = pl.ds(32 * m, 32)
        total = DISCOUNT + outflow
        for k in range(4):
            x = mid(k, m)
            mid_ref[k, here, :] = x
            total = total + x
        mid_ref[4, here, :] = OMEGA / total


def fine_kernel(
    own, ill_below, ill_above, below, above, far_below, far_above, jhi, jlo, out,
    val_ref, rhs_ref, lo_ref, hi_ref, v0, v1, v2, inc, f,
):
    value, field, _ = assemblers(own, ill_below, ill_above, below, above, far_below, far_above)
    for a in range(22):
        v0[pl.ds(64 * a, 64), :] = value(a)
    outflow = spread(out[...], 48)
    for a in range(20):
        here = pl.ds(48 * a, 48)
        total = DISCOUNT + outflow
        for k in range(5):
            x = field(k, a)
            f[k, here, :] = x
            if k:
                total = total + x
        f[5, here, :] = OMEGA / total

    def rest(a):
        here = pl.ds(48 * a, 48)
        return f[0, here, :], f[1, here, :], f[2, here, :], f[3, here, :], f[4, here, :]

    income(v0, inc, [(64, 64, 16 * 20)], jhi, jlo)
    for a in range(20):
        rhs, fa, ba, fb, bb = rest(a)
        center = row(v0, a + 1, 64)
        total = rhs + inc[pl.ds(64 * (a + 1) + 8, 48), :]
        total = total + fa * v0[pl.ds(64 * (a + 2) + 8, 48), :]
        total = total + ba * v0[pl.ds(64 * a + 8, 48), :]
        total = total + fb * later(center)[8:56] + bb * earlier(center)[8:56]
        here = pl.ds(48 * a, 48)
        v1[here, :] = (1.0 - OMEGA) * center[8:56] + f[5, here, :] * total

    def applied(src, a):
        rhs, fa, ba, fb, bb = rest(a)
        center = row(src, a, 48)
        total = rhs + row(inc, a, 48) + fa * row(src, a + 1, 48) + ba * row(src, a - 1, 48)
        return center, total + fb * later(center) + bb * earlier(center)

    income(v1, inc, [(48, 48, 12 * 18)], jhi, jlo)
    for a in range(1, 19):
        center, total = applied(v1, a)
        here = pl.ds(48 * a, 48)
        v2[here, :] = (1.0 - OMEGA) * center + f[5, here, :] * total
    income(v2, inc, [(96, 96, 12 * 16)], jhi, jlo)

    def residual(a):
        center, total = applied(v2, a)
        diag = DISCOUNT + outflow
        for x in rest(a)[1:]:
            diag = diag + x
        return (total - diag * center)[8:40]

    for m in range(8):
        coarse = 0.25 * pair_sums(residual(2 + 2 * m) + residual(3 + 2 * m))
        rhs_ref[pl.ds(16 * m, 16), :] = coarse
        lo_ref[pl.ds(8 * m, 8), :] = coarse[:8]
        hi_ref[pl.ds(8 * m, 8), :] = coarse[8:]
    for a in range(12):
        value = row(v2, a + 4, 48)[8:40]
        val_ref[pl.ds(32 * a, 32), :] = value
        lo_ref[pl.ds(64 + 8 * a, 8), :] = value[:8]
        hi_ref[pl.ds(64 + 8 * a, 8), :] = value[24:]


def widen_rhs(own, below, above, rhs_ref):
    for a in range(8):
        for i, piece in enumerate((below[pl.ds(8 * a, 8), :], row(own, a, 16), above[pl.ds(8 * a, 8), :])):
            rhs_ref[pl.ds(32 * a + (0, 8, 24)[i], piece.shape[0]), :] = piece


def widen_value(val, below, above, wide_ref):
    for a in range(12):
        ends = [src[pl.ds(64 + 8 * a, 8), :] for src in (below, above)]
        wide_ref[pl.ds(48 * a, 8), :] = ends[0]
        wide_ref[pl.ds(48 * a + 8, 32), :] = row(val, a, 32)
        wide_ref[pl.ds(48 * a + 40, 8), :] = ends[1]


def mid_kernel(own, below, above, mid, jhi, jlo, out, _, pay_ref, err_ref, rhs_ref, e0, e1, inc):
    widen_rhs(own, below, above, rhs_ref)
    e0[...] = mid[4] * rhs_ref[...]

    def applied(src, a):
        here = pl.ds(32 * a, 32)
        center = src[here, :]
        total = rhs_ref[here, :] + inc[here, :]
        total = total + mid[0, here, :] * row(src, a + 1, 32)
        total = total + mid[1, here, :] * row(src, a - 1, 32)
        total = total + mid[2, here, :] * later(center)
        total = total + mid[3, here, :] * earlier(center)
        return center, total

    income(e0, inc, [(32, 32, 8 * 6)], jhi, jlo)
    for a in range(1, 7):
        center, total = applied(e0, a)
        here = pl.ds(32 * a, 32)
        e1[here, :] = (1.0 - OMEGA) * center + mid[4, here, :] * total
    income(e1, inc, [(64, 64, 8 * 4)], jhi, jlo)
    outflow = spread(out[...], 32)

    def residual(a):
        center, total = applied(e1, a)
        here = pl.ds(32 * a, 32)
        diag = DISCOUNT + outflow
        for k in range(4):
            diag = diag + mid[k, here, :]
        return (total - diag * center)[8:24]

    low = [0.25 * pair_sums(residual(2 + 2 * m) + residual(3 + 2 * m)) for m in range(2)]
    for a in range(6):
        err_ref[pl.ds(16 * a, 16), :] = e1[pl.ds(32 * (a + 1) + 8, 16), :]
    piece = jnp.concatenate(low + [err_ref[32:64, :]], axis=0)
    for i in range(pay_ref.shape[0] // 48):
        pay_ref[pl.ds(48 * i, 48), :] = piece


def solve_lines(target, weight, carry, link, middle, y, x_ref, offset):
    count = y.shape[0] // TILE
    half = count // 2
    top = bottom = None
    for i in range(half):
        j = count - 1 - i
        t = weight(i) * target(i)
        u = weight(j) * target(j)
        top = t if i == 0 else t + carry(i) * top
        bottom = u if i == 0 else u + carry(j) * bottom
        if i < half - 1:
            y[pl.ds(TILE * i, TILE), :] = top
            y[pl.ds(TILE * j, TILE), :] = bottom
    head = (top + link(half - 1) * bottom) * middle
    tail = bottom + link(half) * head
    for i in range(half - 1, -1, -1):
        j = count - 1 - i
        if i < half - 1:
            head = row(y, i, TILE) + link(i) * head
            tail = row(y, j, TILE) + link(j) * tail
        x_ref[pl.ds(offset + TILE * i, TILE), :] = head
        x_ref[pl.ds(offset + TILE * j, TILE), :] = tail


def send_lines(e, lo_ref, hi_ref):
    pairs = e[...].reshape(-1, 2, TILE, LANES)
    first, second = pairs[:, 0], pairs[:, 1]
    mask = first_half(first.shape)
    lo_ref[...] = jnp.where(mask, first, pltpu.roll(second, Z, 1)).reshape(-1, LANES)
    hi_ref[...] = jnp.where(mask, pltpu.roll(first, Z, 1), second).reshape(-1, LANES)


def factor_kernel(gathered, out, fac_ref, middle_ref):
    count = fac_ref.shape[1] // TILE

    def part(k, a):
        return gathered[pl.ds(64 * (a // 2) + 16 * k + 8 * (a % 2), TILE), :]

    outflow = DISCOUNT + out[...]
    gaps = [None, None]
    links = [None, None]
    for i in range(count // 2):
        for side, a in ((0, i), (1, count - 1 - i)):
            here = pl.ds(TILE * a, TILE)
            inner, outer = (part(0, a), part(1, a)) if side == 0 else (part(1, a), part(0, a))
            fb, bb = part(2, a), part(3, a)
            slack = outflow + fb + bb
            slack = slack + (outer if i == 0 else outer * gaps[side])
            weight = 1.0 / (slack + inner)
            links[side] = inner * weight
            gaps[side] = slack * weight
            fac_ref[0, here, :] = fb
            fac_ref[1, here, :] = bb
            fac_ref[2, here, :] = weight
            fac_ref[3, here, :] = outer * weight
            fac_ref[4, here, :] = links[side]
    middle_ref[...] = 1.0 / (gaps[0] + links[0] * gaps[1])


def first_solve_kernel(gathered, fac, middle, e_ref, lo_ref, hi_ref, y):
    solve_lines(
        lambda a: gathered[pl.ds(48 * (a // 2) + 8 * (a % 2), TILE), :],
        lambda a: row(fac.at[2], a, TILE),
        lambda a: row(fac.at[3], a, TILE),
        lambda a: row(fac.at[4], a, TILE),
        middle[...], y, e_ref, 0,
    )
    send_lines(e_ref, lo_ref, hi_ref)


def local_target(e, rhs, fac, jhi, jlo, t_ref):
    income(e, t_ref, [(0, 0, e.shape[0] // Z)], jhi, jlo)
    other = swapped(e[...])
    mask = first_half(other.shape)
    t_ref[...] = t_ref[...] + rhs[...] + jnp.where(mask, fac[0], fac[1]) * other


def first_target_kernel(
    gathered, err, e, fac, jhi, jlo, rhs_mid, val, below, above,
    t_ref, rhs_ref, wide_ref, rhs_wide_ref, val_wide_ref,
):
    blocks = e.shape[0] // (2 * TILE)
    for i in range(blocks):
        rhs_ref[pl.ds(16 * i, 16), :] = gathered[pl.ds(48 * i, 16), :]
    local_target(e, rhs_ref, fac, jhi, jlo, t_ref)
    widen_rhs(rhs_mid, below, above, rhs_wide_ref)
    widen_value(val, below, above, val_wide_ref)
    here = lax.axis_index("liq")
    wide_ref[32:128, :] = err[...]
    for at, block, inside in ((0, here - 1, here > 0), (128, here + 1, here < blocks - 1)):
        block = jnp.minimum(jnp.maximum(block, 0), blocks - 1)
        start = pl.multiple_of(block * 48 + 16, 16)
        piece = gathered[pl.ds(start, 32), :]
        wide_ref[pl.ds(at, 32), :] = jnp.where(inside, piece, jnp.zeros_like(piece))


def swept(t, fac, middle, below, above, y, x_ref, offset):
    mask = first_half((TILE, LANES))

    def target(a):
        low_side, high_side = row(below, a // 2, TILE), row(above, a // 2, TILE)
        if a % 2:
            low_side = pltpu.roll(low_side, Z, 0)
        else:
            high_side = pltpu.roll(high_side, Z, 0)
        near = jnp.where(mask, low_side, high_side)
        coupling = jnp.where(mask, row(fac.at[1], a, TILE), row(fac.at[0], a, TILE))
        return row(t, a, TILE) + coupling * near

    solve_lines(
        target,
        lambda a: row(fac.at[2], a, TILE),
        lambda a: row(fac.at[3], a, TILE),
        lambda a: row(fac.at[4], a, TILE),
        middle[...], y, x_ref, offset,
    )


def sweep_kernel(t, fac, middle, below, above, e_ref, lo_ref, hi_ref, y):
    swept(t, fac, middle, below, above, y, e_ref, 0)
    send_lines(e_ref, lo_ref, hi_ref)


def last_sweep_kernel(t, fac, middle, below, above, err, sum_ref, y, x):
    edge = 2 * TILE
    x[0:edge, :] = jnp.zeros((edge, LANES), F32)
    x[pl.ds(x.shape[0] - edge, edge), :] = jnp.zeros((edge, LANES), F32)
    swept(t, fac, middle, below, above, y, x, edge)
    start = lax.axis_index("liq") * 2 * TILE
    for i in range(6):
        low = x[pl.ds(pl.multiple_of(start + i * TILE, TILE), TILE), :]
        fill = doubled(low)
        for m in (2 * i - 1, 2 * i):
            if 0 <= m < 10:
                sum_ref[pl.ds(16 * m, 16), :] = err[pl.ds(16 * m, 16), :] + fill


def last_kernel(
    own, below, above, mid, rhs_mid, fine, val, jhi, jlo, out_ref, ev, e1, e2, v0, v1, v2, inc
):
    for a in range(10):
        for i, src in enumerate((below, own, above)):
            ev[pl.ds(48 * a + 16 * i, 16), :] = src[pl.ds(16 * a, 16), :]

    income(ev, inc, [(48 * (a + 1) + 8, 32 * a, 8) for a in range(8)], jhi, jlo)
    for a in range(8):
        here = pl.ds(32 * a, 32)
        center = row(ev, a + 1, 48)
        total = rhs_mid[here, :] + inc[here, :]
        total = total + mid[0, here, :] * ev[pl.ds(48 * (a + 2) + 8, 32), :]
        total = total + mid[1, here, :] * ev[pl.ds(48 * a + 8, 32), :]
        total = total + mid[2, here, :] * later(center)[8:40]
        total = total + mid[3, here, :] * earlier(center)[8:40]
        e1[here, :] = (1.0 - OMEGA) * center[8:40] + mid[4, here, :] * total

    income(e1, inc, [(32, 32, 8 * 6)], jhi, jlo)
    for a in range(1, 7):
        here = pl.ds(32 * a, 32)
        center = e1[here, :]
        total = rhs_mid[here, :] + inc[here, :]
        total = total + mid[0, here, :] * row(e1, a + 1, 32)
        total = total + mid[1, here, :] * row(e1, a - 1, 32)
        total = total + mid[2, here, :] * later(center)
        total = total + mid[3, here, :] * earlier(center)
        error = (1.0 - OMEGA) * center + mid[4, here, :] * total
        fill = doubled(error)[8:56]
        for f in (2 * a - 2, 2 * a - 1):
            v0[pl.ds(48 * f, 48), :] = row(val, f, 48) + fill

    def sweep(src, dst, begin, end):
        income(src, inc, [(48 * begin, 48 * begin, 12 * (end - begin))], jhi, jlo)
        for a in range(begin, end):
            here = pl.ds(48 * a, 48)
            center = src[here, :]
            total = fine[0, here, :] + inc[here, :]
            total = total + fine[1, here, :] * row(src, a + 1, 48)
            total = total + fine[2, here, :] * row(src, a - 1, 48)
            total = total + fine[3, here, :] * later(center)
            total = total + fine[4, here, :] * earlier(center)
            dst[here, :] = (1.0 - OMEGA) * center + fine[5, here, :] * total

    sweep(v0, v1, 1, 11)
    sweep(v1, v2, 2, 10)
    for a in range(8):
        for c in range(Z):
            piece = v2[pl.ds(48 * (a + 2) + 8 + c, 8, stride=Z), :]
            out_ref[a, :, c * LANES : (c + 1) * LANES] = piece


def call(kernel, args, outs, scratch=(), flops=0, places=(), limit=24):
    outs = [x if isinstance(x, jax.ShapeDtypeStruct) else jax.ShapeDtypeStruct(x, F32) for x in outs]
    moved = sum(x.size * x.dtype.itemsize for x in (*args, *outs))
    kinds = list(places) + [pltpu.VMEM] * (len(args) - len(places))
    return pl.pallas_call(
        kernel,
        out_shape=outs,
        in_specs=[pl.BlockSpec(memory_space=kind) for kind in kinds],
        out_specs=[pl.BlockSpec(memory_space=pltpu.VMEM)] * len(outs),
        scratch_shapes=[pltpu.VMEM(s, F32) if isinstance(s, tuple) else s for s in scratch],
        compiler_params=pltpu.CompilerParams(vmem_limit_bytes=limit * 2**20),
        cost_estimate=pl.CostEstimate(flops=flops, bytes_accessed=moved, transcendentals=0),
    )(*args)


def neighbours(lo, hi, axis):
    count = lax.axis_size(axis)
    below = lax.ppermute(hi, axis, [(i, i + 1) for i in range(count - 1)])
    above = lax.ppermute(lo, axis, [(i + 1, i) for i in range(count - 1)])
    return below, above


def body(right_side, value_guess, speed_liq, speed_ill, flag_liq, flag_ill, jump_rates):
    nz = jump_rates.shape[0]
    dot_flops = 2 * 3 * nz * nz
    inputs = (right_side, value_guess, speed_liq, speed_ill, flag_liq, flag_ill)
    buffers = [pltpu.VMEM(x.shape, x.dtype) for x in inputs]
    sems = pltpu.SemaphoreType.DMA((6,))
    lo, hi, up, down, low = call(
        pack_kernel,
        inputs,
        [(576, LANES)] * 2 + [(1184, LANES)] * 2 + [(64, LANES)],
        buffers + [(1792, LANES), sems],
        places=[pltpu.HBM] * 6,
        limit=57,
    )
    ill_below, ill_above = neighbours(lo, hi, "ill")
    below, above = neighbours(down, up, "liq")
    rates = jax.ShapeDtypeStruct((nz, nz), BF16)
    (own,) = call(
        own_kernel, inputs, [(1792, LANES)], buffers + [sems], places=[pltpu.HBM] * 6, limit=57,
        flops=10**10,
    )
    jhi, jlo, out, own = call(
        rates_kernel, (jump_rates, own), [rates, rates, (TILE, LANES), own.shape]
    )
    up, down = call(corner_kernel, (ill_below, ill_above), [(720, LANES)] * 2)
    far_below, far_above = neighbours(down, up, "liq")
    (copies,) = call(copies_kernel, (low, above), [(64 * lax.axis_size("liq"), LANES)])
    coefs = lax.all_to_all(copies, "liq", 0, 0, tiled=True)
    pieces = (own, ill_below, ill_above, below, above, far_below, far_above)
    value, rhs_mid, lo, hi = call(
        fine_kernel,
        (*pieces, jhi, jlo, out),
        [(384, LANES), (128, LANES), (160, LANES), (160, LANES)],
        [(1408, LANES), (960, LANES), (960, LANES), (1408, LANES), (6, 960, LANES)],
        flops=dot_flops * 730,
    )
    mid_below, mid_above = neighbours(lo, hi, "ill")
    fine, mid = call(keep_kernel, (*pieces, out), [(6, 576, LANES), (5, 256, LANES)])
    lines = coefs.shape[0] // 4
    line, message = (lines, LANES), (lines // 2, LANES)
    fac, middle = call(factor_kernel, (coefs, out), [(5, *line), (TILE, LANES)])
    payload, err = call(
        mid_kernel,
        (rhs_mid, mid_below, mid_above, mid, jhi, jlo, out, middle),
        [(48 * lax.axis_size("liq"), LANES), (96, LANES)],
        [(256, LANES)] * 4,
        flops=dot_flops * 80,
    )
    gathered = lax.all_to_all(payload, "liq", 0, 0, tiled=True)
    e, lo, hi = call(
        first_solve_kernel, (gathered, fac, middle), [line, message, message], [line]
    )
    for step in range(SWEEPS - 1):
        below, above = neighbours(lo, hi, "ill")
        flops = dot_flops * lines // Z
        if step == 0:
            target, rhs, err, rhs_mid, value = call(
                first_target_kernel,
                (gathered, err, e, fac, jhi, jlo, rhs_mid, value, mid_below, mid_above),
                [line, line, (160, LANES), (256, LANES), (576, LANES)],
                flops=flops,
            )
        else:
            (target,) = call(local_target, (e, rhs, fac, jhi, jlo), [line], flops=flops)
        if step < SWEEPS - 2:
            e, lo, hi = call(
                sweep_kernel, (target, fac, middle, below, above), [line, message, message], [line]
            )
    (total,) = call(
        last_sweep_kernel,
        (target, fac, middle, below, above, err),
        [(160, LANES)],
        [line, (lines + 4 * TILE, LANES)],
    )
    below, above = neighbours(total, total, "ill")
    (result,) = call(
        last_kernel,
        (total, below, above, mid, rhs_mid, fine, value, jhi, jlo),
        [right_side.shape],
        [(480, LANES), (256, LANES), (256, LANES)] + [(576, LANES)] * 4,
        flops=dot_flops * 330,
    )
    return result


def solution(mesh):
    block = P("liq", "ill", None)
    return jax.shard_map(
        body, mesh=mesh, in_specs=(block,) * 6 + (P(),), out_specs=block, check_vma=False
    )
```

```python
import functools

import jax
import jax.numpy as jnp
from jax import lax
from jax.experimental import pallas as pl
from jax.experimental.pallas import tpu as pltpu
from jax.sharding import PartitionSpec as P

SWEEPS = 4
OMEGA = 0.8
DISCOUNT = 0.05
LANES = 128
F32 = jnp.float32
BF16 = jnp.bfloat16

Z = 4
TILE = 8


def first_half(shape):
    return lax.broadcasted_iota(jnp.int32, shape, len(shape) - 2) % TILE < Z


def swapped(x):
    return pltpu.roll(x.reshape(-1, TILE, LANES), Z, 1).reshape(x.shape)


def later(x):
    return pltpu.roll(x, x.shape[0] - Z, 0)


def earlier(x):
    return pltpu.roll(x, Z, 0)


def pair_sums(x):
    total = x + swapped(x)
    total = total.reshape(-1, 2, TILE, LANES)
    first, second = total[:, 0], total[:, 1]
    return jnp.where(first_half(first.shape), first, second).reshape(-1, LANES)


def doubled(x):
    other = swapped(x).reshape(-1, 1, TILE, LANES)
    x = x.reshape(-1, 1, TILE, LANES)
    mask = first_half(x.shape)
    pair = jnp.concatenate([jnp.where(mask, x, other), jnp.where(mask, other, x)], axis=1)
    return pair.reshape(-1, LANES)


def spread(outflow, rows):
    return jnp.concatenate([outflow] * (rows // TILE), axis=0)


def row(ref, a, width):
    return ref[pl.ds(a * width, width), :]


def product(wide, jhi_ref, jlo_ref):
    high = wide.astype(BF16)
    rest = (wide - high.astype(F32)).astype(BF16)
    dot = functools.partial(jnp.dot, preferred_element_type=F32)
    count = wide.shape[0]
    both = dot(jnp.concatenate([high, rest], axis=0), jhi_ref[...])
    return both[:count] + (both[count:] + dot(high, jlo_ref[...]))


def income(src, dst, pieces, jhi_ref, jlo_ref):
    wide = jnp.concatenate(
        [
            jnp.concatenate([src[pl.ds(s + c, n, stride=Z), :] for s, _, n in pieces], axis=0)
            for c in range(Z)
        ],
        axis=1,
    )
    result = product(wide, jhi_ref, jlo_ref)
    at = 0
    for _, d, n in pieces:
        for c in range(Z):
            dst[pl.ds(d + c, n, stride=Z), :] = result[at : at + n, c * LANES : (c + 1) * LANES]
        at += n


def rates_kernel(j_ref, own, jhi_ref, jlo_ref, out_ref, own_ref):
    own_ref[...] = own[...]
    rates = j_ref[...]
    high = rates.astype(BF16)
    jhi_ref[...] = high
    jlo_ref[...] = (rates - high.astype(F32)).astype(BF16)
    total = jnp.sum(rates, axis=0, keepdims=True)
    for c in range(Z):
        piece = total[:, c * LANES : (c + 1) * LANES]
        out_ref[c : c + 1, :] = piece
        out_ref[c + Z : c + Z + 1, :] = piece


def unpack(sources, buffers, own_ref, sems):
    copies = [
        pltpu.make_async_copy(src, dst, sems.at[i])
        for i, (src, dst) in enumerate(zip(sources, buffers))
    ]
    for copy in copies:
        copy.start()
    rhs, value, speed_a, speed_b, flag_a, flag_b = buffers

    def put(start, x):
        for c in range(Z):
            own_ref[pl.ds(start + c, 8, stride=Z), :] = x[:, c * LANES : (c + 1) * LANES]

    for copy in copies:
        copy.wait()
    for a in range(8):
        put(32 * a, value[a])
        put(256 + 32 * a, rhs[a])
        for k, speed, flag in ((2, speed_a, flag_a), (4, speed_b, flag_b)):
            up = flag[a].astype(F32)
            put(256 * k + 32 * a, speed[a] * up)
            put(256 * (k + 1) + 32 * a, speed[a] * (1.0 - up))
    for k in range(4):
        for m in range(4):
            at = 256 * (k + 2) + 64 * m
            mid = 0.125 * pair_sums(own_ref[pl.ds(at, 32), :] + own_ref[pl.ds(at + 32, 32), :])
            own_ref[pl.ds(1536 + 64 * k + 16 * m, 16), :] = mid


def pack_kernel(*refs):
    sources, outs, buffers = refs[:6], refs[6:11], refs[11:17]
    lo_ref, hi_ref, up_ref, down_ref, low_ref = outs
    own_ref, sems = refs[17:]
    unpack(sources, buffers, own_ref, sems)
    for k in range(4):
        for m in range(4):
            mid = own_ref[pl.ds(1536 + 64 * k + 16 * m, 16), :]
            lo_ref[pl.ds(448 + 32 * k + 8 * m, 8), :] = mid[:8]
            hi_ref[pl.ds(448 + 32 * k + 8 * m, 8), :] = mid[8:]
    for a in range(8):
        lo_ref[pl.ds(16 * a, 16), :] = own_ref[pl.ds(32 * a, 16), :]
        hi_ref[pl.ds(16 * a, 16), :] = own_ref[pl.ds(32 * a + 16, 16), :]
        for k in range(5):
            at = 256 * (k + 1) + 32 * a
            lo_ref[pl.ds(128 + 64 * k + 8 * a, 8), :] = own_ref[pl.ds(at, 8), :]
            hi_ref[pl.ds(128 + 64 * k + 8 * a, 8), :] = own_ref[pl.ds(at + 24, 8), :]
    up_ref[0:224, :] = own_ref[32:256, :]
    down_ref[0:224, :] = own_ref[0:224, :]
    for k in range(5):
        here = pl.ds(224 + 192 * k, 192)
        up_ref[here, :] = own_ref[pl.ds(256 * (k + 1) + 64, 192), :]
        down_ref[here, :] = own_ref[pl.ds(256 * (k + 1), 192), :]
    for k in range(4):
        for m in range(2):
            at = 1536 + 64 * k + 32 * m
            both = own_ref[pl.ds(at, 16), :] + own_ref[pl.ds(at + 16, 16), :]
            low_ref[pl.ds(16 * k + 8 * m, 8), :] = 0.125 * pair_sums(both)


def own_kernel(*refs):
    unpack(refs[:6], refs[7:13], refs[6], refs[13])


def corner_kernel(below, above, up_ref, down_ref):
    def put(out, at, src, width):
        out[pl.ds(at, width), :] = below[pl.ds(src, width), :]
        out[pl.ds(at + width, width), :] = above[pl.ds(src, width), :]

    for out, shift in ((up_ref, 1), (down_ref, 0)):
        for i in range(6):
            put(out, 32 * i, 16 * (i + 2 * shift), 16)
        for k in range(5):
            for i in range(5):
                put(out, 192 + 80 * k + 16 * i, 128 + 64 * k + 8 * (i + 3 * shift), 8)
        for k in range(4):
            for i in range(2):
                put(out, 592 + 32 * k + 16 * i, 448 + 32 * k + 8 * (i + 2 * shift), 8)


def assemblers(own, ill_below, ill_above, below, above, far_below, far_above):
    def joined(first, middle, last):
        parts = [ref[pl.ds(at, width), :] for ref, at, width in (first, middle, last)]
        return jnp.concatenate(parts, axis=0)

    def padded(middle, width):
        edge = jnp.zeros((width, LANES), F32)
        ref, at, count = middle
        return jnp.concatenate([edge, ref[pl.ds(at, count), :], edge], axis=0)

    def value(a):
        if a < 7:
            i, far, middle = a - 1, far_below, (below, 32 * a, 32)
        elif a < 15:
            i, far, middle = a - 7, None, (own, 32 * (a - 7), 32)
        else:
            i, far, middle = a - 15, far_above, (above, 32 * (a - 15), 32)
        if far is None:
            return joined((ill_below, 16 * i, 16), middle, (ill_above, 16 * i, 16))
        if 0 <= i < 6:
            return joined((far, 32 * i, 16), middle, (far, 32 * i + 16, 16))
        return padded(middle, 16)

    def field(k, a):
        if a < 6:
            i, far, middle = a - 1, far_below, (below, 224 + 192 * k + 32 * a, 32)
        elif a < 14:
            i, far, middle = a - 6, None, (own, 256 * (k + 1) + 32 * (a - 6), 32)
        else:
            i, far, middle = a - 14, far_above, (above, 224 + 192 * k + 32 * (a - 14), 32)
        if far is None:
            at = 128 + 64 * k + 8 * i
            return joined((ill_below, at, 8), middle, (ill_above, at, 8))
        if 0 <= i < 5:
            at = 192 + 80 * k + 16 * i
            return joined((far, at, 8), middle, (far, at + 8, 8))
        return padded(middle, 8)

    def mid(k, m):
        if 1 < m < 6:
            at = 448 + 32 * k + 8 * (m - 2)
            middle = (own, 1536 + 64 * k + 16 * (m - 2), 16)
            return joined((ill_below, at, 8), middle, (ill_above, at, 8))
        near, i = (below, 2 * m + 2) if m < 2 else (above, 2 * m - 12)
        at = 224 + 192 * (k + 1) + 32 * i
        far, corner = (far_below, 16 * m) if m < 2 else (far_above, 16 * (m - 6))
        corner += 592 + 32 * k
        middle = 0.125 * pair_sums(near[pl.ds(at, 32), :] + near[pl.ds(at + 32, 32), :])
        return jnp.concatenate([far[pl.ds(corner, 8), :], middle, far[pl.ds(corner + 8, 8), :]], axis=0)

    return value, field, mid


def keep_kernel(own, ill_below, ill_above, below, above, far_below, far_above, out, keep_ref, mid_ref):
    _, field, mid = assemblers(own, ill_below, ill_above, below, above, far_below, far_above)
    outflow = spread(out[...], 48)
    for a in range(12):
        here = pl.ds(48 * a, 48)
        total = DISCOUNT + outflow
        for k in range(5):
            x = field(k, a + 4)
            keep_ref[k, here, :] = x
            if k:
                total = total + x
        keep_ref[5, here, :] = OMEGA / total
    outflow = spread(out[...], 32)
    for m in range(8):
        here = pl.ds(32 * m, 32)
        total = DISCOUNT + outflow
        for k in range(4):
            x = mid(k, m)
            mid_ref[k, here, :] = x
            total = total + x
        mid_ref[4, here, :] = OMEGA / total


def fine_kernel(
    own, ill_below, ill_above, below, above, far_below, far_above, jhi, jlo, out,
    val_ref, rhs_ref, lo_ref, hi_ref, v0, v1, v2, inc, f,
):
    value, field, _ = assemblers(own, ill_below, ill_above, below, above, far_below, far_above)
    for a in range(22):
        v0[pl.ds(64 * a, 64), :] = value(a)
    outflow = spread(out[...], 48)
    for a in range(20):
        here = pl.ds(48 * a, 48)
        total = DISCOUNT + outflow
        for k in range(5):
            x = field(k, a)
            f[k, here, :] = x
            if k:
                total = total + x
        f[5, here, :] = OMEGA / total

    def rest(a):
        here = pl.ds(48 * a, 48)
        return f[0, here, :], f[1, here, :], f[2, here, :], f[3, here, :], f[4, here, :]

    income(v0, inc, [(64, 64, 16 * 20)], jhi, jlo)
    for a in range(20):
        rhs, fa, ba, fb, bb = rest(a)
        center = row(v0, a + 1, 64)
        total = rhs + inc[pl.ds(64 * (a + 1) + 8, 48), :]
        total = total + fa * v0[pl.ds(64 * (a + 2) + 8, 48), :]
        total = total + ba * v0[pl.ds(64 * a + 8, 48), :]
        total = total + fb * later(center)[8:56] + bb * earlier(center)[8:56]
        here = pl.ds(48 * a, 48)
        v1[here, :] = (1.0 - OMEGA) * center[8:56] + f[5, here, :] * total

    def applied(src, a):
        rhs, fa, ba, fb, bb = rest(a)
        center = row(src, a, 48)
        total = rhs + row(inc, a, 48) + fa * row(src, a + 1, 48) + ba * row(src, a - 1, 48)
        return center, total + fb * later(center) + bb * earlier(center)

    income(v1, inc, [(48, 48, 12 * 18)], jhi, jlo)
    for a in range(1, 19):
        center, total = applied(v1, a)
        here = pl.ds(48 * a, 48)
        v2[here, :] = (1.0 - OMEGA) * center + f[5, here, :] * total
    income(v2, inc, [(96, 96, 12 * 16)], jhi, jlo)

    def residual(a):
        center, total = applied(v2, a)
        diag = DISCOUNT + outflow
        for x in rest(a)[1:]:
            diag = diag + x
        return (total - diag * center)[8:40]

    for m in range(8):
        coarse = 0.25 * pair_sums(residual(2 + 2 * m) + residual(3 + 2 * m))
        rhs_ref[pl.ds(16 * m, 16), :] = coarse
        lo_ref[pl.ds(8 * m, 8), :] = coarse[:8]
        hi_ref[pl.ds(8 * m, 8), :] = coarse[8:]
    for a in range(12):
        value = row(v2, a + 4, 48)[8:40]
        val_ref[pl.ds(32 * a, 32), :] = value
        lo_ref[pl.ds(64 + 8 * a, 8), :] = value[:8]
        hi_ref[pl.ds(64 + 8 * a, 8), :] = value[24:]


def widen_rhs(own, below, above, rhs_ref):
    for a in range(8):
        for i, piece in enumerate((below[pl.ds(8 * a, 8), :], row(own, a, 16), above[pl.ds(8 * a, 8), :])):
            rhs_ref[pl.ds(32 * a + (0, 8, 24)[i], piece.shape[0]), :] = piece


def widen_value(val, below, above, wide_ref):
    for a in range(12):
        ends = [src[pl.ds(64 + 8 * a, 8), :] for src in (below, above)]
        wide_ref[pl.ds(48 * a, 8), :] = ends[0]
        wide_ref[pl.ds(48 * a + 8, 32), :] = row(val, a, 32)
        wide_ref[pl.ds(48 * a + 40, 8), :] = ends[1]


def mid_kernel(own, below, above, mid, jhi, jlo, out, coefs, pay_ref, err_ref, rhs_ref, e0, e1, inc):
    widen_rhs(own, below, above, rhs_ref)
    e0[...] = mid[4] * rhs_ref[...]

    def applied(src, a):
        here = pl.ds(32 * a, 32)
        center = src[here, :]
        total = rhs_ref[here, :] + inc[here, :]
        total = total + mid[0, here, :] * row(src, a + 1, 32)
        total = total + mid[1, here, :] * row(src, a - 1, 32)
        total = total + mid[2, here, :] * later(center)
        total = total + mid[3, here, :] * earlier(center)
        return center, total

    income(e0, inc, [(32, 32, 8 * 6)], jhi, jlo)
    for a in range(1, 7):
        center, total = applied(e0, a)
        here = pl.ds(32 * a, 32)
        e1[here, :] = (1.0 - OMEGA) * center + mid[4, here, :] * total
    income(e1, inc, [(64, 64, 8 * 4)], jhi, jlo)
    outflow = spread(out[...], 32)

    def residual(a):
        center, total = applied(e1, a)
        here = pl.ds(32 * a, 32)
        diag = DISCOUNT + outflow
        for k in range(4):
            diag = diag + mid[k, here, :]
        return (total - diag * center)[8:24]

    low = [0.25 * pair_sums(residual(2 + 2 * m) + residual(3 + 2 * m)) for m in range(2)]
    for a in range(6):
        err_ref[pl.ds(16 * a, 16), :] = e1[pl.ds(32 * (a + 1) + 8, 16), :]
    piece = jnp.concatenate(low + [err_ref[32:64, :], coefs[...]], axis=0)
    for i in range(pay_ref.shape[0] // 112):
        pay_ref[pl.ds(112 * i, 112), :] = piece


def solve_lines(target, weight, carry, link, middle, y, x_ref, offset):
    count = y.shape[0] // TILE
    half = count // 2
    top = bottom = None
    for i in range(half):
        j = count - 1 - i
        t = weight(i) * target(i)
        u = weight(j) * target(j)
        top = t if i == 0 else t + carry(i) * top
        bottom = u if i == 0 else u + carry(j) * bottom
        if i < half - 1:
            y[pl.ds(TILE * i, TILE), :] = top
            y[pl.ds(TILE * j, TILE), :] = bottom
    head = (top + link(half - 1) * bottom) * middle
    tail = bottom + link(half) * head
    for i in range(half - 1, -1, -1):
        j = count - 1 - i
        if i < half - 1:
            head = row(y, i, TILE) + link(i) * head
            tail = row(y, j, TILE) + link(j) * tail
        x_ref[pl.ds(offset + TILE * i, TILE), :] = head
        x_ref[pl.ds(offset + TILE * j, TILE), :] = tail


def send_lines(e, lo_ref, hi_ref):
    pairs = e[...].reshape(-1, 2, TILE, LANES)
    first, second = pairs[:, 0], pairs[:, 1]
    mask = first_half(first.shape)
    lo_ref[...] = jnp.where(mask, first, pltpu.roll(second, Z, 1)).reshape(-1, LANES)
    hi_ref[...] = jnp.where(mask, pltpu.roll(first, Z, 1), second).reshape(-1, LANES)


def factor_kernel(gathered, out, fac_ref, middle_ref):
    count = fac_ref.shape[1] // TILE

    def part(k, a):
        return gathered[pl.ds(112 * (a // 2) + 48 + 16 * k + 8 * (a % 2), TILE), :]

    outflow = DISCOUNT + out[...]
    gaps = [None, None]
    links = [None, None]
    for i in range(count // 2):
        for side, a in ((0, i), (1, count - 1 - i)):
            here = pl.ds(TILE * a, TILE)
            inner, outer = (part(0, a), part(1, a)) if side == 0 else (part(1, a), part(0, a))
            fb, bb = part(2, a), part(3, a)
            slack = outflow + fb + bb
            slack = slack + (outer if i == 0 else outer * gaps[side])
            weight = 1.0 / (slack + inner)
            links[side] = inner * weight
            gaps[side] = slack * weight
            fac_ref[0, here, :] = fb
            fac_ref[1, here, :] = bb
            fac_ref[2, here, :] = weight
            fac_ref[3, here, :] = outer * weight
            fac_ref[4, here, :] = links[side]
    middle_ref[...] = 1.0 / (gaps[0] + links[0] * gaps[1])


def first_solve_kernel(gathered, fac, middle, e_ref, lo_ref, hi_ref, y):
    solve_lines(
        lambda a: gathered[pl.ds(112 * (a // 2) + 8 * (a % 2), TILE), :],
        lambda a: row(fac.at[2], a, TILE),
        lambda a: row(fac.at[3], a, TILE),
        lambda a: row(fac.at[4], a, TILE),
        middle[...], y, e_ref, 0,
    )
    send_lines(e_ref, lo_ref, hi_ref)


def local_target(e, rhs, fac, jhi, jlo, t_ref):
    income(e, t_ref, [(0, 0, e.shape[0] // Z)], jhi, jlo)
    other = swapped(e[...])
    mask = first_half(other.shape)
    t_ref[...] = t_ref[...] + rhs[...] + jnp.where(mask, fac[0], fac[1]) * other


def first_target_kernel(
    gathered, err, e, fac, jhi, jlo, rhs_mid, val, below, above,
    t_ref, rhs_ref, wide_ref, rhs_wide_ref, val_wide_ref,
):
    blocks = e.shape[0] // (2 * TILE)
    for i in range(blocks):
        rhs_ref[pl.ds(16 * i, 16), :] = gathered[pl.ds(112 * i, 16), :]
    local_target(e, rhs_ref, fac, jhi, jlo, t_ref)
    widen_rhs(rhs_mid, below, above, rhs_wide_ref)
    widen_value(val, below, above, val_wide_ref)
    here = lax.axis_index("liq")
    wide_ref[32:128, :] = err[...]
    for at, block, inside in ((0, here - 1, here > 0), (128, here + 1, here < blocks - 1)):
        block = jnp.minimum(jnp.maximum(block, 0), blocks - 1)
        start = pl.multiple_of(block * 112 + 16, 16)
        piece = gathered[pl.ds(start, 32), :]
        wide_ref[pl.ds(at, 32), :] = jnp.where(inside, piece, jnp.zeros_like(piece))


def swept(t, fac, middle, below, above, y, x_ref, offset):
    mask = first_half((TILE, LANES))

    def target(a):
        low_side, high_side = row(below, a // 2, TILE), row(above, a // 2, TILE)
        if a % 2:
            low_side = pltpu.roll(low_side, Z, 0)
        else:
            high_side = pltpu.roll(high_side, Z, 0)
        near = jnp.where(mask, low_side, high_side)
        coupling = jnp.where(mask, row(fac.at[1], a, TILE), row(fac.at[0], a, TILE))
        return row(t, a, TILE) + coupling * near

    solve_lines(
        target,
        lambda a: row(fac.at[2], a, TILE),
        lambda a: row(fac.at[3], a, TILE),
        lambda a: row(fac.at[4], a, TILE),
        middle[...], y, x_ref, offset,
    )


def sweep_kernel(t, fac, middle, below, above, e_ref, lo_ref, hi_ref, y):
    swept(t, fac, middle, below, above, y, e_ref, 0)
    send_lines(e_ref, lo_ref, hi_ref)


def last_sweep_kernel(t, fac, middle, below, above, err, sum_ref, y, x):
    edge = 2 * TILE
    x[0:edge, :] = jnp.zeros((edge, LANES), F32)
    x[pl.ds(x.shape[0] - edge, edge), :] = jnp.zeros((edge, LANES), F32)
    swept(t, fac, middle, below, above, y, x, edge)
    start = lax.axis_index("liq") * 2 * TILE
    for i in range(6):
        low = x[pl.ds(pl.multiple_of(start + i * TILE, TILE), TILE), :]
        fill = doubled(low)
        for m in (2 * i - 1, 2 * i):
            if 0 <= m < 10:
                sum_ref[pl.ds(16 * m, 16), :] = err[pl.ds(16 * m, 16), :] + fill


def last_kernel(
    own, below, above, mid, rhs_mid, fine, val, jhi, jlo, out_ref, ev, e1, e2, v0, v1, v2, inc
):
    for a in range(10):
        for i, src in enumerate((below, own, above)):
            ev[pl.ds(48 * a + 16 * i, 16), :] = src[pl.ds(16 * a, 16), :]

    income(ev, inc, [(48 * (a + 1) + 8, 32 * a, 8) for a in range(8)], jhi, jlo)
    for a in range(8):
        here = pl.ds(32 * a, 32)
        center = row(ev, a + 1, 48)
        total = rhs_mid[here, :] + inc[here, :]
        total = total + mid[0, here, :] * ev[pl.ds(48 * (a + 2) + 8, 32), :]
        total = total + mid[1, here, :] * ev[pl.ds(48 * a + 8, 32), :]
        total = total + mid[2, here, :] * later(center)[8:40]
        total = total + mid[3, here, :] * earlier(center)[8:40]
        e1[here, :] = (1.0 - OMEGA) * center[8:40] + mid[4, here, :] * total

    income(e1, inc, [(32, 32, 8 * 6)], jhi, jlo)
    for a in range(1, 7):
        here = pl.ds(32 * a, 32)
        center = e1[here, :]
        total = rhs_mid[here, :] + inc[here, :]
        total = total + mid[0, here, :] * row(e1, a + 1, 32)
        total = total + mid[1, here, :] * row(e1, a - 1, 32)
        total = total + mid[2, here, :] * later(center)
        total = total + mid[3, here, :] * earlier(center)
        error = (1.0 - OMEGA) * center + mid[4, here, :] * total
        fill = doubled(error)[8:56]
        for f in (2 * a - 2, 2 * a - 1):
            v0[pl.ds(48 * f, 48), :] = row(val, f, 48) + fill

    def sweep(src, dst, begin, end):
        income(src, inc, [(48 * begin, 48 * begin, 12 * (end - begin))], jhi, jlo)
        for a in range(begin, end):
            here = pl.ds(48 * a, 48)
            center = src[here, :]
            total = fine[0, here, :] + inc[here, :]
            total = total + fine[1, here, :] * row(src, a + 1, 48)
            total = total + fine[2, here, :] * row(src, a - 1, 48)
            total = total + fine[3, here, :] * later(center)
            total = total + fine[4, here, :] * earlier(center)
            dst[here, :] = (1.0 - OMEGA) * center + fine[5, here, :] * total

    sweep(v0, v1, 1, 11)
    sweep(v1, v2, 2, 10)
    for a in range(8):
        for c in range(Z):
            piece = v2[pl.ds(48 * (a + 2) + 8 + c, 8, stride=Z), :]
            out_ref[a, :, c * LANES : (c + 1) * LANES] = piece


def call(kernel, args, outs, scratch=(), flops=0, places=(), limit=24):
    outs = [x if isinstance(x, jax.ShapeDtypeStruct) else jax.ShapeDtypeStruct(x, F32) for x in outs]
    moved = sum(x.size * x.dtype.itemsize for x in (*args, *outs))
    kinds = list(places) + [pltpu.VMEM] * (len(args) - len(places))
    return pl.pallas_call(
        kernel,
        out_shape=outs,
        in_specs=[pl.BlockSpec(memory_space=kind) for kind in kinds],
        out_specs=[pl.BlockSpec(memory_space=pltpu.VMEM)] * len(outs),
        scratch_shapes=[pltpu.VMEM(s, F32) if isinstance(s, tuple) else s for s in scratch],
        compiler_params=pltpu.CompilerParams(vmem_limit_bytes=limit * 2**20),
        cost_estimate=pl.CostEstimate(flops=flops, bytes_accessed=moved, transcendentals=0),
    )(*args)


def neighbours(lo, hi, axis):
    count = lax.axis_size(axis)
    below = lax.ppermute(hi, axis, [(i, i + 1) for i in range(count - 1)])
    above = lax.ppermute(lo, axis, [(i + 1, i) for i in range(count - 1)])
    return below, above


def body(right_side, value_guess, speed_liq, speed_ill, flag_liq, flag_ill, jump_rates):
    nz = jump_rates.shape[0]
    dot_flops = 2 * 3 * nz * nz
    inputs = (right_side, value_guess, speed_liq, speed_ill, flag_liq, flag_ill)
    buffers = [pltpu.VMEM(x.shape, x.dtype) for x in inputs]
    sems = pltpu.SemaphoreType.DMA((6,))
    lo, hi, up, down, low = call(
        pack_kernel,
        inputs,
        [(576, LANES)] * 2 + [(1184, LANES)] * 2 + [(64, LANES)],
        buffers + [(1792, LANES), sems],
        places=[pltpu.HBM] * 6,
        limit=57,
    )
    ill_below, ill_above = neighbours(lo, hi, "ill")
    below, above = neighbours(down, up, "liq")
    rates = jax.ShapeDtypeStruct((nz, nz), BF16)
    (own,) = call(
        own_kernel, inputs, [(1792, LANES)], buffers + [sems], places=[pltpu.HBM] * 6, limit=57
    )
    jhi, jlo, out, own = call(
        rates_kernel, (jump_rates, own), [rates, rates, (TILE, LANES), own.shape]
    )
    up, down = call(corner_kernel, (ill_below, ill_above), [(720, LANES)] * 2)
    far_below, far_above = neighbours(down, up, "liq")
    pieces = (own, ill_below, ill_above, below, above, far_below, far_above)
    value, rhs_mid, lo, hi = call(
        fine_kernel,
        (*pieces, jhi, jlo, out),
        [(384, LANES), (128, LANES), (160, LANES), (160, LANES)],
        [(1408, LANES), (960, LANES), (960, LANES), (1408, LANES), (6, 960, LANES)],
        flops=dot_flops * 730,
    )
    mid_below, mid_above = neighbours(lo, hi, "ill")
    fine, mid = call(keep_kernel, (*pieces, out), [(6, 576, LANES), (5, 256, LANES)])
    payload, err = call(
        mid_kernel,
        (rhs_mid, mid_below, mid_above, mid, jhi, jlo, out, low),
        [(112 * lax.axis_size("liq"), LANES), (96, LANES)],
        [(256, LANES)] * 4,
        flops=dot_flops * 80,
    )
    gathered = lax.all_to_all(payload, "liq", 0, 0, tiled=True)
    lines = gathered.shape[0] // 112 * 2 * TILE
    line, message = (lines, LANES), (lines // 2, LANES)
    fac, middle = call(factor_kernel, (gathered, out), [(5, *line), (TILE, LANES)])
    e, lo, hi = call(
        first_solve_kernel, (gathered, fac, middle), [line, message, message], [line]
    )
    for step in range(SWEEPS - 1):
        below, above = neighbours(lo, hi, "ill")
        flops = dot_flops * lines // Z
        if step == 0:
            target, rhs, err, rhs_mid, value = call(
                first_target_kernel,
                (gathered, err, e, fac, jhi, jlo, rhs_mid, value, mid_below, mid_above),
                [line, line, (160, LANES), (256, LANES), (576, LANES)],
                flops=flops,
            )
        else:
            (target,) = call(local_target, (e, rhs, fac, jhi, jlo), [line], flops=flops)
        if step < SWEEPS - 2:
            e, lo, hi = call(
                sweep_kernel, (target, fac, middle, below, above), [line, message, message], [line]
            )
    (total,) = call(
        last_sweep_kernel,
        (target, fac, middle, below, above, err),
        [(160, LANES)],
        [line, (lines + 4 * TILE, LANES)],
    )
    below, above = neighbours(total, total, "ill")
    (result,) = call(
        last_kernel,
        (total, below, above, mid, rhs_mid, fine, value, jhi, jlo),
        [right_side.shape],
        [(480, LANES), (256, LANES), (256, LANES)] + [(576, LANES)] * 4,
        flops=dot_flops * 330,
    )
    return result


def solution(mesh):
    block = P("liq", "ill", None)
    return jax.shard_map(
        body, mesh=mesh, in_specs=(block,) * 6 + (P(),), out_specs=block, check_vma=False
    )
```
